1024 devices in a mesh: gx: 16 (over z_lo, x), gy: 8 (over y), gz: 8 (over z_hi, core).
Axes of the slice: x: 4, y: 8, z: 16 (z_hi: 4, z_lo: 4; z = z_hi * 4 + z_lo), core: 2. Of those that a mesh axis runs over, the one named last changes fastest.
Arguments:
- conserved: float32 [32, 32, 64, 5, 512], P('gx', 'gy', 'gz'), may hold values from -1 to 6, as said below
- troubled: int32 [32, 32, 64], P('gx', 'gy', 'gz'), may hold values from 0 to 1, as said below
- blend_level: int32 [32, 32, 64], P('gx', 'gy', 'gz'), may hold values from 1 to 4
Outputs:
- residual: float32 [32, 32, 64, 5, 512], P('gx', 'gy', 'gz')
The draws below stay inside these ranges and needn't reach their ends.
Inputs may be any that keep to these rules, and one draw needn't show every extreme that they name: `conserved`: at every node density and pressure lie within 0.5 to 2 and each velocity component within -0.5 to 0.5. `troubled`: flagged elements cluster along a shock plane. In every row of devices along gx exactly one device flags 4 times the number of devices along gx, and every other device flags exactly 4.
All inputs are finite; a program needn't handle non-finite values.
Results may differ from the reference program's by a relative error of at most 0.0001.
Values sent between devices are 32-bit elements; how exact they have to be, the bound alone decides.
No kernel may reach another device: no remote copies, remote signals or barrier semaphores. Data moves between devices by JAX's collectives and lax.ppermute only.
A program may use at most 32 MiB of HBM per device.

```python
import jax
import jax.numpy as jnp
import numpy as np
from jax import lax

EX = 2
EY = 4
EZ = 8
SLOT = 4
NX = 32
NY = 32
NZ = 64
N_GX = 16
N_GY = 8
N_GZ = 8


def to_grid(device_major):
    shaped = device_major.reshape(N_GX, N_GY, N_GZ, EX, EY, EZ)
    return shaped.transpose(0, 3, 1, 4, 2, 5).reshape(EX * N_GX, EY * N_GY, EZ * N_GZ)


def draw_troubled(key, part):
    key = jax.random.fold_in(key, 3)
    key_shock, key_order = jax.random.split(key, 2)
    per_device = EX * EY * EZ
    capacity = SLOT * N_GX
    shock_shift = jax.random.randint(key_shock, (), 0, N_GX)
    device_x = jnp.arange(N_GX, dtype=jnp.int32)[:, None, None]
    device_y = jnp.arange(N_GY, dtype=jnp.int32)[None, :, None]
    device_z = jnp.arange(N_GZ, dtype=jnp.int32)[None, None, :]
    on_shock = (device_x + device_y + device_z) % N_GX == shock_shift
    scores = jax.random.randint(key_order, (N_GX, N_GY, N_GZ, per_device), 0, 1048576) * per_device + jnp.arange(per_device, dtype=jnp.int32)
    rank_in_device = jnp.argsort(jnp.argsort(scores, axis=-1), axis=-1).astype(jnp.int32)
    limit = jnp.where(on_shock, capacity, SLOT)[..., None]
    flagged = rank_in_device < limit
    return to_grid(flagged.astype(jnp.int32))


def draw_conserved(key, part):
    key = jax.random.fold_in(key, 7)
    key_rho, key_vel, key_press = jax.random.split(key, 3)
    full_shape = (EX * N_GX, EY * N_GY, EZ * N_GZ, 512)
    density = jnp.exp(jax.random.uniform(key_rho, full_shape, jnp.float32, -0.69, 0.69))
    velocity = jnp.clip(0.2 * jax.random.normal(key_vel, (3,) + full_shape, jnp.float32), -0.5, 0.5)
    pressure = jnp.exp(jax.random.uniform(key_press, full_shape, jnp.float32, -0.69, 0.69))
    energy = pressure / 0.4 + 0.5 * density * jnp.sum(velocity * velocity, axis=0)
    return jnp.stack([density, density * velocity[0], density * velocity[1], density * velocity[2], energy], axis=3)


def with_ends(result, stream_key, smallest, high):
    longest = result.shape.index(max(result.shape))
    spots = []
    for shift in (0, 1):
        where = [jax.random.randint(jax.random.fold_in(stream_key, axis), (), 0, length) for axis, length in enumerate(result.shape)]
        where[longest] = (where[longest] + shift) % result.shape[longest]
        spots.append(tuple(where))
    return result.at[spots[0]].set(smallest).at[spots[1]].set(high)


def setup_inputs(seed: int = 0) -> dict:
    splits = jax.random.split(jax.random.key(seed), 4)
    conserved = draw_conserved(jax.random.fold_in(splits[3], 71), 0)
    troubled = draw_troubled(jax.random.fold_in(splits[3], 71), 0)
    blend_level = with_ends(jax.random.randint(splits[2], (NX, NY, NZ), 1, 5), jax.random.fold_in(splits[2], 1), 1, 4).astype(jnp.int32)
    return dict(conserved=conserved, troubled=troubled, blend_level=blend_level)


PRECISE = lax.Precision.HIGHEST
HEAT_RATIO = 1.4
GRID_SCALE = 0.05
LOBATTO_POINTS = [-1.0, -0.8717401485096066, -0.5917001814331423, -0.2092992179024789, 0.2092992179024789, 0.5917001814331423, 0.8717401485096066, 1.0]
LOBATTO_WEIGHTS = [0.03571428571428571, 0.21070422714350603, 0.34112269248350435, 0.4124587946587039, 0.4124587946587039, 0.34112269248350435, 0.21070422714350603, 0.03571428571428571]

def node_tables():
    points = np.array(LOBATTO_POINTS)
    weights = np.array(LOBATTO_WEIGHTS)
    barycentric = np.array([1.0 / np.prod([points[row_index] - points[other_index] for other_index in range(8) if other_index != row_index]) for row_index in range(8)])
    derivative = np.zeros((8, 8))
    for row_index in range(8):
        for column in range(8):
            if row_index != column:
                derivative[row_index, column] = barycentric[column] / barycentric[row_index] / (points[row_index] - points[column])
        derivative[row_index, row_index] = -np.sum(derivative[row_index])
    identity = np.eye(8)
    kron_list = [np.kron(np.kron(derivative, identity), identity), np.kron(np.kron(identity, derivative), identity), np.kron(np.kron(identity, identity), derivative)]
    stacked = np.concatenate([matrix.T for matrix in kron_list], axis=0)
    numbers = np.arange(512).reshape(8, 8, 8)
    face_nodes = [numbers[0], numbers[7], numbers[:, 0], numbers[:, 7], numbers[:, :, 0], numbers[:, :, 7]]
    extract = np.zeros((512, 384))
    for face_index, node_list in enumerate(face_nodes):
        extract[node_list.ravel(), face_index * 64 + np.arange(64)] = 1.0
    lifting = extract.T / weights[0]
    node_grid = np.stack(np.meshgrid(np.arange(8), np.arange(8), np.arange(8), indexing='ij')).reshape(3, 512)
    inverse = 1.0 / weights[node_grid]
    return (jnp.asarray(stacked, jnp.float32), jnp.asarray(extract, jnp.float32), jnp.asarray(lifting, jnp.float32), jnp.asarray(inverse, jnp.float32), node_grid)

def face_part(face_data, face_index):
    return face_data[..., face_index * 64:(face_index + 1) * 64]

def euler_flux(values_in, axis_index):
    density = values_in[..., 0, :]
    momenta = [values_in[..., 1, :], values_in[..., 2, :], values_in[..., 3, :]]
    energy = values_in[..., 4, :]
    normal = momenta[axis_index] / density
    kinetic = 0.5 * (momenta[0] * momenta[0] + momenta[1] * momenta[1] + momenta[2] * momenta[2]) / density
    pressure = (HEAT_RATIO - 1.0) * (energy - kinetic)
    sound_speed = jnp.sqrt(HEAT_RATIO * pressure / density)
    components = [momenta[axis_index], momenta[0] * normal, momenta[1] * normal, momenta[2] * normal, (energy + pressure) * normal]
    components[1 + axis_index] = components[1 + axis_index] + pressure
    return (jnp.stack(components, axis=-2), jnp.abs(normal) + sound_speed)

def rusanov(left_state, right_state, axis_index):
    left_flux, left_speed = euler_flux(left_state, axis_index)
    right_flux, right_speed = euler_flux(right_state, axis_index)
    largest = jnp.maximum(left_speed, right_speed)[..., None, :]
    return 0.5 * (left_flux + right_flux) - 0.5 * largest * (right_state - left_state)

def star_fluxes(face_data, below_faces, above_faces):
    columns = []
    for axis_index in range(3):
        columns.append(rusanov(below_faces[axis_index], face_part(face_data, 2 * axis_index), axis_index))
        columns.append(rusanov(face_part(face_data, 2 * axis_index + 1), above_faces[axis_index], axis_index))
    return jnp.concatenate(columns, axis=-1)

def dg_residual(conserved, face_data, star_flux, tables):
    stacked, extract, lifting, inverse, node_grid = tables
    fluxes = jnp.concatenate([euler_flux(conserved, axis_index)[0] for axis_index in range(3)], axis=-1)
    volume = jnp.matmul(fluxes, stacked, precision=PRECISE)
    face_jumps = []
    for axis_index in range(3):
        face_jumps.append(face_part(star_flux, 2 * axis_index) - euler_flux(face_part(face_data, 2 * axis_index), axis_index)[0])
        face_jumps.append(euler_flux(face_part(face_data, 2 * axis_index + 1), axis_index)[0] - face_part(star_flux, 2 * axis_index + 1))
    surface = jnp.matmul(jnp.concatenate(face_jumps, axis=-1), lifting, precision=PRECISE)
    return GRID_SCALE * (surface - volume)

def fv_residual(conserved, star_flux, tables):
    stacked, extract, lifting, inverse, node_grid = tables
    summed = jnp.zeros_like(conserved)
    for axis_index in range(3):
        stride = 8 ** (2 - axis_index)
        neighbour = jnp.roll(conserved, -stride, axis=-1)
        interface = rusanov(conserved, neighbour, axis_index)
        lower_face = jnp.matmul(face_part(star_flux, 2 * axis_index), extract[:, 128 * axis_index:128 * axis_index + 64].T, precision=PRECISE)
        upper_face = jnp.matmul(face_part(star_flux, 2 * axis_index + 1), extract[:, 128 * axis_index + 64:128 * axis_index + 128].T, precision=PRECISE)
        upper_flux = jnp.where(node_grid[axis_index] == 7, upper_face, interface)
        lower_flux = jnp.where(node_grid[axis_index] == 0, lower_face, jnp.roll(upper_flux, stride, axis=-1))
        summed = summed + (lower_flux - upper_flux) * inverse[axis_index]
    return GRID_SCALE * summed

def reference(conserved, troubled, blend_level):
    tables = node_tables()
    face_data = jnp.matmul(conserved, tables[1], precision=PRECISE)
    below_faces = [jnp.roll(face_part(face_data, 2 * axis_index + 1), 1, axis=axis_index) for axis_index in range(3)]
    above_faces = [jnp.roll(face_part(face_data, 2 * axis_index), -1, axis=axis_index) for axis_index in range(3)]
    star_flux = star_fluxes(face_data, below_faces, above_faces)
    weight = troubled.astype(jnp.float32) * blend_level.astype(jnp.float32) / 5.0

    def slab_residual(slab_items):
        state_slab, faces_slab, stars_slab, weight_slab = slab_items
        smooth = dg_residual(state_slab, faces_slab, stars_slab, tables)
        subcell = fv_residual(state_slab, stars_slab, tables)
        return smooth + weight_slab[..., None, None] * (subcell - smooth)
    return lax.map(slab_residual, (conserved, face_data, star_flux, weight))
```

```python
import functools

import jax
import jax.numpy as jnp
import numpy as np
from jax import lax
from jax.experimental import pallas as pl
from jax.experimental.pallas import tpu as pltpu
from jax.sharding import PartitionSpec as P

AXES = ("gx", "gy", "gz")
HEAT_RATIO = 1.4
GRID_SCALE = 0.05
PRECISE = lax.Precision.HIGHEST
LOBATTO_POINTS = [
    -1.0,
    -0.8717401485096066,
    -0.5917001814331423,
    -0.2092992179024789,
    0.2092992179024789,
    0.5917001814331423,
    0.8717401485096066,
    1.0,
]
LOBATTO_WEIGHTS = [
    0.03571428571428571,
    0.21070422714350603,
    0.34112269248350435,
    0.4124587946587039,
    0.4124587946587039,
    0.34112269248350435,
    0.21070422714350603,
    0.03571428571428571,
]
EDGE = GRID_SCALE / LOBATTO_WEIGHTS[0]
ROWS = 40


def weak_tables():
    points = np.array(LOBATTO_POINTS)
    weights = np.array(LOBATTO_WEIGHTS)
    bary = np.array([1.0 / np.prod([points[i] - points[j] for j in range(8) if j != i]) for i in range(8)])
    derivative = np.zeros((8, 8))
    for i in range(8):
        for j in range(8):
            if i != j:
                derivative[i, j] = bary[j] / bary[i] / (points[i] - points[j])
        derivative[i, i] = -np.sum(derivative[i])
    derivative[0, 0] += 1.0 / weights[0]
    derivative[7, 7] -= 1.0 / weights[0]
    weak = -GRID_SCALE * derivative.T
    eye = np.eye(8)
    along_x = np.kron(weak, np.eye(64))
    along_y = np.kron(np.eye(4), np.kron(weak, eye))
    along_z = np.kron(np.eye(32), weak)
    return [jnp.asarray(m, jnp.float32) for m in (along_x, along_y, along_z)]


def lanes_of(shape):
    return lax.broadcasted_iota(jnp.int32, shape, len(shape) - 1)


def roll(value, shift):
    shift = shift % 128
    return value if shift == 0 else pltpu.roll(value, shift, value.ndim - 1)


def euler(u, d):
    rho, mom, energy = u[0], u[1:4], u[4]
    inv = 1.0 / rho
    normal = mom[d] * inv
    kinetic = 0.5 * (mom[0] * mom[0] + mom[1] * mom[1] + mom[2] * mom[2]) * inv
    pressure = (HEAT_RATIO - 1.0) * (energy - kinetic)
    sound = jnp.sqrt(HEAT_RATIO * pressure * inv)
    flux = [mom[d], mom[0] * normal, mom[1] * normal, mom[2] * normal, (energy + pressure) * normal]
    flux[1 + d] = flux[1 + d] + pressure
    return flux, jnp.abs(normal) + sound


def upwind(left, left_flux, left_speed, right, right_flux, right_speed):
    half = 0.5 * jnp.maximum(left_speed, right_speed)
    return [0.5 * (fl + fr) - half * (ur - ul) for ul, fl, ur, fr in zip(left, left_flux, right, right_flux)]


def rusanov(left, right, d):
    return upwind(left, *euler(left, d), right, *euler(right, d))


def squeeze(tile, lane, first):
    tile = roll(tile, -first)
    for bit in range(4):
        step = 1 << bit
        moved = functools.reduce(
            jnp.logical_or, [lane == 8 * m - 7 * (m % (2 * step)) for m in range(16) if m & step]
        )
        tile = jnp.where(moved, roll(tile, -7 * step), tile)
    return tile


def spread(tile, lane):
    for bit in reversed(range(4)):
        step = 1 << bit
        moved = functools.reduce(
            jnp.logical_or, [lane == 8 * m - 7 * (m % step) for m in range(16) if m & step]
        )
        tile = jnp.where(moved, roll(tile, 7 * step), tile)
    return tile


def faces_kernel(x_ref, out_ref):
    lane3 = lanes_of((ROWS, 128))
    for q in range(2):
        first = x_ref[pl.ds((2 * q) * ROWS, ROWS), 0:128]
        second = x_ref[pl.ds((2 * q + 1) * ROWS, ROWS), 0:128]
        out_ref[pl.ds(q * ROWS, ROWS), :] = jnp.where(lane3 < 64, first, roll(second, 64))
        first = x_ref[pl.ds((4 + 2 * q) * ROWS, ROWS), 384:512]
        second = x_ref[pl.ds((4 + 2 * q + 1) * ROWS, ROWS), 384:512]
        out_ref[pl.ds((2 + q) * ROWS, ROWS), :] = jnp.where(lane3 < 64, roll(first, 64), second)
    for face, (ey, j) in enumerate(((0, 0), (3, 7))):
        packed = None
        for ex in range(2):
            for i in range(8):
                chunk, half = i // 2, i % 2
                goal = ex * 64 + i * 8
                piece = x_ref[pl.ds((ex * 4 + ey) * ROWS, ROWS), chunk * 128 : (chunk + 1) * 128]
                piece = roll(piece, goal - half * 64 - j * 8)
                packed = piece if packed is None else jnp.where(lane3 >= goal, piece, packed)
        out_ref[pl.ds((4 + face) * ROWS, ROWS), :] = packed
    lane = lanes_of((8, 128))
    sub = lax.broadcasted_iota(jnp.int32, (8, 128), 0)
    for comp in range(5):
        packed = None
        for face, (ez, k) in enumerate(((0, 0), (7, 7))):
            for chunk in range(4):
                piece = None
                for e in range(8):
                    row = x_ref[pl.ds(e * ROWS + comp * 8 + ez, 1), chunk * 128 : (chunk + 1) * 128]
                    row = jnp.broadcast_to(row, (8, 128))
                    piece = row if piece is None else jnp.where(sub >= e, row, piece)
                piece = squeeze(piece, lane, k)
                goal = face * 64 + chunk * 16
                packed = piece if packed is None else jnp.where(lane >= goal, roll(piece, goal), packed)
        out_ref[pl.ds(6 * ROWS + comp * 8, 8), :] = packed


def inner_kernel(x_ref, blend_ref, mx_ref, my_ref, mz_ref, out_ref, flux_ref, speed_ref, gy_ref, gx_ref):
    lane = lanes_of((8, 128))
    sub = lax.broadcasted_iota(jnp.int32, (8, 128), 0)
    k, j, half = lane % 8, (lane // 8) % 8, lane // 64
    weights = [float(w) for w in LOBATTO_WEIGHTS]

    def by_index(index, table):
        value = jnp.full(index.shape, table[0], jnp.float32)
        for n in range(1, 8):
            value = jnp.where(index == n, table[n], value)
        return value

    scale = [GRID_SCALE / w for w in weights]
    scale_z, scale_y = by_index(k, scale), by_index(j, scale)
    scale_x = [jnp.where(half == 0, scale[2 * c], scale[2 * c + 1]) for c in range(4)]

    def tile(ref, row, c):
        return ref[pl.ds(pl.multiple_of(row, 8), 8), c * 128 : (c + 1) * 128]

    def put(ref, row, c, value):
        ref[pl.ds(pl.multiple_of(row, 8), 8), c * 128 : (c + 1) * 128] = value

    def fluxes(e, carry):
        for c in range(4):
            u = [tile(x_ref, e * ROWS + 8 * n, c) for n in range(5)]
            rho, mom, energy = u[0], u[1:4], u[4]
            inv = 1.0 / rho
            vel = [m * inv for m in mom]
            kinetic = 0.5 * (mom[0] * vel[0] + mom[1] * vel[1] + mom[2] * vel[2])
            pressure = (HEAT_RATIO - 1.0) * (energy - kinetic)
            sound = jnp.sqrt(HEAT_RATIO * pressure * inv)
            total = energy + pressure
            for d in range(3):
                f = [mom[d]] + [mom[n] * vel[d] for n in range(3)] + [total * vel[d]]
                f[1 + d] = f[1 + d] + pressure
                for n in range(5):
                    put(flux_ref.at[d], e * ROWS + 8 * n, c, f[n])
                put(speed_ref.at[d], e * 8, c, jnp.abs(vel[d]) + sound)
        return carry

    lax.fori_loop(0, 8, fluxes, 0)

    def volume(r, carry):
        rows = pl.ds(pl.multiple_of(r * 80, 8), 80)
        total = jnp.dot(flux_ref[0, rows, :], mx_ref[...], precision=PRECISE, preferred_element_type=jnp.float32)
        for h in range(2):
            cols = slice(256 * h, 256 * h + 256)
            part = jnp.dot(
                flux_ref[1, rows, cols], my_ref[...], precision=PRECISE, preferred_element_type=jnp.float32
            ) + jnp.dot(flux_ref[2, rows, cols], mz_ref[...], precision=PRECISE, preferred_element_type=jnp.float32)
            out_ref[rows, cols] = total[:, cols] + part
        return carry

    lax.fori_loop(0, 4, volume, 0)

    def subcells(e, carry):
        ex, ey = e // 4, e % 4
        blend = blend_ref[pl.ds(pl.multiple_of(e * 8, 8), 8), :]
        up_y = jnp.minimum(e + 1, 7)
        up_x = jnp.minimum(e + 4, 7)
        has_up_y = jnp.where(ey < 3, 1.0, 0.0)
        has_up_x = jnp.where(ex == 0, 1.0, 0.0)
        low_y = jnp.maximum(e - 1, 0)
        has_low_y, has_low_x = ey > 0, ex == 1
        acc = {}

        def gather(e_row, c, d):
            u = [tile(x_ref, e_row * ROWS + 8 * n, c) for n in range(5)]
            f = [u[1 + d]] + [tile(flux_ref.at[d], e_row * ROWS + 8 * n, c) for n in range(1, 5)]
            return u + f[1:] + [tile(speed_ref.at[d], e_row * 8, c)]

        def interface(own, other, d):
            lu, ru = own[:5], other[:5]
            lf, rf = [lu[1 + d]] + own[5:9], [ru[1 + d]] + other[5:9]
            return upwind(lu, lf, own[9], ru, rf, other[9])

        for c in range(4):
            own = gather(e, c, 2)
            other = [
                jnp.where(k == 7, pltpu.roll(roll(v, 7), 7, 0), roll(v, -1)) for v in own
            ]
            weight = jnp.where(k == 7, jnp.where(sub < 7, 1.0, 0.0), blend)
            for n, g in enumerate(interface(own, other, 2)):
                g = g * weight
                low = jnp.where(k == 0, pltpu.roll(roll(g, -7), 1, 0), roll(g, 1))
                acc[n, c] = (low - g) * scale_z
            own = gather(e, c, 1)
            beyond = gather(up_y, c, 1)
            other = [jnp.where(j == 7, roll(b, 56), roll(v, -8)) for v, b in zip(own, beyond)]
            weight = jnp.where(j == 7, has_up_y, blend)
            for n, g in enumerate(interface(own, other, 1)):
                g = g * weight
                below = jnp.where(has_low_y, tile(gy_ref, low_y * ROWS + 8 * n, c), 0.0)
                low = jnp.where(j == 0, roll(below, -56), roll(g, 8))
                put(gy_ref, e * ROWS + 8 * n, c, g)
                acc[n, c] = acc[n, c] + (low - g) * scale_y
        own = [gather(e, c, 0) for c in range(4)]
        turned = [[roll(v, 64) for v in own[c]] for c in range(4)]
        turned.append([roll(v, 64) for v in gather(up_x, 0, 0)])
        before = [roll(jnp.where(has_low_x, tile(gx_ref, (e % 4) * ROWS + 8 * n, 0), 0.0), 64) for n in range(5)]
        for c in range(4):
            other = [jnp.where(half == 0, a, b) for a, b in zip(turned[c], turned[c + 1])]
            weight = jnp.where(half == 1, has_up_x, blend) if c == 3 else blend
            for n, g in enumerate(interface(own[c], other, 0)):
                g = g * weight
                if c == 3:
                    put(gx_ref, (e % 4) * ROWS + 8 * n, 0, g)
                moved = roll(g, 64)
                low = jnp.where(half == 0, before[n], moved)
                before[n] = moved
                here = acc[n, c] + (low - g) * scale_x[c]
                row = e * ROWS + 8 * n
                put(out_ref, row, c, tile(out_ref, row, c) * (1.0 - blend) + here)
        return carry

    lax.fori_loop(0, 8, subcells, 0)


def outer_kernel(place_ref, pre_ref, own_ref, halo_ref, near_ref, far_ref, out_ref):
    lane = lanes_of((8, 128))
    left_half = lane < 64
    core, odd_x, odd_y = place_ref[0], place_ref[1], place_ref[2]
    out_ref[...] = pre_ref[...]

    def own(tile):
        return own_ref[pl.ds(tile * 8, 8), :]

    def add(row, c, value):
        out_ref[pl.ds(row, 8), c * 128 : (c + 1) * 128] = (
            out_ref[pl.ds(row, 8), c * 128 : (c + 1) * 128] + value
        )

    zero = jnp.zeros((8, 128), jnp.float32)
    for q in range(2):
        mine = [own(5 * q + n) for n in range(5)]
        below = [halo_ref[0, 1 - odd_x, core, pl.ds((5 * q + n) * 8, 8), :] for n in range(5)]
        for n, star in enumerate(rusanov(below, mine, 0)):
            star = EDGE * star
            add((2 * q) * ROWS + 8 * n, 0, jnp.where(left_half, star, zero))
            add((2 * q + 1) * ROWS + 8 * n, 0, jnp.where(left_half, roll(star, 64), zero))
        mine = [own(10 + 5 * q + n) for n in range(5)]
        above = [halo_ref[0, odd_x, core, pl.ds((5 * q + n) * 8, 8), :] for n in range(5)]
        for n, star in enumerate(rusanov(mine, above, 0)):
            star = -EDGE * star
            add((4 + 2 * q) * ROWS + 8 * n, 3, jnp.where(left_half, zero, roll(star, 64)))
            add((4 + 2 * q + 1) * ROWS + 8 * n, 3, jnp.where(left_half, zero, star))
    for face, (ey, j) in enumerate(((0, 0), (3, 7))):
        mine = [own(20 + 5 * face + n) for n in range(5)]
        if face == 0:
            below = [halo_ref[1, 1 - odd_y, core, pl.ds((5 + n) * 8, 8), :] for n in range(5)]
            stars = [EDGE * s for s in rusanov(below, mine, 1)]
        else:
            above = [halo_ref[1, odd_y, core, pl.ds(n * 8, 8), :] for n in range(5)]
            stars = [-EDGE * s for s in rusanov(mine, above, 1)]
        for n, star in enumerate(stars):
            for ex in range(2):
                for c in range(4):
                    start = ex * 64 + 16 * c
                    first = roll(star, j * 8 - start)
                    second = roll(star, 64 + j * 8 - start - 8)
                    value = jnp.where(left_half, first, second)
                    value = jnp.where((lane // 8) % 8 == j, value, zero)
                    add((ex * 4 + ey) * ROWS + 8 * n, c, value)
    first_core = core == 0
    mine = [own(30 + n) for n in range(5)]
    other = []
    for n in range(5):
        near = near_ref[1 - core, pl.ds((30 + n) * 8, 8), :]
        far = far_ref[pl.ds(n * 8, 8), :]
        above = jnp.where(first_core, near, far)
        below = jnp.where(first_core, far, near)
        other.append(roll(jnp.where(left_half, above, below), 64))
    left = [jnp.where(left_half, o, m) for o, m in zip(other, mine)]
    right = [jnp.where(left_half, m, o) for o, m in zip(other, mine)]
    for n, star in enumerate(rusanov(left, right, 2)):
        for face, (ez, k) in enumerate(((0, 0), (7, 7))):
            signed = (EDGE if face == 0 else -EDGE) * star
            for c in range(4):
                value = roll(spread(roll(signed, -(face * 64 + 16 * c)), lane), k)
                value = jnp.where(lane % 8 == k, value, zero)
                cols = slice(c * 128, (c + 1) * 128)
                for e in range(8):
                    row = pl.ds(e * ROWS + n * 8 + ez, 1)
                    out_ref[row, cols] = out_ref[row, cols] + value[e : e + 1, :]


def pairs(size, shift):
    return [[(2 * n + shift) % size, (2 * n + 1 + shift) % size] for n in range(size // 2)]


def crossed(sizes, shift):
    nx, ny, nz = sizes
    moves = []
    for z in range(nz):
        for a, b in pairs(nx, shift) if z % 2 == 0 else pairs(ny, shift):
            for other in range(ny if z % 2 == 0 else nx):
                ends = [((v * ny + other) if z % 2 == 0 else (other * ny + v)) * nz + z for v in (a, b)]
                moves += [(ends[0], ends[1]), (ends[1], ends[0])]
    return sorted(set(moves))


def in_vmem():
    return pl.BlockSpec(memory_space=pltpu.VMEM)


LIMIT = pltpu.CompilerParams(vmem_limit_bytes=32 * 1024 * 1024)


def on_device(conserved, troubled, blend_level):
    sizes = [lax.axis_size(a) for a in AXES]
    ix, iy, iz = [lax.axis_index(a) for a in AXES]
    core, odd_x, odd_y = iz & 1, ix & 1, iy & 1
    state = conserved.transpose(0, 1, 3, 2, 4).reshape(8 * ROWS, 512)

    own = pl.pallas_call(
        faces_kernel,
        out_shape=jax.ShapeDtypeStruct((7 * ROWS, 128), jnp.float32),
        in_specs=[in_vmem()],
        out_specs=in_vmem(),
        compiler_params=LIMIT,
        name="faces",
    )(state)

    both = lax.all_gather(own, "gz", axis_index_groups=pairs(sizes[2], 0))
    x_faces = both[:, : 4 * ROWS].reshape(2, 2, 2 * ROWS, 128)
    y_faces = both[:, 4 * ROWS : 6 * ROWS]
    arrived = []
    for shift in range(2):
        face = odd_x if shift else 1 - odd_x
        x_part = lax.dynamic_index_in_dim(x_faces, face, 1, keepdims=False)
        sent = jnp.where(core == 0, x_part, y_faces)
        arrived.append(lax.ppermute(sent, AXES, crossed(sizes, shift)))
    swap = pairs(sizes[2], 1)
    far = lax.ppermute(own[6 * ROWS :], "gz", [(a, b) for a, b in swap] + [(b, a) for a, b in swap])

    blend = troubled.reshape(64).astype(jnp.float32) * blend_level.reshape(64).astype(jnp.float32) / 5.0
    inner = pl.pallas_call(
        inner_kernel,
        out_shape=jax.ShapeDtypeStruct((8 * ROWS, 512), jnp.float32),
        in_specs=[in_vmem()] * 5,
        out_specs=in_vmem(),
        scratch_shapes=[
            pltpu.VMEM((3, 8 * ROWS, 512), jnp.float32),
            pltpu.VMEM((3, 64, 512), jnp.float32),
            pltpu.VMEM((8 * ROWS, 512), jnp.float32),
            pltpu.VMEM((4 * ROWS, 128), jnp.float32),
        ],
        compiler_params=LIMIT,
        cost_estimate=pl.CostEstimate(flops=4_000_000_000, bytes_accessed=3_000_000, transcendentals=65536),
        name="inner",
    )(state, jnp.broadcast_to(blend[:, None], (64, 128)), *weak_tables())

    halo = lax.all_gather(jnp.stack(arrived), "gz", axis_index_groups=pairs(sizes[2], 0))
    place = jnp.stack([core, odd_x, odd_y]).astype(jnp.int32)
    full = pl.pallas_call(
        outer_kernel,
        out_shape=jax.ShapeDtypeStruct((8 * ROWS, 512), jnp.float32),
        in_specs=[pl.BlockSpec(memory_space=pltpu.SMEM)] + [in_vmem()] * 5,
        out_specs=in_vmem(),
        compiler_params=LIMIT,
        name="outer",
    )(place, inner, own, halo, both, far)
    return full.reshape(2, 4, 5, 8, 512).transpose(0, 1, 3, 2, 4)


def solution(mesh):
    placed = (P("gx", "gy", "gz", None, None), P("gx", "gy", "gz"), P("gx", "gy", "gz"))
    return jax.shard_map(
        on_device,
        mesh=mesh,
        in_specs=placed,
        out_specs=P("gx", "gy", "gz", None, None),
        check_vma=False,
    )
```

```python
import functools

import jax
import jax.numpy as jnp
import numpy as np
from jax import lax
from jax.experimental import pallas as pl
from jax.experimental.pallas import tpu as pltpu
from jax.sharding import PartitionSpec as P

AXES = ("gx", "gy", "gz")
HEAT_RATIO = 1.4
GRID_SCALE = 0.05
LOBATTO_POINTS = [
    -1.0,
    -0.8717401485096066,
    -0.5917001814331423,
    -0.2092992179024789,
    0.2092992179024789,
    0.5917001814331423,
    0.8717401485096066,
    1.0,
]
LOBATTO_WEIGHTS = [
    0.03571428571428571,
    0.21070422714350603,
    0.34112269248350435,
    0.4124587946587039,
    0.4124587946587039,
    0.34112269248350435,
    0.21070422714350603,
    0.03571428571428571,
]
EDGE = GRID_SCALE / LOBATTO_WEIGHTS[0]
ROWS = 40


def weak_matrix():
    points = np.array(LOBATTO_POINTS)
    weights = np.array(LOBATTO_WEIGHTS)
    bary = np.array([1.0 / np.prod([points[i] - points[j] for j in range(8) if j != i]) for i in range(8)])
    derivative = np.zeros((8, 8))
    for i in range(8):
        for j in range(8):
            if i != j:
                derivative[i, j] = bary[j] / bary[i] / (points[i] - points[j])
        derivative[i, i] = -np.sum(derivative[i])
    derivative[0, 0] += 1.0 / weights[0]
    derivative[7, 7] -= 1.0 / weights[0]
    return -GRID_SCALE * derivative


def lanes_of(shape):
    return lax.broadcasted_iota(jnp.int32, shape, len(shape) - 1)


def roll(value, shift):
    shift = shift % 128
    return value if shift == 0 else pltpu.roll(value, shift, value.ndim - 1)


def euler(u, d):
    rho, mom, energy = u[0], u[1:4], u[4]
    inv = 1.0 / rho
    normal = mom[d] * inv
    kinetic = 0.5 * (mom[0] * mom[0] + mom[1] * mom[1] + mom[2] * mom[2]) * inv
    pressure = (HEAT_RATIO - 1.0) * (energy - kinetic)
    sound = jnp.sqrt(HEAT_RATIO * pressure * inv)
    flux = [mom[d], mom[0] * normal, mom[1] * normal, mom[2] * normal, (energy + pressure) * normal]
    flux[1 + d] = flux[1 + d] + pressure
    return flux, jnp.abs(normal) + sound


def upwind(left, left_flux, left_speed, right, right_flux, right_speed):
    half = 0.5 * jnp.maximum(left_speed, right_speed)
    return [0.5 * (fl + fr) - half * (ur - ul) for ul, fl, ur, fr in zip(left, left_flux, right, right_flux)]


def rusanov(left, right, d):
    return upwind(left, *euler(left, d), right, *euler(right, d))


def squeeze(tile, lane, first):
    tile = roll(tile, -first)
    for bit in range(4):
        step = 1 << bit
        moved = functools.reduce(
            jnp.logical_or, [lane == 8 * m - 7 * (m % (2 * step)) for m in range(16) if m & step]
        )
        tile = jnp.where(moved, roll(tile, -7 * step), tile)
    return tile


def spread(tile, lane):
    for bit in reversed(range(4)):
        step = 1 << bit
        moved = functools.reduce(
            jnp.logical_or, [lane == 8 * m - 7 * (m % step) for m in range(16) if m & step]
        )
        tile = jnp.where(moved, roll(tile, 7 * step), tile)
    return tile


def faces_kernel(x_ref, out_ref):
    lane3 = lanes_of((ROWS, 128))
    for q in range(2):
        first = x_ref[pl.ds((2 * q) * ROWS, ROWS), 0:128]
        second = x_ref[pl.ds((2 * q + 1) * ROWS, ROWS), 0:128]
        out_ref[pl.ds(q * ROWS, ROWS), :] = jnp.where(lane3 < 64, first, roll(second, 64))
        first = x_ref[pl.ds((4 + 2 * q) * ROWS, ROWS), 384:512]
        second = x_ref[pl.ds((4 + 2 * q + 1) * ROWS, ROWS), 384:512]
        out_ref[pl.ds((2 + q) * ROWS, ROWS), :] = jnp.where(lane3 < 64, roll(first, 64), second)
    for face, (ey, j) in enumerate(((0, 0), (3, 7))):
        packed = None
        for ex in range(2):
            for i in range(8):
                chunk, half = i // 2, i % 2
                goal = ex * 64 + i * 8
                piece = x_ref[pl.ds((ex * 4 + ey) * ROWS, ROWS), chunk * 128 : (chunk + 1) * 128]
                piece = roll(piece, goal - half * 64 - j * 8)
                packed = piece if packed is None else jnp.where(lane3 >= goal, piece, packed)
        out_ref[pl.ds((4 + face) * ROWS, ROWS), :] = packed
    lane = lanes_of((8, 128))
    sub = lax.broadcasted_iota(jnp.int32, (8, 128), 0)
    for comp in range(5):
        packed = None
        for face, (ez, k) in enumerate(((0, 0), (7, 7))):
            for chunk in range(4):
                piece = None
                for e in range(8):
                    row = x_ref[pl.ds(e * ROWS + comp * 8 + ez, 1), chunk * 128 : (chunk + 1) * 128]
                    row = jnp.broadcast_to(row, (8, 128))
                    piece = row if piece is None else jnp.where(sub >= e, row, piece)
                piece = squeeze(piece, lane, k)
                goal = face * 64 + chunk * 16
                packed = piece if packed is None else jnp.where(lane >= goal, roll(piece, goal), packed)
        out_ref[pl.ds(6 * ROWS + comp * 8, 8), :] = packed


def inner_kernel(x_ref, blend_ref, out_ref, u_ref, flux_ref, speed_ref, acc_ref):
    weak, scale = weak_matrix(), [GRID_SCALE / w for w in LOBATTO_WEIGHTS]
    lane = lanes_of((8, 128))
    k = lax.broadcasted_iota(jnp.int32, (8, 128), 0)
    upper, ex, ey, ez = lane >= 64, (lane // 32) % 2, (lane // 8) % 4, lane % 8
    blend = blend_ref[...]
    smooth, half_blend = 1.0 - blend, 0.5 * blend

    def by_row(values):
        value = jnp.full((8, 128), float(values[0]), jnp.float32)
        for n in range(1, 8):
            value = jnp.where(k == n, float(values[n]), value)
        return value

    def by_half(low, high):
        return jnp.where(upper, float(high), float(low))

    def rows(row):
        return pl.ds(pl.multiple_of(row, 8), 8)

    for n in range(5):
        for h in range(2):
            parts = [
                x_ref[pl.ds(e * ROWS + 8 * n, 8), 256 * g + 128 * h : 256 * g + 128 * h + 128]
                for g in range(2)
                for e in range(8)
            ]
            u_ref[n, pl.ds(128 * h, 128), :] = jnp.concatenate(parts, axis=0).T

    weak_z = [by_row([weak[r][(r + s) % 8] for r in range(8)]) for s in range(8)]
    scale_z = by_row(scale)
    weight_z = jnp.where(k == 7, 0.0, half_blend)

    def first(t, carry):
        at = rows(t * 8)
        u = [u_ref[n, at, :] for n in range(5)]
        rho, mom, energy = u[0], u[1:4], u[4]
        inv = 1.0 / rho
        vel = [m * inv for m in mom]
        kinetic = 0.5 * (mom[0] * vel[0] + mom[1] * vel[1] + mom[2] * vel[2])
        pressure = (HEAT_RATIO - 1.0) * (energy - kinetic)
        sound = jnp.sqrt(HEAT_RATIO * pressure * inv)
        total = energy + pressure
        for d in range(3):
            f = [mom[d]] + [mom[n] * vel[d] for n in range(3)] + [total * vel[d]]
            f[1 + d] = f[1 + d] + pressure
            speed = jnp.abs(vel[d]) + sound
            speed_ref[d, at, :] = speed
            for n in range(1, 5):
                flux_ref[d, n - 1, at, :] = f[n]
        largest = jnp.maximum(speed, pltpu.roll(speed, 7, 0))
        for n in range(5):
            turned = [f[n]] + [pltpu.roll(f[n], 8 - s, 0) for s in range(1, 8)]
            volume = weak_z[0] * turned[0]
            for s in range(1, 8):
                volume = volume + weak_z[s] * turned[s]
            g = weight_z * (f[n] + turned[1] - largest * (pltpu.roll(u[n], 7, 0) - u[n]))
            acc_ref[n, at, :] = smooth * volume + scale_z * (pltpu.roll(g, 1, 0) - g)
        return carry

    lax.fori_loop(0, 32, first, 0, unroll=2)

    def flux(d, n, at):
        return u_ref[1 + d, at, :] if n == 0 else flux_ref[d, n - 1, at, :]

    def between(i, carry):
        last, start = pl.ds(i * 64 + 7, 8, stride=8), pl.ds(i * 64, 8, stride=8)
        weight = jnp.where(ez < 7, 0.5 * EDGE, 0.0)
        largest = jnp.maximum(speed_ref[2, last, :], roll(speed_ref[2, start, :], -1))
        for n in range(5):
            jump = roll(u_ref[n, start, :], -1) - u_ref[n, last, :]
            star = weight * (flux(2, n, last) + roll(flux(2, n, start), -1) - largest * jump)
            acc_ref[n, last, :] = acc_ref[n, last, :] - star
            acc_ref[n, start, :] = acc_ref[n, start, :] + roll(star, 1)
        return carry

    lax.fori_loop(0, 4, between, 0)

    end_y = jnp.where(ey < 3, 0.5, 0.0)

    def second(i, carry):
        at = [rows(i * 64 + 8 * j) for j in range(8)]
        speed = [speed_ref[1, a, :] for a in at]
        largest = [jnp.maximum(speed[j], speed[j + 1]) for j in range(7)]
        largest.append(jnp.maximum(speed[7], roll(speed[0], -8)))
        for n in range(5):
            u, f = [u_ref[n, a, :] for a in at], [flux(1, n, a) for a in at]
            g = [half_blend * (f[j] + f[j + 1] - largest[j] * (u[j + 1] - u[j])) for j in range(7)]
            g.append(end_y * (f[7] + roll(f[0], -8) - largest[7] * (roll(u[0], -8) - u[7])))
            for j in range(8):
                volume = float(weak[j][0]) * f[0]
                for m in range(1, 8):
                    volume = volume + float(weak[j][m]) * f[m]
                low = g[j - 1] if j else roll(g[7], 8)
                acc_ref[n, at[j], :] = acc_ref[n, at[j], :] + (smooth * volume + scale[j] * (low - g[j]))
        return carry

    lax.fori_loop(0, 4, second, 0)

    weak_x = [[by_half(weak[r][m], weak[4 + r][4 + m]) for m in range(4)] for r in range(4)]
    cross_x = [[by_half(weak[r][4 + m], weak[4 + r][m]) for m in range(4)] for r in range(4)]
    scale_x = [by_half(scale[r], scale[4 + r]) for r in range(4)]
    end_x = jnp.where(upper, jnp.where(ex == 0, 0.5, 0.0), half_blend)

    def following(value, swapped):
        return jnp.where(upper, roll(value, 32), swapped)

    def third(j, carry):
        at = [rows(i * 64 + 8 * j) for i in range(4)]
        speed = [speed_ref[0, a, :] for a in at]
        largest = [jnp.maximum(speed[i], speed[i + 1]) for i in range(3)]
        largest.append(jnp.maximum(speed[3], following(speed[0], roll(speed[0], 64))))
        for n in range(5):
            u, f = [u_ref[n, a, :] for a in at], [flux(0, n, a) for a in at]
            swapped = [roll(v, 64) for v in f]
            g = [half_blend * (f[i] + f[i + 1] - largest[i] * (u[i + 1] - u[i])) for i in range(3)]
            jump = following(u[0], roll(u[0], 64)) - u[3]
            g.append(end_x * (f[3] + following(f[0], swapped[0]) - largest[3] * jump))
            start = jnp.where(upper, roll(g[3], 64), jnp.where(ex == 1, roll(g[3], -32), 0.0))
            for i in range(4):
                volume = weak_x[i][0] * f[0] + cross_x[i][0] * swapped[0]
                for m in range(1, 4):
                    volume = volume + weak_x[i][m] * f[m] + cross_x[i][m] * swapped[m]
                low = g[i - 1] if i else start
                acc_ref[n, at[i], :] = acc_ref[n, at[i], :] + (smooth * volume + scale_x[i] * (low - g[i]))
        return carry

    lax.fori_loop(0, 8, third, 0)

    for n in range(5):
        for h in range(2):
            block = acc_ref[n, pl.ds(128 * h, 128), :].T
            for g in range(2):
                for e in range(8):
                    out_ref[pl.ds(e * ROWS + 8 * n, 8), 256 * g + 128 * h : 256 * g + 128 * h + 128] = block[
                        64 * g + 8 * e : 64 * g + 8 * e + 8, :
                    ]


def outer_kernel(place_ref, pre_ref, own_ref, halo_ref, near_ref, far_ref, out_ref):
    lane = lanes_of((8, 128))
    left_half = lane < 64
    core, odd_x, odd_y = place_ref[0], place_ref[1], place_ref[2]
    out_ref[...] = pre_ref[...]

    def own(tile):
        return own_ref[pl.ds(tile * 8, 8), :]

    def add(row, c, value):
        out_ref[pl.ds(row, 8), c * 128 : (c + 1) * 128] = (
            out_ref[pl.ds(row, 8), c * 128 : (c + 1) * 128] + value
        )

    zero = jnp.zeros((8, 128), jnp.float32)
    for q in range(2):
        mine = [own(5 * q + n) for n in range(5)]
        below = [halo_ref[0, 1 - odd_x, core, pl.ds((5 * q + n) * 8, 8), :] for n in range(5)]
        for n, star in enumerate(rusanov(below, mine, 0)):
            star = EDGE * star
            add((2 * q) * ROWS + 8 * n, 0, jnp.where(left_half, star, zero))
            add((2 * q + 1) * ROWS + 8 * n, 0, jnp.where(left_half, roll(star, 64), zero))
        mine = [own(10 + 5 * q + n) for n in range(5)]
        above = [halo_ref[0, odd_x, core, pl.ds((5 * q + n) * 8, 8), :] for n in range(5)]
        for n, star in enumerate(rusanov(mine, above, 0)):
            star = -EDGE * star
            add((4 + 2 * q) * ROWS + 8 * n, 3, jnp.where(left_half, zero, roll(star, 64)))
            add((4 + 2 * q + 1) * ROWS + 8 * n, 3, jnp.where(left_half, zero, star))
    for face, (ey, j) in enumerate(((0, 0), (3, 7))):
        mine = [own(20 + 5 * face + n) for n in range(5)]
        if face == 0:
            below = [halo_ref[1, 1 - odd_y, core, pl.ds((5 + n) * 8, 8), :] for n in range(5)]
            stars = [EDGE * s for s in rusanov(below, mine, 1)]
        else:
            above = [halo_ref[1, odd_y, core, pl.ds(n * 8, 8), :] for n in range(5)]
            stars = [-EDGE * s for s in rusanov(mine, above, 1)]
        for n, star in enumerate(stars):
            for ex in range(2):
                for c in range(4):
                    start = ex * 64 + 16 * c
                    first = roll(star, j * 8 - start)
                    second = roll(star, 64 + j * 8 - start - 8)
                    value = jnp.where(left_half, first, second)
                    value = jnp.where((lane // 8) % 8 == j, value, zero)
                    add((ex * 4 + ey) * ROWS + 8 * n, c, value)
    first_core = core == 0
    mine = [own(30 + n) for n in range(5)]
    other = []
    for n in range(5):
        near = near_ref[1 - core, pl.ds((30 + n) * 8, 8), :]
        far = far_ref[pl.ds(n * 8, 8), :]
        above = jnp.where(first_core, near, far)
        below = jnp.where(first_core, far, near)
        other.append(roll(jnp.where(left_half, above, below), 64))
    left = [jnp.where(left_half, o, m) for o, m in zip(other, mine)]
    right = [jnp.where(left_half, m, o) for o, m in zip(other, mine)]
    for n, star in enumerate(rusanov(left, right, 2)):
        for face, (ez, k) in enumerate(((0, 0), (7, 7))):
            signed = (EDGE if face == 0 else -EDGE) * star
            for c in range(4):
                value = roll(spread(roll(signed, -(face * 64 + 16 * c)), lane), k)
                value = jnp.where(lane % 8 == k, value, zero)
                cols = slice(c * 128, (c + 1) * 128)
                for e in range(8):
                    row = pl.ds(e * ROWS + n * 8 + ez, 1)
                    out_ref[row, cols] = out_ref[row, cols] + value[e : e + 1, :]


def pairs(size, shift):
    return [[(2 * n + shift) % size, (2 * n + 1 + shift) % size] for n in range(size // 2)]


def crossed(sizes, shift):
    nx, ny, nz = sizes
    moves = []
    for z in range(nz):
        for a, b in pairs(nx, shift) if z % 2 == 0 else pairs(ny, shift):
            for other in range(ny if z % 2 == 0 else nx):
                ends = [((v * ny + other) if z % 2 == 0 else (other * ny + v)) * nz + z for v in (a, b)]
                moves += [(ends[0], ends[1]), (ends[1], ends[0])]
    return sorted(set(moves))


def in_vmem():
    return pl.BlockSpec(memory_space=pltpu.VMEM)


LIMIT = pltpu.CompilerParams(vmem_limit_bytes=32 * 1024 * 1024)


def on_device(conserved, troubled, blend_level):
    sizes = [lax.axis_size(a) for a in AXES]
    ix, iy, iz = [lax.axis_index(a) for a in AXES]
    core, odd_x, odd_y = iz & 1, ix & 1, iy & 1
    state = conserved.transpose(0, 1, 3, 2, 4).reshape(8 * ROWS, 512)

    own = pl.pallas_call(
        faces_kernel,
        out_shape=jax.ShapeDtypeStruct((7 * ROWS, 128), jnp.float32),
        in_specs=[in_vmem()],
        out_specs=in_vmem(),
        compiler_params=LIMIT,
        name="faces",
    )(state)

    both = lax.all_gather(own, "gz", axis_index_groups=pairs(sizes[2], 0))
    x_faces = both[:, : 4 * ROWS].reshape(2, 2, 2 * ROWS, 128)
    y_faces = both[:, 4 * ROWS : 6 * ROWS]
    arrived = []
    for shift in range(2):
        face = odd_x if shift else 1 - odd_x
        x_part = lax.dynamic_index_in_dim(x_faces, face, 1, keepdims=False)
        sent = jnp.where(core == 0, x_part, y_faces)
        arrived.append(lax.ppermute(sent, AXES, crossed(sizes, shift)))
    swap = pairs(sizes[2], 1)
    far = lax.ppermute(own[6 * ROWS :], "gz", [(a, b) for a, b in swap] + [(b, a) for a, b in swap])

    blend = troubled.reshape(64).astype(jnp.float32) * blend_level.reshape(64).astype(jnp.float32) / 5.0
    inner = pl.pallas_call(
        inner_kernel,
        out_shape=jax.ShapeDtypeStruct((8 * ROWS, 512), jnp.float32),
        in_specs=[in_vmem()] * 2,
        out_specs=in_vmem(),
        scratch_shapes=[
            pltpu.VMEM((5, 256, 128), jnp.float32),
            pltpu.VMEM((3, 4, 256, 128), jnp.float32),
            pltpu.VMEM((3, 256, 128), jnp.float32),
            pltpu.VMEM((5, 256, 128), jnp.float32),
        ],
        compiler_params=LIMIT,
        cost_estimate=pl.CostEstimate(flops=20_000_000, bytes_accessed=1_400_000, transcendentals=65536),
        name="inner",
    )(state, jnp.broadcast_to(jnp.concatenate([blend, blend])[None, :], (8, 128)))

    halo = lax.all_gather(jnp.stack(arrived), "gz", axis_index_groups=pairs(sizes[2], 0))
    place = jnp.stack([core, odd_x, odd_y]).astype(jnp.int32)
    full = pl.pallas_call(
        outer_kernel,
        out_shape=jax.ShapeDtypeStruct((8 * ROWS, 512), jnp.float32),
        in_specs=[pl.BlockSpec(memory_space=pltpu.SMEM)] + [in_vmem()] * 5,
        out_specs=in_vmem(),
        compiler_params=LIMIT,
        name="outer",
    )(place, inner, own, halo, both, far)
    return full.reshape(2, 4, 5, 8, 512).transpose(0, 1, 3, 2, 4)


def solution(mesh):
    placed = (P("gx", "gy", "gz", None, None), P("gx", "gy", "gz"), P("gx", "gy", "gz"))
    return jax.shard_map(
        on_device,
        mesh=mesh,
        in_specs=placed,
        out_specs=P("gx", "gy", "gz", None, None),
        check_vma=False,
    )
```

```python
import jax
import jax.numpy as jnp
import numpy as np
from jax import lax
from jax.experimental import pallas as pl
from jax.experimental.pallas import tpu as pltpu
from jax.sharding import PartitionSpec as P

AXES = ("gx", "gy", "gz")
HEAT_RATIO = 1.4
GRID_SCALE = 0.05
LOBATTO_POINTS = [
    -1.0,
    -0.8717401485096066,
    -0.5917001814331423,
    -0.2092992179024789,
    0.2092992179024789,
    0.5917001814331423,
    0.8717401485096066,
    1.0,
]
LOBATTO_WEIGHTS = [
    0.03571428571428571,
    0.21070422714350603,
    0.34112269248350435,
    0.4124587946587039,
    0.4124587946587039,
    0.34112269248350435,
    0.21070422714350603,
    0.03571428571428571,
]
EDGE = GRID_SCALE / LOBATTO_WEIGHTS[0]
ROWS = 40


def weak_matrix():
    points = np.array(LOBATTO_POINTS)
    weights = np.array(LOBATTO_WEIGHTS)
    bary = np.array([1.0 / np.prod([points[i] - points[j] for j in range(8) if j != i]) for i in range(8)])
    derivative = np.zeros((8, 8))
    for i in range(8):
        for j in range(8):
            if i != j:
                derivative[i, j] = bary[j] / bary[i] / (points[i] - points[j])
        derivative[i, i] = -np.sum(derivative[i])
    derivative[0, 0] += 1.0 / weights[0]
    derivative[7, 7] -= 1.0 / weights[0]
    return -GRID_SCALE * derivative


def lanes_of(shape):
    return lax.broadcasted_iota(jnp.int32, shape, len(shape) - 1)


def roll(value, shift):
    shift = shift % 128
    return value if shift == 0 else pltpu.roll(value, shift, value.ndim - 1)


def euler(u, d):
    rho, mom, energy = u[0], u[1:4], u[4]
    inv = 1.0 / rho
    normal = mom[d] * inv
    kinetic = 0.5 * (mom[0] * mom[0] + mom[1] * mom[1] + mom[2] * mom[2]) * inv
    pressure = (HEAT_RATIO - 1.0) * (energy - kinetic)
    sound = jnp.sqrt(HEAT_RATIO * pressure * inv)
    flux = [mom[d], mom[0] * normal, mom[1] * normal, mom[2] * normal, (energy + pressure) * normal]
    flux[1 + d] = flux[1 + d] + pressure
    return flux, jnp.abs(normal) + sound


def upwind(left, left_flux, left_speed, right, right_flux, right_speed):
    half = 0.5 * jnp.maximum(left_speed, right_speed)
    return [0.5 * (fl + fr) - half * (ur - ul) for ul, fl, ur, fr in zip(left, left_flux, right, right_flux)]


def rusanov(left, right, d):
    return upwind(left, *euler(left, d), right, *euler(right, d))


def faces_kernel(x_hbm, out_ref, x_ref, arrived):
    parts = ((3, 2), (0, 1), (7, 1), (1, 2), (5, 2))
    copies = [
        pltpu.make_async_copy(
            x_hbm.at[pl.ds(e * ROWS, many * ROWS)], x_ref.at[pl.ds(e * ROWS, many * ROWS)], arrived.at[n]
        )
        for n, (e, many) in enumerate(parts)
    ]
    for copy in copies:
        copy.start()
    lane = lanes_of((ROWS, 128))
    for copy in copies[:3]:
        copy.wait()
    for face, (ey, j) in enumerate(((0, 0), (3, 7))):
        packed = None
        for ex in range(2):
            for chunk in range(4):
                goal = 32 * ex + 8 * chunk
                piece = x_ref[pl.ds((ex * 4 + ey) * ROWS, ROWS), chunk * 128 : (chunk + 1) * 128]
                piece = roll(piece, goal - 8 * j)
                packed = piece if packed is None else jnp.where(lane % 64 >= goal, piece, packed)
        out_ref[pl.ds((4 + face) * ROWS, ROWS), :] = packed
    for copy in copies[3:]:
        copy.wait()
    for q in range(2):
        first = x_ref[pl.ds((2 * q) * ROWS, ROWS), 0:128]
        second = x_ref[pl.ds((2 * q + 1) * ROWS, ROWS), 0:128]
        out_ref[pl.ds(q * ROWS, ROWS), :] = jnp.where(lane < 64, first, roll(second, 64))
        first = x_ref[pl.ds((4 + 2 * q) * ROWS, ROWS), 384:512]
        second = x_ref[pl.ds((4 + 2 * q + 1) * ROWS, ROWS), 384:512]
        out_ref[pl.ds((2 + q) * ROWS, ROWS), :] = jnp.where(lane < 64, roll(first, 64), second)
    lane = lanes_of((8, 128))
    sub = lax.broadcasted_iota(jnp.int32, (8, 128), 0)
    for comp in range(5):
        packed = None
        for face, (ez, k) in enumerate(((0, 0), (7, 7))):
            for chunk in range(4):
                piece = None
                for e in range(8):
                    row = x_ref[pl.ds(e * ROWS + comp * 8 + ez, 1), chunk * 128 : (chunk + 1) * 128]
                    row = jnp.broadcast_to(row, (8, 128))
                    piece = row if piece is None else jnp.where(sub == e, row, piece)
                goal = 4 * face + chunk
                piece = roll(piece, goal - k)
                packed = piece if packed is None else jnp.where(lane % 8 >= goal, piece, packed)
        out_ref[pl.ds(6 * ROWS + comp * 8, 8), :] = packed


def inner_kernel(x_ref, blend_ref, out_ref, u_ref, flux_ref, speed_ref, acc_ref, acc_x_ref):
    weak, scale = weak_matrix(), [GRID_SCALE / w for w in LOBATTO_WEIGHTS]
    lane = lanes_of((8, 128))
    k = lax.broadcasted_iota(jnp.int32, (8, 128), 0)
    upper, ex, ey, ez = lane >= 64, (lane // 32) % 2, (lane // 8) % 4, lane % 8
    blend = blend_ref[...]
    smooth, half_blend = 1.0 - blend, 0.5 * blend

    def by_row(values):
        value = jnp.full((8, 128), float(values[0]), jnp.float32)
        for n in range(1, 8):
            value = jnp.where(k == n, float(values[n]), value)
        return value

    def by_half(low, high):
        return jnp.where(upper, float(high), float(low))

    def rows(row):
        return pl.ds(pl.multiple_of(row, 8), 8)

    for n in range(5):
        for h in range(2):
            parts = [
                x_ref[pl.ds(e * ROWS + 8 * n, 8), 256 * g + 128 * h : 256 * g + 128 * h + 128]
                for g in range(2)
                for e in range(8)
            ]
            u_ref[n, pl.ds(128 * h, 128), :] = jnp.concatenate(parts, axis=0).T

    weak_z = [by_row([weak[r][(r + s) % 8] for r in range(8)]) for s in range(8)]
    scale_z = by_row(scale)
    weight_z = jnp.where(k == 7, 0.0, half_blend)

    def first(t, carry):
        at = rows(t * 8)
        u = [u_ref[n, at, :] for n in range(5)]
        rho, mom, energy = u[0], u[1:4], u[4]
        inv = 1.0 / rho
        vel = [m * inv for m in mom]
        kinetic = 0.5 * (mom[0] * vel[0] + mom[1] * vel[1] + mom[2] * vel[2])
        pressure = (HEAT_RATIO - 1.0) * (energy - kinetic)
        sound = jnp.sqrt(HEAT_RATIO * pressure * inv)
        total = energy + pressure
        for d in range(3):
            f = [mom[d]] + [mom[n] * vel[d] for n in range(3)] + [total * vel[d]]
            f[1 + d] = f[1 + d] + pressure
            speed = jnp.abs(vel[d]) + sound
            speed_ref[d, at, :] = speed
            for n in range(1, 5):
                flux_ref[d, n - 1, at, :] = f[n]
        largest = jnp.maximum(speed, pltpu.roll(speed, 7, 0))
        for n in range(5):
            turned = [f[n]] + [pltpu.roll(f[n], 8 - s, 0) for s in range(1, 8)]
            volume = weak_z[0] * turned[0]
            for s in range(1, 8):
                volume = volume + weak_z[s] * turned[s]
            g = weight_z * (f[n] + turned[1] - largest * (pltpu.roll(u[n], 7, 0) - u[n]))
            acc_ref[n, at, :] = smooth * volume + scale_z * (pltpu.roll(g, 1, 0) - g)
        return carry

    lax.fori_loop(0, 32, first, 0, unroll=2)

    def flux(d, n, at):
        return u_ref[1 + d, at, :] if n == 0 else flux_ref[d, n - 1, at, :]

    def between(i, carry):
        last, start = pl.ds(i * 64 + 7, 8, stride=8), pl.ds(i * 64, 8, stride=8)
        weight = jnp.where(ez < 7, 0.5 * EDGE, 0.0)
        largest = jnp.maximum(speed_ref[2, last, :], roll(speed_ref[2, start, :], -1))
        for n in range(5):
            jump = roll(u_ref[n, start, :], -1) - u_ref[n, last, :]
            star = weight * (flux(2, n, last) + roll(flux(2, n, start), -1) - largest * jump)
            acc_ref[n, last, :] = acc_ref[n, last, :] - star
            acc_ref[n, start, :] = acc_ref[n, start, :] + roll(star, 1)
        return carry

    lax.fori_loop(0, 4, between, 0)

    end_y = jnp.where(ey < 3, 0.5, 0.0)

    def second(i, carry):
        at = [rows(i * 64 + 8 * j) for j in range(8)]
        speed = [speed_ref[1, a, :] for a in at]
        largest = [jnp.maximum(speed[j], speed[j + 1]) for j in range(7)]
        largest.append(jnp.maximum(speed[7], roll(speed[0], -8)))
        for n in range(5):
            u, f = [u_ref[n, a, :] for a in at], [flux(1, n, a) for a in at]
            g = [half_blend * (f[j] + f[j + 1] - largest[j] * (u[j + 1] - u[j])) for j in range(7)]
            g.append(end_y * (f[7] + roll(f[0], -8) - largest[7] * (roll(u[0], -8) - u[7])))
            for j in range(8):
                volume = float(weak[j][0]) * f[0]
                for m in range(1, 8):
                    volume = volume + float(weak[j][m]) * f[m]
                low = g[j - 1] if j else roll(g[7], 8)
                acc_ref[n, at[j], :] = acc_ref[n, at[j], :] + (smooth * volume + scale[j] * (low - g[j]))
        return carry


    weak_x = [[by_half(weak[r][m], weak[4 + r][4 + m]) for m in range(4)] for r in range(4)]
    cross_x = [[by_half(weak[r][4 + m], weak[4 + r][m]) for m in range(4)] for r in range(4)]
    scale_x = [by_half(scale[r], scale[4 + r]) for r in range(4)]
    end_x = jnp.where(upper, jnp.where(ex == 0, 0.5, 0.0), half_blend)

    def following(value, swapped):
        return jnp.where(upper, roll(value, 32), swapped)

    def third(j, carry):
        at = [rows(i * 64 + 8 * j) for i in range(4)]
        speed = [speed_ref[0, a, :] for a in at]
        largest = [jnp.maximum(speed[i], speed[i + 1]) for i in range(3)]
        largest.append(jnp.maximum(speed[3], following(speed[0], roll(speed[0], 64))))
        for n in range(5):
            u, f = [u_ref[n, a, :] for a in at], [flux(0, n, a) for a in at]
            swapped = [roll(v, 64) for v in f]
            g = [half_blend * (f[i] + f[i + 1] - largest[i] * (u[i + 1] - u[i])) for i in range(3)]
            jump = following(u[0], roll(u[0], 64)) - u[3]
            g.append(end_x * (f[3] + following(f[0], swapped[0]) - largest[3] * jump))
            start = jnp.where(upper, roll(g[3], 64), jnp.where(ex == 1, roll(g[3], -32), 0.0))
            for i in range(4):
                volume = weak_x[i][0] * f[0] + cross_x[i][0] * swapped[0]
                for m in range(1, 4):
                    volume = volume + weak_x[i][m] * f[m] + cross_x[i][m] * swapped[m]
                low = g[i - 1] if i else start
                acc_x_ref[n, at[i], :] = smooth * volume + scale_x[i] * (low - g[i])
        return carry

    def both(t, carry):
        second(t, carry)
        third(2 * t, carry)
        third(2 * t + 1, carry)
        return carry

    lax.fori_loop(0, 4, both, 0)

    for n in range(5):
        for h in range(2):
            at = pl.ds(128 * h, 128)
            block = (acc_ref[n, at, :] + acc_x_ref[n, at, :]).T
            for g in range(2):
                for e in range(8):
                    out_ref[pl.ds(e * ROWS + 8 * n, 8), 256 * g + 128 * h : 256 * g + 128 * h + 128] = block[
                        64 * g + 8 * e : 64 * g + 8 * e + 8, :
                    ]


def outer_kernel(place_ref, pre_ref, own_ref, halo_ref, near_ref, far_ref, out_hbm, out_ref, star_ref, left_sem):
    lane = lanes_of((8, 128))
    sub = lax.broadcasted_iota(jnp.int32, (8, 128), 0)
    left_half, low_face = lane < 64, lane % 8 < 4
    core, odd_x, odd_y = place_ref[0], place_ref[1], place_ref[2]
    zero = jnp.zeros((8, 128), jnp.float32)

    def own(tile):
        return own_ref[pl.ds(tile * 8, 8), :]

    first_core = core == 0
    mine = [own(30 + n) for n in range(5)]
    other = []
    for n in range(5):
        near = near_ref[1 - core, pl.ds((30 + n) * 8, 8), :]
        far = far_ref[pl.ds(n * 8, 8), :]
        above = jnp.where(first_core, near, far)
        below = jnp.where(first_core, far, near)
        other.append(jnp.where(low_face, roll(below, -4), roll(above, 4)))
    left = [jnp.where(low_face, o, m) for o, m in zip(other, mine)]
    right = [jnp.where(low_face, m, o) for o, m in zip(other, mine)]
    for n, star in enumerate(rusanov(left, right, 2)):
        star = EDGE * star
        for c in range(4):
            cols = slice(c * 128, (c + 1) * 128)
            star_ref[pl.ds(8 * n, 8), cols] = jnp.where(lane % 8 == 0, roll(star, -c), zero)
            star_ref[pl.ds(ROWS + 8 * n, 8), cols] = jnp.where(lane % 8 == 7, -roll(star, 3 - c), zero)

    along_x = {}
    for q in range(2):
        mine = [own(5 * q + n) for n in range(5)]
        below = [halo_ref[0, 1 - odd_x, core, pl.ds((5 * q + n) * 8, 8), :] for n in range(5)]
        for n, star in enumerate(rusanov(below, mine, 0)):
            star = EDGE * star
            along_x[2 * q, n] = jnp.where(left_half, star, zero)
            along_x[2 * q + 1, n] = jnp.where(left_half, roll(star, 64), zero)
        mine = [own(10 + 5 * q + n) for n in range(5)]
        above = [halo_ref[0, odd_x, core, pl.ds((5 * q + n) * 8, 8), :] for n in range(5)]
        for n, star in enumerate(rusanov(mine, above, 0)):
            star = -EDGE * star
            along_x[4 + 2 * q, n] = jnp.where(left_half, zero, roll(star, 64))
            along_x[5 + 2 * q, n] = jnp.where(left_half, zero, star)

    mine = [own(20 + n) for n in range(5)]
    below = [halo_ref[1, 1 - odd_y, core, pl.ds((5 + n) * 8, 8), :] for n in range(5)]
    low_y = [EDGE * s for s in rusanov(below, mine, 1)]
    mine = [own(25 + n) for n in range(5)]
    above = [halo_ref[1, odd_y, core, pl.ds(n * 8, 8), :] for n in range(5)]
    high_y = [-EDGE * s for s in rusanov(mine, above, 1)]
    row_j = (lane // 8) % 8

    copies = []
    for e in (1, 2, 5, 6, 0, 3, 4, 7):
        ex, ey = e // 4, e % 4
        for n in range(5):
            for c in range(4):
                cols = slice(c * 128, (c + 1) * 128)
                value = pre_ref[pl.ds(e * ROWS + 8 * n, 8), cols]
                low = jnp.broadcast_to(star_ref[pl.ds(8 * n + e, 1), cols], (8, 128))
                high = jnp.broadcast_to(star_ref[pl.ds(ROWS + 8 * n + e, 1), cols], (8, 128))
                value = value + jnp.where(sub == 0, low, jnp.where(sub == 7, high, zero))
                if c == (0, 3)[ex]:
                    value = value + along_x[e, n]
                start = 32 * ex + 8 * c
                if ey == 0:
                    value = value + jnp.where(row_j == 0, roll(low_y[n], -start), zero)
                if ey == 3:
                    value = value + jnp.where(row_j == 7, roll(high_y[n], 56 - start), zero)
                out_ref[pl.ds(e * ROWS + 8 * n, 8), cols] = value
        at = pl.ds(e * ROWS, ROWS)
        copies.append(pltpu.make_async_copy(out_ref.at[at], out_hbm.at[at], left_sem.at[e]))
        copies[-1].start()
    for copy in copies:
        copy.wait()


def pairs(size, shift):
    return [[(2 * n + shift) % size, (2 * n + 1 + shift) % size] for n in range(size // 2)]


def crossed(sizes, shift):
    nx, ny, nz = sizes
    moves = []
    for z in range(nz):
        for a, b in pairs(nx, shift) if z % 2 == 0 else pairs(ny, shift):
            for other in range(ny if z % 2 == 0 else nx):
                ends = [((v * ny + other) if z % 2 == 0 else (other * ny + v)) * nz + z for v in (a, b)]
                moves += [(ends[0], ends[1]), (ends[1], ends[0])]
    return sorted(set(moves))


def in_vmem():
    return pl.BlockSpec(memory_space=pltpu.VMEM)


def in_hbm():
    return pl.BlockSpec(memory_space=pl.ANY)


LIMIT = pltpu.CompilerParams(vmem_limit_bytes=32 * 1024 * 1024)


def on_device(conserved, troubled, blend_level):
    sizes = [lax.axis_size(a) for a in AXES]
    ix, iy, iz = [lax.axis_index(a) for a in AXES]
    core, odd_x, odd_y = iz & 1, ix & 1, iy & 1
    state = conserved.transpose(0, 1, 3, 2, 4).reshape(8 * ROWS, 512)

    own = pl.pallas_call(
        faces_kernel,
        out_shape=jax.ShapeDtypeStruct((7 * ROWS, 128), jnp.float32),
        in_specs=[in_hbm()],
        out_specs=in_vmem(),
        scratch_shapes=[pltpu.VMEM((8 * ROWS, 512), jnp.float32), pltpu.SemaphoreType.DMA((5,))],
        compiler_params=LIMIT,
        name="faces",
    )(state)

    both = lax.all_gather(own, "gz", axis_index_groups=pairs(sizes[2], 0))
    x_faces = both[:, : 4 * ROWS].reshape(2, 2, 2 * ROWS, 128)
    y_faces = both[:, 4 * ROWS : 6 * ROWS]
    arrived = []
    for shift in range(2):
        face = odd_x if shift else 1 - odd_x
        x_part = lax.dynamic_index_in_dim(x_faces, face, 1, keepdims=False)
        sent = jnp.where(core == 0, x_part, y_faces)
        arrived.append(lax.ppermute(sent, AXES, crossed(sizes, shift)))
    swap = pairs(sizes[2], 1)
    far = lax.ppermute(own[6 * ROWS :], "gz", [(a, b) for a, b in swap] + [(b, a) for a, b in swap])

    blend = troubled.reshape(64).astype(jnp.float32) * blend_level.reshape(64).astype(jnp.float32) / 5.0
    inner = pl.pallas_call(
        inner_kernel,
        out_shape=jax.ShapeDtypeStruct((8 * ROWS, 512), jnp.float32),
        in_specs=[in_vmem()] * 2,
        out_specs=in_vmem(),
        scratch_shapes=[
            pltpu.VMEM((5, 256, 128), jnp.float32),
            pltpu.VMEM((3, 4, 256, 128), jnp.float32),
            pltpu.VMEM((3, 256, 128), jnp.float32),
            pltpu.VMEM((5, 256, 128), jnp.float32),
            pltpu.VMEM((5, 256, 128), jnp.float32),
        ],
        compiler_params=LIMIT,
        cost_estimate=pl.CostEstimate(flops=20_000_000, bytes_accessed=1_400_000, transcendentals=65536),
        name="inner",
    )(state, jnp.broadcast_to(jnp.concatenate([blend, blend])[None, :], (8, 128)))

    halo = lax.all_gather(jnp.stack(arrived), "gz", axis_index_groups=pairs(sizes[2], 0))
    place = jnp.stack([core, odd_x, odd_y]).astype(jnp.int32)
    full = pl.pallas_call(
        outer_kernel,
        out_shape=jax.ShapeDtypeStruct((8 * ROWS, 512), jnp.float32),
        in_specs=[pl.BlockSpec(memory_space=pltpu.SMEM)] + [in_vmem()] * 5,
        out_specs=in_hbm(),
        scratch_shapes=[
            pltpu.VMEM((8 * ROWS, 512), jnp.float32),
            pltpu.VMEM((2 * ROWS, 512), jnp.float32),
            pltpu.SemaphoreType.DMA((8,)),
        ],
        compiler_params=LIMIT,
        name="outer",
    )(place, inner, own, halo, both, far)
    return full.reshape(2, 4, 5, 8, 512).transpose(0, 1, 3, 2, 4)


def solution(mesh):
    placed = (P("gx", "gy", "gz", None, None), P("gx", "gy", "gz"), P("gx", "gy", "gz"))
    return jax.shard_map(
        on_device,
        mesh=mesh,
        in_specs=placed,
        out_specs=P("gx", "gy", "gz", None, None),
        check_vma=False,
    )
```

```python
import jax
import jax.numpy as jnp
import numpy as np
from jax import lax
from jax.experimental import pallas as pl
from jax.experimental.pallas import tpu as pltpu
from jax.sharding import PartitionSpec as P

AXES = ("gx", "gy", "gz")
HEAT_RATIO = 1.4
GRID_SCALE = 0.05
LOBATTO_POINTS = [
    -1.0,
    -0.8717401485096066,
    -0.5917001814331423,
    -0.2092992179024789,
    0.2092992179024789,
    0.5917001814331423,
    0.8717401485096066,
    1.0,
]
LOBATTO_WEIGHTS = [
    0.03571428571428571,
    0.21070422714350603,
    0.34112269248350435,
    0.4124587946587039,
    0.4124587946587039,
    0.34112269248350435,
    0.21070422714350603,
    0.03571428571428571,
]
EDGE = GRID_SCALE / LOBATTO_WEIGHTS[0]
ROWS = 40


def weak_matrix():
    points = np.array(LOBATTO_POINTS)
    weights = np.array(LOBATTO_WEIGHTS)
    bary = np.array([1.0 / np.prod([points[i] - points[j] for j in range(8) if j != i]) for i in range(8)])
    derivative = np.zeros((8, 8))
    for i in range(8):
        for j in range(8):
            if i != j:
                derivative[i, j] = bary[j] / bary[i] / (points[i] - points[j])
        derivative[i, i] = -np.sum(derivative[i])
    derivative[0, 0] += 1.0 / weights[0]
    derivative[7, 7] -= 1.0 / weights[0]
    return -GRID_SCALE * derivative


def lanes_of(shape):
    return lax.broadcasted_iota(jnp.int32, shape, len(shape) - 1)


def roll(value, shift):
    shift = shift % 128
    return value if shift == 0 else pltpu.roll(value, shift, value.ndim - 1)


def euler(u, d):
    rho, mom, energy = u[0], u[1:4], u[4]
    inv = 1.0 / rho
    normal = mom[d] * inv
    kinetic = 0.5 * (mom[0] * mom[0] + mom[1] * mom[1] + mom[2] * mom[2]) * inv
    pressure = (HEAT_RATIO - 1.0) * (energy - kinetic)
    sound = jnp.sqrt(HEAT_RATIO * pressure * inv)
    flux = [mom[d], mom[0] * normal, mom[1] * normal, mom[2] * normal, (energy + pressure) * normal]
    flux[1 + d] = flux[1 + d] + pressure
    return flux, jnp.abs(normal) + sound


def upwind(left, left_flux, left_speed, right, right_flux, right_speed):
    half = 0.5 * jnp.maximum(left_speed, right_speed)
    return [0.5 * (fl + fr) - half * (ur - ul) for ul, fl, ur, fr in zip(left, left_flux, right, right_flux)]


def rusanov(left, right, d):
    return upwind(left, *euler(left, d), right, *euler(right, d))


def faces_kernel(x_hbm, out_ref, x_ref, arrived):
    parts = ((3, 2), (0, 1), (7, 1), (1, 2), (5, 2))
    copies = [
        pltpu.make_async_copy(
            x_hbm.at[pl.ds(e * ROWS, many * ROWS)], x_ref.at[pl.ds(e * ROWS, many * ROWS)], arrived.at[n]
        )
        for n, (e, many) in enumerate(parts)
    ]
    for copy in copies:
        copy.start()
    lane = lanes_of((ROWS, 128))
    for copy in copies[:3]:
        copy.wait()
    for face, (ey, j) in enumerate(((0, 0), (3, 7))):
        packed = None
        for ex in range(2):
            for chunk in range(4):
                goal = 32 * ex + 8 * chunk
                piece = x_ref[pl.ds((ex * 4 + ey) * ROWS, ROWS), chunk * 128 : (chunk + 1) * 128]
                piece = roll(piece, goal - 8 * j)
                packed = piece if packed is None else jnp.where(lane % 64 >= goal, piece, packed)
        out_ref[pl.ds((4 + face) * ROWS, ROWS), :] = packed
    for copy in copies[3:]:
        copy.wait()
    for q in range(2):
        first = x_ref[pl.ds((2 * q) * ROWS, ROWS), 0:128]
        second = x_ref[pl.ds((2 * q + 1) * ROWS, ROWS), 0:128]
        out_ref[pl.ds(q * ROWS, ROWS), :] = jnp.where(lane < 64, first, roll(second, 64))
        first = x_ref[pl.ds((4 + 2 * q) * ROWS, ROWS), 384:512]
        second = x_ref[pl.ds((4 + 2 * q + 1) * ROWS, ROWS), 384:512]
        out_ref[pl.ds((2 + q) * ROWS, ROWS), :] = jnp.where(lane < 64, roll(first, 64), second)
    lane = lanes_of((8, 128))
    sub = lax.broadcasted_iota(jnp.int32, (8, 128), 0)
    for comp in range(5):
        packed = None
        for face, (ez, k) in enumerate(((0, 0), (7, 7))):
            for chunk in range(4):
                piece = None
                for e in range(8):
                    row = x_ref[pl.ds(e * ROWS + comp * 8 + ez, 1), chunk * 128 : (chunk + 1) * 128]
                    row = jnp.broadcast_to(row, (8, 128))
                    piece = row if piece is None else jnp.where(sub == e, row, piece)
                goal = 4 * face + chunk
                piece = roll(piece, goal - k)
                packed = piece if packed is None else jnp.where(lane % 8 >= goal, piece, packed)
        out_ref[pl.ds(6 * ROWS + comp * 8, 8), :] = packed


def inner_kernel(x_ref, blend_ref, out_ref, u_ref, flux_ref, speed_ref, acc_ref, acc_x_ref):
    weak, scale = weak_matrix(), [GRID_SCALE / w for w in LOBATTO_WEIGHTS]
    lane = lanes_of((8, 128))
    k = lax.broadcasted_iota(jnp.int32, (8, 128), 0)
    upper, ex, ey, ez = lane >= 64, (lane // 32) % 2, (lane // 8) % 4, lane % 8
    blend = blend_ref[...]
    smooth, half_blend = 1.0 - blend, 0.5 * blend

    def by_row(values):
        value = jnp.full((8, 128), float(values[0]), jnp.float32)
        for n in range(1, 8):
            value = jnp.where(k == n, float(values[n]), value)
        return value

    def by_half(low, high):
        return jnp.where(upper, float(high), float(low))

    def rows(row):
        return pl.ds(pl.multiple_of(row, 8), 8)

    for n in range(5):
        for h in range(2):
            parts = [
                x_ref[pl.ds(e * ROWS + 8 * n, 8), 256 * g + 128 * h : 256 * g + 128 * h + 128]
                for g in range(2)
                for e in range(8)
            ]
            u_ref[n, pl.ds(128 * h, 128), :] = jnp.concatenate(parts, axis=0).T

    weak_z = [by_row([weak[r][(r + s) % 8] for r in range(8)]) for s in range(8)]
    scale_z = by_row(scale)
    weight_z = jnp.where(k == 7, 0.0, half_blend)

    def first(t, carry):
        at = rows(t * 8)
        u = [u_ref[n, at, :] for n in range(5)]
        rho, mom, energy = u[0], u[1:4], u[4]
        inv = 1.0 / rho
        vel = [m * inv for m in mom]
        kinetic = 0.5 * (mom[0] * vel[0] + mom[1] * vel[1] + mom[2] * vel[2])
        pressure = (HEAT_RATIO - 1.0) * (energy - kinetic)
        sound = jnp.sqrt(HEAT_RATIO * pressure * inv)
        total = energy + pressure
        for d in range(3):
            f = [mom[d]] + [mom[n] * vel[d] for n in range(3)] + [total * vel[d]]
            f[1 + d] = f[1 + d] + pressure
            speed = jnp.abs(vel[d]) + sound
            speed_ref[d, at, :] = speed
            for n in range(1, 5):
                flux_ref[d, n - 1, at, :] = f[n]
        largest = jnp.maximum(speed, pltpu.roll(speed, 7, 0))
        for n in range(5):
            turned = [f[n]] + [pltpu.roll(f[n], 8 - s, 0) for s in range(1, 8)]
            volume = weak_z[0] * turned[0]
            for s in range(1, 8):
                volume = volume + weak_z[s] * turned[s]
            g = weight_z * (f[n] + turned[1] - largest * (pltpu.roll(u[n], 7, 0) - u[n]))
            acc_ref[n, at, :] = smooth * volume + scale_z * (pltpu.roll(g, 1, 0) - g)
        return carry

    lax.fori_loop(0, 32, first, 0, unroll=2)

    def flux(d, n, at):
        return u_ref[1 + d, at, :] if n == 0 else flux_ref[d, n - 1, at, :]

    def between(i, carry):
        last, start = pl.ds(i * 64 + 7, 8, stride=8), pl.ds(i * 64, 8, stride=8)
        weight = jnp.where(ez < 7, 0.5 * EDGE, 0.0)
        largest = jnp.maximum(speed_ref[2, last, :], roll(speed_ref[2, start, :], -1))
        for n in range(5):
            jump = roll(u_ref[n, start, :], -1) - u_ref[n, last, :]
            star = weight * (flux(2, n, last) + roll(flux(2, n, start), -1) - largest * jump)
            acc_ref[n, last, :] = acc_ref[n, last, :] - star
            acc_ref[n, start, :] = acc_ref[n, start, :] + roll(star, 1)
        return carry

    lax.fori_loop(0, 4, between, 0)

    end_y = jnp.where(ey < 3, 0.5, 0.0)

    def second(i, carry):
        at = [rows(i * 64 + 8 * j) for j in range(8)]
        speed = [speed_ref[1, a, :] for a in at]
        largest = [jnp.maximum(speed[j], speed[j + 1]) for j in range(7)]
        largest.append(jnp.maximum(speed[7], roll(speed[0], -8)))
        for n in range(5):
            u, f = [u_ref[n, a, :] for a in at], [flux(1, n, a) for a in at]
            g = [half_blend * (f[j] + f[j + 1] - largest[j] * (u[j + 1] - u[j])) for j in range(7)]
            g.append(end_y * (f[7] + roll(f[0], -8) - largest[7] * (roll(u[0], -8) - u[7])))
            for j in range(8):
                volume = float(weak[j][0]) * f[0]
                for m in range(1, 8):
                    volume = volume + float(weak[j][m]) * f[m]
                low = g[j - 1] if j else roll(g[7], 8)
                acc_ref[n, at[j], :] = acc_ref[n, at[j], :] + (smooth * volume + scale[j] * (low - g[j]))
        return carry


    weak_x = [[by_half(weak[r][m], weak[4 + r][4 + m]) for m in range(4)] for r in range(4)]
    cross_x = [[by_half(weak[r][4 + m], weak[4 + r][m]) for m in range(4)] for r in range(4)]
    scale_x = [by_half(scale[r], scale[4 + r]) for r in range(4)]
    end_x = jnp.where(upper, jnp.where(ex == 0, 0.5, 0.0), half_blend)

    def following(value, swapped):
        return jnp.where(upper, roll(value, 32), swapped)

    def third(j, carry):
        at = [rows(i * 64 + 8 * j) for i in range(4)]
        speed = [speed_ref[0, a, :] for a in at]
        largest = [jnp.maximum(speed[i], speed[i + 1]) for i in range(3)]
        largest.append(jnp.maximum(speed[3], following(speed[0], roll(speed[0], 64))))
        for n in range(5):
            u, f = [u_ref[n, a, :] for a in at], [flux(0, n, a) for a in at]
            swapped = [roll(v, 64) for v in f]
            g = [half_blend * (f[i] + f[i + 1] - largest[i] * (u[i + 1] - u[i])) for i in range(3)]
            jump = following(u[0], roll(u[0], 64)) - u[3]
            g.append(end_x * (f[3] + following(f[0], swapped[0]) - largest[3] * jump))
            start = jnp.where(upper, roll(g[3], 64), jnp.where(ex == 1, roll(g[3], -32), 0.0))
            for i in range(4):
                volume = weak_x[i][0] * f[0] + cross_x[i][0] * swapped[0]
                for m in range(1, 4):
                    volume = volume + weak_x[i][m] * f[m] + cross_x[i][m] * swapped[m]
                low = g[i - 1] if i else start
                acc_x_ref[n, at[i], :] = smooth * volume + scale_x[i] * (low - g[i])
        return carry

    def both(t, carry):
        second(t, carry)
        third(2 * t, carry)
        third(2 * t + 1, carry)
        return carry

    lax.fori_loop(0, 4, both, 0)

    for n in range(5):
        for h in range(2):
            at = pl.ds(128 * h, 128)
            block = (acc_ref[n, at, :] + acc_x_ref[n, at, :]).T
            for g in range(2):
                for e in range(8):
                    out_ref[pl.ds(e * ROWS + 8 * n, 8), 256 * g + 128 * h : 256 * g + 128 * h + 128] = block[
                        64 * g + 8 * e : 64 * g + 8 * e + 8, :
                    ]


def outer_kernel(place_ref, pre_ref, own_ref, halo_ref, near_ref, far_ref, out_hbm, out_ref, star_ref, left_sem):
    lane = lanes_of((8, 128))
    sub = lax.broadcasted_iota(jnp.int32, (8, 128), 0)
    left_half, low_face = lane < 64, lane % 8 < 4
    core, odd_x, odd_y = place_ref[0], place_ref[1], place_ref[2]
    zero = jnp.zeros((8, 128), jnp.float32)

    def own(tile):
        return own_ref[pl.ds(tile * 8, 8), :]

    first_core = core == 0
    mine = [own(30 + n) for n in range(5)]
    other = []
    for n in range(5):
        near = near_ref[1 - core, pl.ds((30 + n) * 8, 8), :]
        far = far_ref[pl.ds(n * 8, 8), :]
        above = jnp.where(first_core, near, far)
        below = jnp.where(first_core, far, near)
        other.append(jnp.where(low_face, roll(below, -4), roll(above, 4)))
    left = [jnp.where(low_face, o, m) for o, m in zip(other, mine)]
    right = [jnp.where(low_face, m, o) for o, m in zip(other, mine)]
    for n, star in enumerate(rusanov(left, right, 2)):
        star = EDGE * star
        for c in range(4):
            cols = slice(c * 128, (c + 1) * 128)
            star_ref[pl.ds(8 * n, 8), cols] = jnp.where(lane % 8 == 0, roll(star, -c), zero)
            star_ref[pl.ds(ROWS + 8 * n, 8), cols] = jnp.where(lane % 8 == 7, -roll(star, 3 - c), zero)

    along_x = {}
    for q in range(2):
        mine = [own(5 * q + n) for n in range(5)]
        below = [halo_ref[0, odd_x, core, pl.ds((5 * q + n) * 8, 8), :] for n in range(5)]
        for n, star in enumerate(rusanov(below, mine, 0)):
            star = EDGE * star
            along_x[2 * q, n] = jnp.where(left_half, star, zero)
            along_x[2 * q + 1, n] = jnp.where(left_half, roll(star, 64), zero)
        mine = [own(10 + 5 * q + n) for n in range(5)]
        above = [halo_ref[0, 1 - odd_x, core, pl.ds((5 * q + n) * 8, 8), :] for n in range(5)]
        for n, star in enumerate(rusanov(mine, above, 0)):
            star = -EDGE * star
            along_x[4 + 2 * q, n] = jnp.where(left_half, zero, roll(star, 64))
            along_x[5 + 2 * q, n] = jnp.where(left_half, zero, star)

    mine = [own(20 + n) for n in range(5)]
    below = [halo_ref[1, odd_y, core, pl.ds((5 + n) * 8, 8), :] for n in range(5)]
    low_y = [EDGE * s for s in rusanov(below, mine, 1)]
    mine = [own(25 + n) for n in range(5)]
    above = [halo_ref[1, 1 - odd_y, core, pl.ds(n * 8, 8), :] for n in range(5)]
    high_y = [-EDGE * s for s in rusanov(mine, above, 1)]
    row_j = (lane // 8) % 8

    copies = []
    for e in (1, 2, 5, 6, 0, 3, 4, 7):
        ex, ey = e // 4, e % 4
        for n in range(5):
            for c in range(4):
                cols = slice(c * 128, (c + 1) * 128)
                value = pre_ref[pl.ds(e * ROWS + 8 * n, 8), cols]
                low = jnp.broadcast_to(star_ref[pl.ds(8 * n + e, 1), cols], (8, 128))
                high = jnp.broadcast_to(star_ref[pl.ds(ROWS + 8 * n + e, 1), cols], (8, 128))
                value = value + jnp.where(sub == 0, low, jnp.where(sub == 7, high, zero))
                if c == (0, 3)[ex]:
                    value = value + along_x[e, n]
                start = 32 * ex + 8 * c
                if ey == 0:
                    value = value + jnp.where(row_j == 0, roll(low_y[n], -start), zero)
                if ey == 3:
                    value = value + jnp.where(row_j == 7, roll(high_y[n], 56 - start), zero)
                out_ref[pl.ds(e * ROWS + 8 * n, 8), cols] = value
        at = pl.ds(e * ROWS, ROWS)
        copies.append(pltpu.make_async_copy(out_ref.at[at], out_hbm.at[at], left_sem.at[e]))
        copies[-1].start()
    for copy in copies:
        copy.wait()


def pairs(size, shift):
    return [[(2 * n + shift) % size, (2 * n + 1 + shift) % size] for n in range(size // 2)]


def crossed(sizes, shift):
    nx, ny, nz = sizes
    moves = []
    for z in range(nz):
        for a, b in pairs(nx, shift) if z % 2 == 0 else pairs(ny, shift):
            for other in range(ny if z % 2 == 0 else nx):
                ends = [((v * ny + other) if z % 2 == 0 else (other * ny + v)) * nz + z for v in (a, b)]
                moves += [(ends[0], ends[1]), (ends[1], ends[0])]
    return sorted(set(moves))


def in_vmem():
    return pl.BlockSpec(memory_space=pltpu.VMEM)


def in_hbm():
    return pl.BlockSpec(memory_space=pltpu.HBM)


LIMIT = pltpu.CompilerParams(vmem_limit_bytes=32 * 1024 * 1024)


def on_device(conserved, troubled, blend_level):
    sizes = [lax.axis_size(a) for a in AXES]
    ix, iy, iz = [lax.axis_index(a) for a in AXES]
    core, odd_x, odd_y = iz & 1, ix & 1, iy & 1
    state = conserved.transpose(0, 1, 3, 2, 4).reshape(8 * ROWS, 512)

    own = pl.pallas_call(
        faces_kernel,
        out_shape=jax.ShapeDtypeStruct((7 * ROWS, 128), jnp.float32),
        in_specs=[in_hbm()],
        out_specs=in_vmem(),
        scratch_shapes=[pltpu.VMEM((8 * ROWS, 512), jnp.float32), pltpu.SemaphoreType.DMA((5,))],
        compiler_params=LIMIT,
        name="faces",
    )(pltpu.with_memory_space_constraint(state, pltpu.HBM))

    both = lax.all_gather(own, "gz", axis_index_groups=pairs(sizes[2], 0))
    x_faces = both[:, : 4 * ROWS].reshape(2, 2, 2 * ROWS, 128)
    y_faces = both[:, 4 * ROWS : 6 * ROWS]
    arrived = {}
    for shift in (1, 0):
        face = odd_x if shift else 1 - odd_x
        x_part = lax.dynamic_index_in_dim(x_faces, face, 1, keepdims=False)
        sent = jnp.where(core == 0, x_part, y_faces)
        arrived[shift] = lax.ppermute(sent, AXES, crossed(sizes, shift))
    swap = pairs(sizes[2], 1)
    far = lax.ppermute(own[6 * ROWS :], "gz", [(a, b) for a, b in swap] + [(b, a) for a, b in swap])

    blend = troubled.reshape(64).astype(jnp.float32) * blend_level.reshape(64).astype(jnp.float32) / 5.0
    inner = pl.pallas_call(
        inner_kernel,
        out_shape=jax.ShapeDtypeStruct((8 * ROWS, 512), jnp.float32),
        in_specs=[in_vmem()] * 2,
        out_specs=in_vmem(),
        scratch_shapes=[
            pltpu.VMEM((5, 256, 128), jnp.float32),
            pltpu.VMEM((3, 4, 256, 128), jnp.float32),
            pltpu.VMEM((3, 256, 128), jnp.float32),
            pltpu.VMEM((5, 256, 128), jnp.float32),
            pltpu.VMEM((5, 256, 128), jnp.float32),
        ],
        compiler_params=LIMIT,
        cost_estimate=pl.CostEstimate(flops=20_000_000, bytes_accessed=1_400_000, transcendentals=65536),
        name="inner",
    )(state, jnp.broadcast_to(jnp.concatenate([blend, blend])[None, :], (8, 128)))

    halo = lax.all_gather(jnp.stack([arrived[1], arrived[0]]), "gz", axis_index_groups=pairs(sizes[2], 0))
    place = jnp.stack([core, odd_x, odd_y]).astype(jnp.int32)
    full = pl.pallas_call(
        outer_kernel,
        out_shape=jax.ShapeDtypeStruct((8 * ROWS, 512), jnp.float32),
        in_specs=[pl.BlockSpec(memory_space=pltpu.SMEM)] + [in_vmem()] * 5,
        out_specs=in_hbm(),
        scratch_shapes=[
            pltpu.VMEM((8 * ROWS, 512), jnp.float32),
            pltpu.VMEM((2 * ROWS, 512), jnp.float32),
            pltpu.SemaphoreType.DMA((8,)),
        ],
        compiler_params=LIMIT,
        name="outer",
    )(place, inner, own, halo, both, far)
    return full.reshape(2, 4, 5, 8, 512).transpose(0, 1, 3, 2, 4)


def solution(mesh):
    placed = (P("gx", "gy", "gz", None, None), P("gx", "gy", "gz"), P("gx", "gy", "gz"))
    return jax.shard_map(
        on_device,
        mesh=mesh,
        in_specs=placed,
        out_specs=P("gx", "gy", "gz", None, None),
        check_vma=False,
    )
```

```python
import functools

import jax
import jax.numpy as jnp
import numpy as np
from jax import lax
from jax.experimental import pallas as pl
from jax.experimental.pallas import tpu as pltpu
from jax.sharding import PartitionSpec as P

AXES = ("gx", "gy", "gz")
HEAT_RATIO = 1.4
GRID_SCALE = 0.05
LOBATTO_POINTS = [
    -1.0,
    -0.8717401485096066,
    -0.5917001814331423,
    -0.2092992179024789,
    0.2092992179024789,
    0.5917001814331423,
    0.8717401485096066,
    1.0,
]
LOBATTO_WEIGHTS = [
    0.03571428571428571,
    0.21070422714350603,
    0.34112269248350435,
    0.4124587946587039,
    0.4124587946587039,
    0.34112269248350435,
    0.21070422714350603,
    0.03571428571428571,
]
EDGE = GRID_SCALE / LOBATTO_WEIGHTS[0]
ROWS = 40


def weak_matrix():
    points = np.array(LOBATTO_POINTS)
    weights = np.array(LOBATTO_WEIGHTS)
    bary = np.array([1.0 / np.prod([points[i] - points[j] for j in range(8) if j != i]) for i in range(8)])
    derivative = np.zeros((8, 8))
    for i in range(8):
        for j in range(8):
            if i != j:
                derivative[i, j] = bary[j] / bary[i] / (points[i] - points[j])
        derivative[i, i] = -np.sum(derivative[i])
    derivative[0, 0] += 1.0 / weights[0]
    derivative[7, 7] -= 1.0 / weights[0]
    return -GRID_SCALE * derivative


def lanes_of(shape):
    return lax.broadcasted_iota(jnp.int32, shape, len(shape) - 1)


def roll(value, shift):
    shift = shift % 128
    return value if shift == 0 else pltpu.roll(value, shift, value.ndim - 1)


def euler(u, d):
    rho, mom, energy = u[0], u[1:4], u[4]
    inv = 1.0 / rho
    normal = mom[d] * inv
    kinetic = 0.5 * (mom[0] * mom[0] + mom[1] * mom[1] + mom[2] * mom[2]) * inv
    pressure = (HEAT_RATIO - 1.0) * (energy - kinetic)
    sound = jnp.sqrt(HEAT_RATIO * pressure * inv)
    flux = [mom[d], mom[0] * normal, mom[1] * normal, mom[2] * normal, (energy + pressure) * normal]
    flux[1 + d] = flux[1 + d] + pressure
    return flux, jnp.abs(normal) + sound


def upwind(left, left_flux, left_speed, right, right_flux, right_speed):
    half = 0.5 * jnp.maximum(left_speed, right_speed)
    return [0.5 * (fl + fr) - half * (ur - ul) for ul, fl, ur, fr in zip(left, left_flux, right, right_flux)]


def rusanov(left, right, d):
    return upwind(left, *euler(left, d), right, *euler(right, d))


def faces_kernel(x_hbm, out_ref, x_ref, arrived):
    parts = ((3, 2), (0, 1), (7, 1), (1, 2), (5, 2))
    copies = [
        pltpu.make_async_copy(
            x_hbm.at[pl.ds(e * ROWS, many * ROWS)], x_ref.at[pl.ds(e * ROWS, many * ROWS)], arrived.at[n]
        )
        for n, (e, many) in enumerate(parts)
    ]
    for copy in copies:
        copy.start()
    lane = lanes_of((ROWS, 128))
    for copy in copies[:3]:
        copy.wait()
    for face, (ey, j) in enumerate(((0, 0), (3, 7))):
        packed = None
        for ex in range(2):
            for chunk in range(4):
                goal = 32 * ex + 8 * chunk
                piece = x_ref[pl.ds((ex * 4 + ey) * ROWS, ROWS), chunk * 128 : (chunk + 1) * 128]
                piece = roll(piece, goal - 8 * j)
                packed = piece if packed is None else jnp.where(lane % 64 >= goal, piece, packed)
        out_ref[pl.ds((4 + face) * ROWS, ROWS), :] = packed
    for copy in copies[3:]:
        copy.wait()
    for q in range(2):
        first = x_ref[pl.ds((2 * q) * ROWS, ROWS), 0:128]
        second = x_ref[pl.ds((2 * q + 1) * ROWS, ROWS), 0:128]
        out_ref[pl.ds(q * ROWS, ROWS), :] = jnp.where(lane < 64, first, roll(second, 64))
        first = x_ref[pl.ds((4 + 2 * q) * ROWS, ROWS), 384:512]
        second = x_ref[pl.ds((4 + 2 * q + 1) * ROWS, ROWS), 384:512]
        out_ref[pl.ds((2 + q) * ROWS, ROWS), :] = jnp.where(lane < 64, roll(first, 64), second)
    lane = lanes_of((8, 128))
    sub = lax.broadcasted_iota(jnp.int32, (8, 128), 0)
    for comp in range(5):
        packed = None
        for face, (ez, k) in enumerate(((0, 0), (7, 7))):
            for chunk in range(4):
                piece = None
                for e in range(8):
                    row = x_ref[pl.ds(e * ROWS + comp * 8 + ez, 1), chunk * 128 : (chunk + 1) * 128]
                    row = jnp.broadcast_to(row, (8, 128))
                    piece = row if piece is None else jnp.where(sub == e, row, piece)
                goal = 4 * face + chunk
                piece = roll(piece, goal - k)
                packed = piece if packed is None else jnp.where(lane % 8 >= goal, piece, packed)
        out_ref[pl.ds(6 * ROWS + comp * 8, 8), :] = packed


def inner_kernel(x_ref, troubled_ref, level_ref, out_ref, u_ref, flux_ref, speed_ref, acc_ref, acc_x_ref):
    weak, scale = weak_matrix(), [GRID_SCALE / w for w in LOBATTO_WEIGHTS]
    lane = lanes_of((8, 128))
    k = lax.broadcasted_iota(jnp.int32, (8, 128), 0)
    upper, ex, ey, ez = lane >= 64, (lane // 32) % 2, (lane // 8) % 4, lane % 8
    blend = jnp.zeros((8, 128), jnp.float32)
    for x in range(2):
        marks = (troubled_ref[x] * level_ref[x]).astype(jnp.float32)
        marks = jnp.dot(marks, jnp.where(ez == k, 1.0, 0.0), preferred_element_type=jnp.float32)
        for y in range(4):
            row = jnp.broadcast_to(marks[y : y + 1, :], (8, 128))
            blend = jnp.where((ex == x) & (ey == y), row, blend)
    blend = blend / 5.0
    smooth, half_blend = 1.0 - blend, 0.5 * blend

    def by_row(values):
        value = jnp.full((8, 128), float(values[0]), jnp.float32)
        for n in range(1, 8):
            value = jnp.where(k == n, float(values[n]), value)
        return value

    def by_half(low, high):
        return jnp.where(upper, float(high), float(low))

    def rows(row):
        return pl.ds(pl.multiple_of(row, 8), 8)

    for n in range(5):
        for h in range(2):
            parts = [
                x_ref[pl.ds(e * ROWS + 8 * n, 8), 256 * g + 128 * h : 256 * g + 128 * h + 128]
                for g in range(2)
                for e in range(8)
            ]
            u_ref[n, pl.ds(128 * h, 128), :] = jnp.concatenate(parts, axis=0).T

    weak_z = [by_row([weak[r][(r + s) % 8] for r in range(8)]) for s in range(8)]
    scale_z = by_row(scale)
    weight_z = jnp.where(k == 7, 0.0, half_blend)

    def first(t, carry):
        at = rows(t * 8)
        u = [u_ref[n, at, :] for n in range(5)]
        rho, mom, energy = u[0], u[1:4], u[4]
        inv = 1.0 / rho
        vel = [m * inv for m in mom]
        kinetic = 0.5 * (mom[0] * vel[0] + mom[1] * vel[1] + mom[2] * vel[2])
        pressure = (HEAT_RATIO - 1.0) * (energy - kinetic)
        sound = jnp.sqrt(HEAT_RATIO * pressure * inv)
        total = energy + pressure
        for d in range(3):
            f = [mom[d]] + [mom[n] * vel[d] for n in range(3)] + [total * vel[d]]
            f[1 + d] = f[1 + d] + pressure
            speed = jnp.abs(vel[d]) + sound
            speed_ref[d, at, :] = speed
            for n in range(1, 5):
                flux_ref[d, n - 1, at, :] = f[n]
        largest = jnp.maximum(speed, pltpu.roll(speed, 7, 0))
        for n in range(5):
            turned = [f[n]] + [pltpu.roll(f[n], 8 - s, 0) for s in range(1, 8)]
            volume = weak_z[0] * turned[0]
            for s in range(1, 8):
                volume = volume + weak_z[s] * turned[s]
            g = weight_z * (f[n] + turned[1] - largest * (pltpu.roll(u[n], 7, 0) - u[n]))
            acc_ref[n, at, :] = smooth * volume + scale_z * (pltpu.roll(g, 1, 0) - g)
        return carry

    lax.fori_loop(0, 32, first, 0, unroll=4)

    def flux(d, n, at):
        return u_ref[1 + d, at, :] if n == 0 else flux_ref[d, n - 1, at, :]

    def between(i, carry):
        last, start = pl.ds(i * 64 + 7, 8, stride=8), pl.ds(i * 64, 8, stride=8)
        weight = jnp.where(ez < 7, 0.5 * EDGE, 0.0)
        largest = jnp.maximum(speed_ref[2, last, :], roll(speed_ref[2, start, :], -1))
        for n in range(5):
            jump = roll(u_ref[n, start, :], -1) - u_ref[n, last, :]
            star = weight * (flux(2, n, last) + roll(flux(2, n, start), -1) - largest * jump)
            acc_ref[n, last, :] = acc_ref[n, last, :] - star
            acc_ref[n, start, :] = acc_ref[n, start, :] + roll(star, 1)
        return carry

    lax.fori_loop(0, 4, between, 0, unroll=4)

    end_y = jnp.where(ey < 3, 0.5, 0.0)

    def second(i, carry):
        at = [rows(i * 64 + 8 * j) for j in range(8)]
        speed = [speed_ref[1, a, :] for a in at]
        largest = [jnp.maximum(speed[j], speed[j + 1]) for j in range(7)]
        largest.append(jnp.maximum(speed[7], roll(speed[0], -8)))
        for n in range(5):
            u, f = [u_ref[n, a, :] for a in at], [flux(1, n, a) for a in at]
            g = [half_blend * (f[j] + f[j + 1] - largest[j] * (u[j + 1] - u[j])) for j in range(7)]
            g.append(end_y * (f[7] + roll(f[0], -8) - largest[7] * (roll(u[0], -8) - u[7])))
            even, odd = [f[m] + f[7 - m] for m in range(4)], [f[m] - f[7 - m] for m in range(4)]
            volumes = [None] * 8
            for j in range(4):
                from_odd, from_even = (
                    sum(float(0.5 * (weak[j][m] + sign * weak[j][7 - m])) * part[m] for m in range(4))
                    for sign, part in ((-1, odd), (1, even))
                )
                volumes[j], volumes[7 - j] = from_odd + from_even, from_odd - from_even
            for j in range(8):
                volume = volumes[j]
                low = g[j - 1] if j else roll(g[7], 8)
                acc_ref[n, at[j], :] = acc_ref[n, at[j], :] + (smooth * volume + scale[j] * (low - g[j]))
        return carry


    weak_x = [[by_half(weak[r][m], weak[4 + r][4 + m]) for m in range(4)] for r in range(4)]
    cross_x = [[by_half(weak[r][4 + m], weak[4 + r][m]) for m in range(4)] for r in range(4)]
    scale_x = [by_half(scale[r], scale[4 + r]) for r in range(4)]
    end_x = jnp.where(upper, jnp.where(ex == 0, 0.5, 0.0), half_blend)

    def following(value, swapped):
        return jnp.where(upper, roll(value, 32), swapped)

    def third(j, carry):
        at = [rows(i * 64 + 8 * j) for i in range(4)]
        speed = [speed_ref[0, a, :] for a in at]
        largest = [jnp.maximum(speed[i], speed[i + 1]) for i in range(3)]
        largest.append(jnp.maximum(speed[3], following(speed[0], roll(speed[0], 64))))
        for n in range(5):
            u, f = [u_ref[n, a, :] for a in at], [flux(0, n, a) for a in at]
            swapped = [roll(v, 64) for v in f]
            g = [half_blend * (f[i] + f[i + 1] - largest[i] * (u[i + 1] - u[i])) for i in range(3)]
            jump = following(u[0], roll(u[0], 64)) - u[3]
            g.append(end_x * (f[3] + following(f[0], swapped[0]) - largest[3] * jump))
            start = jnp.where(upper, roll(g[3], 64), jnp.where(ex == 1, roll(g[3], -32), 0.0))
            for i in range(4):
                volume = weak_x[i][0] * f[0] + cross_x[i][0] * swapped[0]
                for m in range(1, 4):
                    volume = volume + weak_x[i][m] * f[m] + cross_x[i][m] * swapped[m]
                low = g[i - 1] if i else start
                acc_x_ref[n, at[i], :] = smooth * volume + scale_x[i] * (low - g[i])
        return carry

    def both(t, carry):
        second(t, carry)
        third(2 * t, carry)
        third(2 * t + 1, carry)
        return carry

    lax.fori_loop(0, 4, both, 0)

    for n in range(5):
        for h in range(2):
            at = pl.ds(128 * h, 128)
            block = (acc_ref[n, at, :] + acc_x_ref[n, at, :]).T
            for g in range(2):
                for e in range(8):
                    out_ref[pl.ds(e * ROWS + 8 * n, 8), 256 * g + 128 * h : 256 * g + 128 * h + 128] = block[
                        64 * g + 8 * e : 64 * g + 8 * e + 8, :
                    ]


def early_kernel(early_ref, *refs):
    @pl.when(early_ref[0] != 0)
    def _():
        inner_kernel(*refs)


def late_kernel(early_ref, done_ref, *refs):
    @pl.when(early_ref[0] != 0)
    def _():
        refs[3][...] = done_ref[...]

    @pl.when(early_ref[0] == 0)
    def _():
        inner_kernel(*refs)


def outer_kernel(place_ref, pre_ref, own_ref, halo_ref, near_ref, far_ref, out_hbm, out_ref, star_ref, left_sem):
    lane = lanes_of((8, 128))
    sub = lax.broadcasted_iota(jnp.int32, (8, 128), 0)
    left_half, low_face = lane < 64, lane % 8 < 4
    core, odd_x, odd_y = place_ref[0], place_ref[1], place_ref[2]
    zero = jnp.zeros((8, 128), jnp.float32)

    def own(tile):
        return own_ref[pl.ds(tile * 8, 8), :]

    first_core = core == 0
    mine = [own(30 + n) for n in range(5)]
    other = []
    for n in range(5):
        near = near_ref[1 - core, pl.ds((30 + n) * 8, 8), :]
        far = far_ref[pl.ds(n * 8, 8), :]
        above = jnp.where(first_core, near, far)
        below = jnp.where(first_core, far, near)
        other.append(jnp.where(low_face, roll(below, -4), roll(above, 4)))
    left = [jnp.where(low_face, o, m) for o, m in zip(other, mine)]
    right = [jnp.where(low_face, m, o) for o, m in zip(other, mine)]
    for n, star in enumerate(rusanov(left, right, 2)):
        star = EDGE * star
        for c in range(4):
            cols = slice(c * 128, (c + 1) * 128)
            star_ref[pl.ds(8 * n, 8), cols] = jnp.where(lane % 8 == 0, roll(star, -c), zero)
            star_ref[pl.ds(ROWS + 8 * n, 8), cols] = jnp.where(lane % 8 == 7, -roll(star, 3 - c), zero)

    along_x = {}
    for q in range(2):
        mine = [own(5 * q + n) for n in range(5)]
        below = [halo_ref[0, odd_x, core, pl.ds((5 * q + n) * 8, 8), :] for n in range(5)]
        for n, star in enumerate(rusanov(below, mine, 0)):
            star = EDGE * star
            along_x[2 * q, n] = jnp.where(left_half, star, zero)
            along_x[2 * q + 1, n] = jnp.where(left_half, roll(star, 64), zero)
        mine = [own(10 + 5 * q + n) for n in range(5)]
        above = [halo_ref[0, 1 - odd_x, core, pl.ds((5 * q + n) * 8, 8), :] for n in range(5)]
        for n, star in enumerate(rusanov(mine, above, 0)):
            star = -EDGE * star
            along_x[4 + 2 * q, n] = jnp.where(left_half, zero, roll(star, 64))
            along_x[5 + 2 * q, n] = jnp.where(left_half, zero, star)

    mine = [own(20 + n) for n in range(5)]
    below = [halo_ref[1, odd_y, core, pl.ds((5 + n) * 8, 8), :] for n in range(5)]
    low_y = [EDGE * s for s in rusanov(below, mine, 1)]
    mine = [own(25 + n) for n in range(5)]
    above = [halo_ref[1, 1 - odd_y, core, pl.ds(n * 8, 8), :] for n in range(5)]
    high_y = [-EDGE * s for s in rusanov(mine, above, 1)]
    row_j = (lane // 8) % 8

    copies = []
    for e in (1, 2, 5, 6, 0, 3, 4, 7):
        ex, ey = e // 4, e % 4
        for n in range(5):
            for c in range(4):
                cols = slice(c * 128, (c + 1) * 128)
                value = pre_ref[pl.ds(e * ROWS + 8 * n, 8), cols]
                low = jnp.broadcast_to(star_ref[pl.ds(8 * n + e, 1), cols], (8, 128))
                high = jnp.broadcast_to(star_ref[pl.ds(ROWS + 8 * n + e, 1), cols], (8, 128))
                value = value + jnp.where(sub == 0, low, jnp.where(sub == 7, high, zero))
                if c == (0, 3)[ex]:
                    value = value + along_x[e, n]
                start = 32 * ex + 8 * c
                if ey == 0:
                    value = value + jnp.where(row_j == 0, roll(low_y[n], -start), zero)
                if ey == 3:
                    value = value + jnp.where(row_j == 7, roll(high_y[n], 56 - start), zero)
                out_ref[pl.ds(e * ROWS + 8 * n, 8), cols] = value
        at = pl.ds(e * ROWS, ROWS)
        copies.append(pltpu.make_async_copy(out_ref.at[at], out_hbm.at[at], left_sem.at[e]))
        copies[-1].start()
    for copy in copies:
        copy.wait()


def pairs(size, shift):
    return [[(2 * n + shift) % size, (2 * n + 1 + shift) % size] for n in range(size // 2)]


def crossed(sizes, shift):
    nx, ny, nz = sizes
    moves = []
    for z in range(nz):
        for a, b in pairs(nx, shift) if z % 2 == 0 else pairs(ny, shift):
            for other in range(ny if z % 2 == 0 else nx):
                ends = [((v * ny + other) if z % 2 == 0 else (other * ny + v)) * nz + z for v in (a, b)]
                moves += [(ends[0], ends[1]), (ends[1], ends[0])]
    return sorted(set(moves))


def in_vmem():
    return pl.BlockSpec(memory_space=pltpu.VMEM)


def in_hbm():
    return pl.BlockSpec(memory_space=pltpu.HBM)


LIMIT = pltpu.CompilerParams(vmem_limit_bytes=32 * 1024 * 1024)


def on_device(conserved, troubled, blend_level):
    sizes = [lax.axis_size(a) for a in AXES]
    ix, iy, iz = [lax.axis_index(a) for a in AXES]
    core, odd_x, odd_y = iz & 1, ix & 1, iy & 1
    state = conserved.transpose(0, 1, 3, 2, 4).reshape(8 * ROWS, 512)

    own = pl.pallas_call(
        faces_kernel,
        out_shape=jax.ShapeDtypeStruct((7 * ROWS, 128), jnp.float32),
        in_specs=[in_hbm()],
        out_specs=in_vmem(),
        scratch_shapes=[pltpu.VMEM((8 * ROWS, 512), jnp.float32), pltpu.SemaphoreType.DMA((5,))],
        compiler_params=LIMIT,
        name="faces",
    )(pltpu.with_memory_space_constraint(state, pltpu.HBM))

    early = ((iz < sizes[2] // 2) | (ix < sizes[0] // 4)).astype(jnp.int32).reshape(1)
    inner_call = functools.partial(
        pl.pallas_call,
        out_shape=jax.ShapeDtypeStruct((8 * ROWS, 512), jnp.float32),
        out_specs=in_vmem(),
        scratch_shapes=[
            pltpu.VMEM((5, 256, 128), jnp.float32),
            pltpu.VMEM((3, 4, 256, 128), jnp.float32),
            pltpu.VMEM((3, 256, 128), jnp.float32),
            pltpu.VMEM((5, 256, 128), jnp.float32),
            pltpu.VMEM((5, 256, 128), jnp.float32),
        ],
        compiler_params=LIMIT,
        cost_estimate=pl.CostEstimate(flops=20_000_000, bytes_accessed=1_400_000, transcendentals=65536),
    )
    in_smem = pl.BlockSpec(memory_space=pltpu.SMEM)
    done = inner_call(early_kernel, in_specs=[in_smem] + [in_vmem()] * 3, name="early")(
        early, state, troubled, blend_level
    )
    own, done = lax.optimization_barrier((own, done))
    swap = pairs(sizes[2], 1)
    far = lax.ppermute(own[6 * ROWS :], "gz", [(a, b) for a, b in swap] + [(b, a) for a, b in swap])

    both = lax.all_gather(own, "gz", axis_index_groups=pairs(sizes[2], 0))
    x_faces = both[:, : 4 * ROWS].reshape(2, 2, 2 * ROWS, 128)
    y_faces = both[:, 4 * ROWS : 6 * ROWS]
    arrived = {}
    for shift in (1, 0):
        face = odd_x if shift else 1 - odd_x
        x_part = lax.dynamic_index_in_dim(x_faces, face, 1, keepdims=False)
        sent = jnp.where(core == 0, x_part, y_faces)
        arrived[shift] = lax.ppermute(sent, AXES, crossed(sizes, shift))
    inner = inner_call(late_kernel, in_specs=[in_smem] + [in_vmem()] * 4, name="late")(
        early, done, state, troubled, blend_level
    )

    halo = lax.all_gather(jnp.stack([arrived[1], arrived[0]]), "gz", axis_index_groups=pairs(sizes[2], 0))
    place = jnp.stack([core, odd_x, odd_y]).astype(jnp.int32)
    full = pl.pallas_call(
        outer_kernel,
        out_shape=jax.ShapeDtypeStruct((8 * ROWS, 512), jnp.float32),
        in_specs=[pl.BlockSpec(memory_space=pltpu.SMEM)] + [in_vmem()] * 5,
        out_specs=in_hbm(),
        scratch_shapes=[
            pltpu.VMEM((8 * ROWS, 512), jnp.float32),
            pltpu.VMEM((2 * ROWS, 512), jnp.float32),
            pltpu.SemaphoreType.DMA((8,)),
        ],
        compiler_params=LIMIT,
        name="outer",
    )(place, inner, own, halo, both, far)
    return full.reshape(2, 4, 5, 8, 512).transpose(0, 1, 3, 2, 4)


def solution(mesh):
    placed = (P("gx", "gy", "gz", None, None), P("gx", "gy", "gz"), P("gx", "gy", "gz"))
    return jax.shard_map(
        on_device,
        mesh=mesh,
        in_specs=placed,
        out_specs=P("gx", "gy", "gz", None, None),
        check_vma=False,
    )
```

```python
import functools

import jax
import jax.numpy as jnp
import numpy as np
from jax import lax
from jax.experimental import pallas as pl
from jax.experimental.pallas import tpu as pltpu
from jax.sharding import PartitionSpec as P

AXES = ("gx", "gy", "gz")
HEAT_RATIO = 1.4
GRID_SCALE = 0.05
LOBATTO_POINTS = [
    -1.0,
    -0.8717401485096066,
    -0.5917001814331423,
    -0.2092992179024789,
    0.2092992179024789,
    0.5917001814331423,
    0.8717401485096066,
    1.0,
]
LOBATTO_WEIGHTS = [
    0.03571428571428571,
    0.21070422714350603,
    0.34112269248350435,
    0.4124587946587039,
    0.4124587946587039,
    0.34112269248350435,
    0.21070422714350603,
    0.03571428571428571,
]
EDGE = GRID_SCALE / LOBATTO_WEIGHTS[0]
ROWS = 40


def weak_matrix():
    points = np.array(LOBATTO_POINTS)
    weights = np.array(LOBATTO_WEIGHTS)
    bary = np.array([1.0 / np.prod([points[i] - points[j] for j in range(8) if j != i]) for i in range(8)])
    derivative = np.zeros((8, 8))
    for i in range(8):
        for j in range(8):
            if i != j:
                derivative[i, j] = bary[j] / bary[i] / (points[i] - points[j])
        derivative[i, i] = -np.sum(derivative[i])
    derivative[0, 0] += 1.0 / weights[0]
    derivative[7, 7] -= 1.0 / weights[0]
    return -GRID_SCALE * derivative


def lanes_of(shape):
    return lax.broadcasted_iota(jnp.int32, shape, len(shape) - 1)


def roll(value, shift):
    shift = shift % 128
    return value if shift == 0 else pltpu.roll(value, shift, value.ndim - 1)


def euler(u, d):
    rho, mom, energy = u[0], u[1:4], u[4]
    inv = 1.0 / rho
    normal = mom[d] * inv
    kinetic = 0.5 * (mom[0] * mom[0] + mom[1] * mom[1] + mom[2] * mom[2]) * inv
    pressure = (HEAT_RATIO - 1.0) * (energy - kinetic)
    sound = jnp.sqrt(HEAT_RATIO * pressure * inv)
    flux = [mom[d], mom[0] * normal, mom[1] * normal, mom[2] * normal, (energy + pressure) * normal]
    flux[1 + d] = flux[1 + d] + pressure
    return flux, jnp.abs(normal) + sound


def upwind(left, left_flux, left_speed, right, right_flux, right_speed):
    half = 0.5 * jnp.maximum(left_speed, right_speed)
    return [0.5 * (fl + fr) - half * (ur - ul) for ul, fl, ur, fr in zip(left, left_flux, right, right_flux)]


def rusanov(left, right, d):
    return upwind(left, *euler(left, d), right, *euler(right, d))


def faces_kernel(x_hbm, out_ref, x_ref, arrived):
    parts = ((3, 2), (0, 1), (7, 1), (1, 2), (5, 2))
    copies = [
        pltpu.make_async_copy(
            x_hbm.at[pl.ds(e * ROWS, many * ROWS)], x_ref.at[pl.ds(e * ROWS, many * ROWS)], arrived.at[n]
        )
        for n, (e, many) in enumerate(parts)
    ]
    for copy in copies:
        copy.start()
    lane = lanes_of((ROWS, 128))
    for copy in copies[:3]:
        copy.wait()
    for face, (ey, j) in enumerate(((0, 0), (3, 7))):
        packed = None
        for ex in range(2):
            for chunk in range(4):
                goal = 32 * ex + 8 * chunk
                piece = x_ref[pl.ds((ex * 4 + ey) * ROWS, ROWS), chunk * 128 : (chunk + 1) * 128]
                piece = roll(piece, goal - 8 * j)
                packed = piece if packed is None else jnp.where(lane % 64 >= goal, piece, packed)
        out_ref[pl.ds((4 + face) * ROWS, ROWS), :] = packed
    for copy in copies[3:]:
        copy.wait()
    for q in range(2):
        first = x_ref[pl.ds((2 * q) * ROWS, ROWS), 0:128]
        second = x_ref[pl.ds((2 * q + 1) * ROWS, ROWS), 0:128]
        out_ref[pl.ds(q * ROWS, ROWS), :] = jnp.where(lane < 64, first, roll(second, 64))
        first = x_ref[pl.ds((4 + 2 * q) * ROWS, ROWS), 384:512]
        second = x_ref[pl.ds((4 + 2 * q + 1) * ROWS, ROWS), 384:512]
        out_ref[pl.ds((2 + q) * ROWS, ROWS), :] = jnp.where(lane < 64, roll(first, 64), second)
    lane = lanes_of((8, 128))
    sub = lax.broadcasted_iota(jnp.int32, (8, 128), 0)
    for comp in range(5):
        packed = None
        for face, (ez, k) in enumerate(((0, 0), (7, 7))):
            for chunk in range(4):
                piece = None
                for e in range(8):
                    row = x_ref[pl.ds(e * ROWS + comp * 8 + ez, 1), chunk * 128 : (chunk + 1) * 128]
                    row = jnp.broadcast_to(row, (8, 128))
                    piece = row if piece is None else jnp.where(sub == e, row, piece)
                goal = 4 * face + chunk
                piece = roll(piece, goal - k)
                packed = piece if packed is None else jnp.where(lane % 8 >= goal, piece, packed)
        out_ref[pl.ds(6 * ROWS + comp * 8, 8), :] = packed


def inner_kernel(x_ref, troubled_ref, level_ref, out_ref, u_ref, flux_ref, speed_ref, acc_ref, acc_x_ref):
    weak, scale = weak_matrix(), [GRID_SCALE / w for w in LOBATTO_WEIGHTS]
    lane = lanes_of((8, 128))
    k = lax.broadcasted_iota(jnp.int32, (8, 128), 0)
    upper, ex, ey, ez = lane >= 64, (lane // 32) % 2, (lane // 8) % 4, lane % 8
    blend = jnp.zeros((8, 128), jnp.float32)
    for x in range(2):
        marks = (troubled_ref[x] * level_ref[x]).astype(jnp.float32)
        marks = jnp.dot(marks, jnp.where(ez == k, 1.0, 0.0), preferred_element_type=jnp.float32)
        for y in range(4):
            row = jnp.broadcast_to(marks[y : y + 1, :], (8, 128))
            blend = jnp.where((ex == x) & (ey == y), row, blend)
    blend = blend / 5.0
    smooth, half_blend = 1.0 - blend, 0.5 * blend

    def by_row(values):
        value = jnp.full((8, 128), float(values[0]), jnp.float32)
        for n in range(1, 8):
            value = jnp.where(k == n, float(values[n]), value)
        return value

    def by_half(low, high):
        return jnp.where(upper, float(high), float(low))

    def rows(row):
        return pl.ds(pl.multiple_of(row, 8), 8)

    for n in range(5):
        for h in range(2):
            parts = [
                x_ref[pl.ds(e * ROWS + 8 * n, 8), 256 * g + 128 * h : 256 * g + 128 * h + 128]
                for g in range(2)
                for e in range(8)
            ]
            u_ref[n, pl.ds(128 * h, 128), :] = jnp.concatenate(parts, axis=0).T

    weak_z = [by_row([weak[r][(r + s) % 8] for r in range(8)]) for s in range(8)]
    scale_z = by_row(scale)
    weight_z = jnp.where(k == 7, 0.0, half_blend)

    def first(t, carry):
        at = rows(t * 8)
        u = [u_ref[n, at, :] for n in range(5)]
        rho, mom, energy = u[0], u[1:4], u[4]
        inv = 1.0 / rho
        vel = [m * inv for m in mom]
        kinetic = 0.5 * (mom[0] * vel[0] + mom[1] * vel[1] + mom[2] * vel[2])
        pressure = (HEAT_RATIO - 1.0) * (energy - kinetic)
        sound = jnp.sqrt(HEAT_RATIO * pressure * inv)
        total = energy + pressure
        for d in range(3):
            f = [mom[d]] + [mom[n] * vel[d] for n in range(3)] + [total * vel[d]]
            f[1 + d] = f[1 + d] + pressure
            speed = jnp.abs(vel[d]) + sound
            speed_ref[d, at, :] = speed
            for n in range(1, 5):
                flux_ref[d, n - 1, at, :] = f[n]
        largest = jnp.maximum(speed, pltpu.roll(speed, 7, 0))
        for n in range(5):
            turned = [f[n]] + [pltpu.roll(f[n], 8 - s, 0) for s in range(1, 8)]
            volume = weak_z[0] * turned[0]
            for s in range(1, 8):
                volume = volume + weak_z[s] * turned[s]
            g = weight_z * (f[n] + turned[1] - largest * (pltpu.roll(u[n], 7, 0) - u[n]))
            acc_ref[n, at, :] = smooth * volume + scale_z * (pltpu.roll(g, 1, 0) - g)
        return carry

    lax.fori_loop(0, 32, first, 0, unroll=4)

    def flux(d, n, at):
        return u_ref[1 + d, at, :] if n == 0 else flux_ref[d, n - 1, at, :]

    def between(i, carry):
        last, start = pl.ds(i * 64 + 7, 8, stride=8), pl.ds(i * 64, 8, stride=8)
        weight = jnp.where(ez < 7, 0.5 * EDGE, 0.0)
        largest = jnp.maximum(speed_ref[2, last, :], roll(speed_ref[2, start, :], -1))
        for n in range(5):
            jump = roll(u_ref[n, start, :], -1) - u_ref[n, last, :]
            star = weight * (flux(2, n, last) + roll(flux(2, n, start), -1) - largest * jump)
            acc_ref[n, last, :] = acc_ref[n, last, :] - star
            acc_ref[n, start, :] = acc_ref[n, start, :] + roll(star, 1)
        return carry

    lax.fori_loop(0, 4, between, 0, unroll=4)

    end_y = jnp.where(ey < 3, 0.5, 0.0)

    def second(i, carry):
        at = [rows(i * 64 + 8 * j) for j in range(8)]
        speed = [speed_ref[1, a, :] for a in at]
        largest = [jnp.maximum(speed[j], speed[j + 1]) for j in range(7)]
        largest.append(jnp.maximum(speed[7], roll(speed[0], -8)))
        for n in range(5):
            u, f = [u_ref[n, a, :] for a in at], [flux(1, n, a) for a in at]
            g = [half_blend * (f[j] + f[j + 1] - largest[j] * (u[j + 1] - u[j])) for j in range(7)]
            g.append(end_y * (f[7] + roll(f[0], -8) - largest[7] * (roll(u[0], -8) - u[7])))
            even, odd = [f[m] + f[7 - m] for m in range(4)], [f[m] - f[7 - m] for m in range(4)]
            volumes = [None] * 8
            for j in range(4):
                from_odd, from_even = (
                    sum(float(0.5 * (weak[j][m] + sign * weak[j][7 - m])) * part[m] for m in range(4))
                    for sign, part in ((-1, odd), (1, even))
                )
                volumes[j], volumes[7 - j] = from_odd + from_even, from_odd - from_even
            for j in range(8):
                volume = volumes[j]
                low = g[j - 1] if j else roll(g[7], 8)
                acc_ref[n, at[j], :] = acc_ref[n, at[j], :] + (smooth * volume + scale[j] * (low - g[j]))
        return carry


    weak_x = [[by_half(weak[r][m], weak[4 + r][4 + m]) for m in range(4)] for r in range(4)]
    cross_x = [[by_half(weak[r][4 + m], weak[4 + r][m]) for m in range(4)] for r in range(4)]
    scale_x = [by_half(scale[r], scale[4 + r]) for r in range(4)]
    end_x = jnp.where(upper, jnp.where(ex == 0, 0.5, 0.0), half_blend)

    def following(value, swapped):
        return jnp.where(upper, roll(value, 32), swapped)

    def third(j, carry):
        at = [rows(i * 64 + 8 * j) for i in range(4)]
        speed = [speed_ref[0, a, :] for a in at]
        largest = [jnp.maximum(speed[i], speed[i + 1]) for i in range(3)]
        largest.append(jnp.maximum(speed[3], following(speed[0], roll(speed[0], 64))))
        for n in range(5):
            u, f = [u_ref[n, a, :] for a in at], [flux(0, n, a) for a in at]
            swapped = [roll(v, 64) for v in f]
            g = [half_blend * (f[i] + f[i + 1] - largest[i] * (u[i + 1] - u[i])) for i in range(3)]
            jump = following(u[0], roll(u[0], 64)) - u[3]
            g.append(end_x * (f[3] + following(f[0], swapped[0]) - largest[3] * jump))
            start = jnp.where(upper, roll(g[3], 64), jnp.where(ex == 1, roll(g[3], -32), 0.0))
            for i in range(4):
                volume = weak_x[i][0] * f[0] + cross_x[i][0] * swapped[0]
                for m in range(1, 4):
                    volume = volume + weak_x[i][m] * f[m] + cross_x[i][m] * swapped[m]
                low = g[i - 1] if i else start
                acc_x_ref[n, at[i], :] = smooth * volume + scale_x[i] * (low - g[i])
        return carry

    def both(t, carry):
        second(t, carry)
        third(2 * t, carry)
        third(2 * t + 1, carry)
        return carry

    lax.fori_loop(0, 4, both, 0)

    for n in range(5):
        for h in range(2):
            at = pl.ds(128 * h, 128)
            block = (acc_ref[n, at, :] + acc_x_ref[n, at, :]).T
            for g in range(2):
                for e in range(8):
                    out_ref[pl.ds(e * ROWS + 8 * n, 8), 256 * g + 128 * h : 256 * g + 128 * h + 128] = block[
                        64 * g + 8 * e : 64 * g + 8 * e + 8, :
                    ]


def early_kernel(early_ref, *refs):
    @pl.when(early_ref[0] != 0)
    def _():
        inner_kernel(*refs)


def late_kernel(early_ref, done_ref, *refs):
    @pl.when(early_ref[0] != 0)
    def _():
        refs[3][...] = done_ref[...]

    @pl.when(early_ref[0] == 0)
    def _():
        inner_kernel(*refs)


def outer_kernel(place_ref, pre_ref, own_ref, halo_ref, near_ref, far_ref, out_hbm, out_ref, star_ref, left_sem):
    lane = lanes_of((8, 128))
    sub = lax.broadcasted_iota(jnp.int32, (8, 128), 0)
    left_half, low_face = lane < 64, lane % 8 < 4
    core, odd_x, odd_y = place_ref[0], place_ref[1], place_ref[2]
    zero = jnp.zeros((8, 128), jnp.float32)

    def own(tile):
        return own_ref[pl.ds(tile * 8, 8), :]

    first_core = core == 0
    mine = [own(30 + n) for n in range(5)]
    other = []
    for n in range(5):
        near = near_ref[1 - core, pl.ds((30 + n) * 8, 8), :]
        far = far_ref[pl.ds(n * 8, 8), :]
        above = jnp.where(first_core, near, far)
        below = jnp.where(first_core, far, near)
        other.append(jnp.where(low_face, roll(below, -4), roll(above, 4)))
    left = [jnp.where(low_face, o, m) for o, m in zip(other, mine)]
    right = [jnp.where(low_face, m, o) for o, m in zip(other, mine)]
    for n, star in enumerate(rusanov(left, right, 2)):
        star = EDGE * star
        for c in range(4):
            cols = slice(c * 128, (c + 1) * 128)
            star_ref[pl.ds(8 * n, 8), cols] = jnp.where(lane % 8 == 0, roll(star, -c), zero)
            star_ref[pl.ds(ROWS + 8 * n, 8), cols] = jnp.where(lane % 8 == 7, -roll(star, 3 - c), zero)

    along_x = {}
    for q in range(2):
        mine = [own(5 * q + n) for n in range(5)]
        below = [halo_ref[0, odd_x, core, pl.ds((5 * q + n) * 8, 8), :] for n in range(5)]
        for n, star in enumerate(rusanov(below, mine, 0)):
            star = EDGE * star
            along_x[2 * q, n] = jnp.where(left_half, star, zero)
            along_x[2 * q + 1, n] = jnp.where(left_half, roll(star, 64), zero)
        mine = [own(10 + 5 * q + n) for n in range(5)]
        above = [halo_ref[0, 1 - odd_x, core, pl.ds((5 * q + n) * 8, 8), :] for n in range(5)]
        for n, star in enumerate(rusanov(mine, above, 0)):
            star = -EDGE * star
            along_x[4 + 2 * q, n] = jnp.where(left_half, zero, roll(star, 64))
            along_x[5 + 2 * q, n] = jnp.where(left_half, zero, star)

    mine = [own(20 + n) for n in range(5)]
    below = [halo_ref[1, odd_y, core, pl.ds((5 + n) * 8, 8), :] for n in range(5)]
    low_y = [EDGE * s for s in rusanov(below, mine, 1)]
    mine = [own(25 + n) for n in range(5)]
    above = [halo_ref[1, 1 - odd_y, core, pl.ds(n * 8, 8), :] for n in range(5)]
    high_y = [-EDGE * s for s in rusanov(mine, above, 1)]
    row_j = (lane // 8) % 8

    copies = []
    for e in (1, 2, 5, 6, 0, 3, 4, 7):
        ex, ey = e // 4, e % 4
        for n in range(5):
            for c in range(4):
                cols = slice(c * 128, (c + 1) * 128)
                value = pre_ref[pl.ds(e * ROWS + 8 * n, 8), cols]
                low = jnp.broadcast_to(star_ref[pl.ds(8 * n + e, 1), cols], (8, 128))
                high = jnp.broadcast_to(star_ref[pl.ds(ROWS + 8 * n + e, 1), cols], (8, 128))
                value = value + jnp.where(sub == 0, low, jnp.where(sub == 7, high, zero))
                if c == (0, 3)[ex]:
                    value = value + along_x[e, n]
                start = 32 * ex + 8 * c
                if ey == 0:
                    value = value + jnp.where(row_j == 0, roll(low_y[n], -start), zero)
                if ey == 3:
                    value = value + jnp.where(row_j == 7, roll(high_y[n], 56 - start), zero)
                out_ref[pl.ds(e * ROWS + 8 * n, 8), cols] = value
        at = pl.ds(e * ROWS, ROWS)
        copies.append(pltpu.make_async_copy(out_ref.at[at], out_hbm.at[at], left_sem.at[e]))
        copies[-1].start()
    for copy in copies:
        copy.wait()


def pairs(size, shift):
    return [[(2 * n + shift) % size, (2 * n + 1 + shift) % size] for n in range(size // 2)]


def crossed(sizes, shift):
    nx, ny, nz = sizes
    moves = []
    for z in range(nz):
        for a, b in pairs(nx, shift) if z % 2 == 0 else pairs(ny, shift):
            for other in range(ny if z % 2 == 0 else nx):
                ends = [((v * ny + other) if z % 2 == 0 else (other * ny + v)) * nz + z for v in (a, b)]
                moves += [(ends[0], ends[1]), (ends[1], ends[0])]
    return sorted(set(moves))


def in_vmem():
    return pl.BlockSpec(memory_space=pltpu.VMEM)


def in_hbm():
    return pl.BlockSpec(memory_space=pltpu.HBM)


LIMIT = pltpu.CompilerParams(vmem_limit_bytes=32 * 1024 * 1024)


def on_device(conserved, troubled, blend_level):
    sizes = [lax.axis_size(a) for a in AXES]
    ix, iy, iz = [lax.axis_index(a) for a in AXES]
    core, odd_x, odd_y = iz & 1, ix & 1, iy & 1
    state = conserved.transpose(0, 1, 3, 2, 4).reshape(8 * ROWS, 512)

    own = pl.pallas_call(
        faces_kernel,
        out_shape=jax.ShapeDtypeStruct((7 * ROWS, 128), jnp.float32),
        in_specs=[in_hbm()],
        out_specs=in_vmem(),
        scratch_shapes=[pltpu.VMEM((8 * ROWS, 512), jnp.float32), pltpu.SemaphoreType.DMA((5,))],
        compiler_params=LIMIT,
        name="faces",
    )(pltpu.with_memory_space_constraint(state, pltpu.HBM))

    both = lax.all_gather(own, "gz", axis_index_groups=pairs(sizes[2], 0))
    x_faces = both[:, : 4 * ROWS].reshape(2, 2, 2 * ROWS, 128)
    y_faces = both[:, 4 * ROWS : 6 * ROWS]
    sent = []
    for shift in range(2):
        face = odd_x if shift else 1 - odd_x
        x_part = lax.dynamic_index_in_dim(x_faces, face, 1, keepdims=False)
        sent.append(jnp.where(core == 0, x_part, y_faces))
    arrived_long = lax.ppermute(sent[1], AXES, crossed(sizes, 1))

    early = (iz < sizes[2] // 2).astype(jnp.int32).reshape(1)
    inner_call = functools.partial(
        pl.pallas_call,
        out_shape=jax.ShapeDtypeStruct((8 * ROWS, 512), jnp.float32),
        out_specs=in_vmem(),
        scratch_shapes=[
            pltpu.VMEM((5, 256, 128), jnp.float32),
            pltpu.VMEM((3, 4, 256, 128), jnp.float32),
            pltpu.VMEM((3, 256, 128), jnp.float32),
            pltpu.VMEM((5, 256, 128), jnp.float32),
            pltpu.VMEM((5, 256, 128), jnp.float32),
        ],
        compiler_params=LIMIT,
        cost_estimate=pl.CostEstimate(flops=20_000_000, bytes_accessed=1_400_000, transcendentals=65536),
    )
    in_smem = pl.BlockSpec(memory_space=pltpu.SMEM)
    done = inner_call(early_kernel, in_specs=[in_smem] + [in_vmem()] * 3, name="early")(
        early, state, troubled, blend_level
    )
    z_faces, short, done = lax.optimization_barrier((own[6 * ROWS :], sent[0], done))
    swap = pairs(sizes[2], 1)
    far = lax.ppermute(z_faces, "gz", [(a, b) for a, b in swap] + [(b, a) for a, b in swap])
    arrived_short = lax.ppermute(short, AXES, crossed(sizes, 0))

    inner = inner_call(late_kernel, in_specs=[in_smem] + [in_vmem()] * 4, name="late")(
        early, done, state, troubled, blend_level
    )

    halo = lax.all_gather(jnp.stack([arrived_long, arrived_short]), "gz", axis_index_groups=pairs(sizes[2], 0))
    place = jnp.stack([core, odd_x, odd_y]).astype(jnp.int32)
    full = pl.pallas_call(
        outer_kernel,
        out_shape=jax.ShapeDtypeStruct((8 * ROWS, 512), jnp.float32),
        in_specs=[pl.BlockSpec(memory_space=pltpu.SMEM)] + [in_vmem()] * 5,
        out_specs=in_hbm(),
        scratch_shapes=[
            pltpu.VMEM((8 * ROWS, 512), jnp.float32),
            pltpu.VMEM((2 * ROWS, 512), jnp.float32),
            pltpu.SemaphoreType.DMA((8,)),
        ],
        compiler_params=LIMIT,
        name="outer",
    )(place, inner, own, halo, both, far)
    return full.reshape(2, 4, 5, 8, 512).transpose(0, 1, 3, 2, 4)


def solution(mesh):
    placed = (P("gx", "gy", "gz", None, None), P("gx", "gy", "gz"), P("gx", "gy", "gz"))
    return jax.shard_map(
        on_device,
        mesh=mesh,
        in_specs=placed,
        out_specs=P("gx", "gy", "gz", None, None),
        check_vma=False,
    )
```

```python
import functools

import jax
import jax.numpy as jnp
import numpy as np
from jax import lax
from jax.experimental import pallas as pl
from jax.experimental.pallas import tpu as pltpu
from jax.sharding import PartitionSpec as P

AXES = ("gx", "gy", "gz")
HEAT_RATIO = 1.4
GRID_SCALE = 0.05
LOBATTO_POINTS = [
    -1.0,
    -0.8717401485096066,
    -0.5917001814331423,
    -0.2092992179024789,
    0.2092992179024789,
    0.5917001814331423,
    0.8717401485096066,
    1.0,
]
LOBATTO_WEIGHTS = [
    0.03571428571428571,
    0.21070422714350603,
    0.34112269248350435,
    0.4124587946587039,
    0.4124587946587039,
    0.34112269248350435,
    0.21070422714350603,
    0.03571428571428571,
]
EDGE = GRID_SCALE / LOBATTO_WEIGHTS[0]
ROWS = 40


def weak_matrix():
    points = np.array(LOBATTO_POINTS)
    weights = np.array(LOBATTO_WEIGHTS)
    bary = np.array([1.0 / np.prod([points[i] - points[j] for j in range(8) if j != i]) for i in range(8)])
    derivative = np.zeros((8, 8))
    for i in range(8):
        for j in range(8):
            if i != j:
                derivative[i, j] = bary[j] / bary[i] / (points[i] - points[j])
        derivative[i, i] = -np.sum(derivative[i])
    derivative[0, 0] += 1.0 / weights[0]
    derivative[7, 7] -= 1.0 / weights[0]
    return -GRID_SCALE * derivative


def lanes_of(shape):
    return lax.broadcasted_iota(jnp.int32, shape, len(shape) - 1)


def roll(value, shift):
    shift = shift % 128
    return value if shift == 0 else pltpu.roll(value, shift, value.ndim - 1)


def euler(u, d):
    rho, mom, energy = u[0], u[1:4], u[4]
    inv = 1.0 / rho
    normal = mom[d] * inv
    kinetic = 0.5 * (mom[0] * mom[0] + mom[1] * mom[1] + mom[2] * mom[2]) * inv
    pressure = (HEAT_RATIO - 1.0) * (energy - kinetic)
    sound = jnp.sqrt(HEAT_RATIO * pressure * inv)
    flux = [mom[d], mom[0] * normal, mom[1] * normal, mom[2] * normal, (energy + pressure) * normal]
    flux[1 + d] = flux[1 + d] + pressure
    return flux, jnp.abs(normal) + sound


def upwind(left, left_flux, left_speed, right, right_flux, right_speed):
    half = 0.5 * jnp.maximum(left_speed, right_speed)
    return [0.5 * (fl + fr) - half * (ur - ul) for ul, fl, ur, fr in zip(left, left_flux, right, right_flux)]


def rusanov(left, right, d):
    return upwind(left, *euler(left, d), right, *euler(right, d))


def faces_kernel(x_hbm, out_ref, x_ref, arrived):
    parts = ((3, 2), (0, 1), (7, 1), (1, 2), (5, 2))
    copies = [
        pltpu.make_async_copy(
            x_hbm.at[pl.ds(e * ROWS, many * ROWS)], x_ref.at[pl.ds(e * ROWS, many * ROWS)], arrived.at[n]
        )
        for n, (e, many) in enumerate(parts)
    ]
    for copy in copies:
        copy.start()
    lane = lanes_of((ROWS, 128))
    for copy in copies[:3]:
        copy.wait()
    for face, (ey, j) in enumerate(((0, 0), (3, 7))):
        packed = None
        for ex in range(2):
            for chunk in range(4):
                goal = 32 * ex + 8 * chunk
                piece = x_ref[pl.ds((ex * 4 + ey) * ROWS, ROWS), chunk * 128 : (chunk + 1) * 128]
                piece = roll(piece, goal - 8 * j)
                packed = piece if packed is None else jnp.where(lane % 64 >= goal, piece, packed)
        out_ref[pl.ds((4 + face) * ROWS, ROWS), :] = packed
    for copy in copies[3:]:
        copy.wait()
    for q in range(2):
        first = x_ref[pl.ds((2 * q) * ROWS, ROWS), 0:128]
        second = x_ref[pl.ds((2 * q + 1) * ROWS, ROWS), 0:128]
        out_ref[pl.ds(q * ROWS, ROWS), :] = jnp.where(lane < 64, first, roll(second, 64))
        first = x_ref[pl.ds((4 + 2 * q) * ROWS, ROWS), 384:512]
        second = x_ref[pl.ds((4 + 2 * q + 1) * ROWS, ROWS), 384:512]
        out_ref[pl.ds((2 + q) * ROWS, ROWS), :] = jnp.where(lane < 64, roll(first, 64), second)
    lane = lanes_of((8, 128))
    sub = lax.broadcasted_iota(jnp.int32, (8, 128), 0)
    for comp in range(5):
        packed = None
        for face, (ez, k) in enumerate(((0, 0), (7, 7))):
            for chunk in range(4):
                piece = None
                for e in range(8):
                    row = x_ref[pl.ds(e * ROWS + comp * 8 + ez, 1), chunk * 128 : (chunk + 1) * 128]
                    row = jnp.broadcast_to(row, (8, 128))
                    piece = row if piece is None else jnp.where(sub == e, row, piece)
                goal = 4 * face + chunk
                piece = roll(piece, goal - k)
                packed = piece if packed is None else jnp.where(lane % 8 >= goal, piece, packed)
        out_ref[pl.ds(6 * ROWS + comp * 8, 8), :] = packed


def inner_kernel(x_ref, troubled_ref, level_ref, out_ref, u_ref, flux_ref, speed_ref, acc_ref, acc_x_ref):
    weak, scale = weak_matrix(), [GRID_SCALE / w for w in LOBATTO_WEIGHTS]
    lane = lanes_of((8, 128))
    k = lax.broadcasted_iota(jnp.int32, (8, 128), 0)
    upper, ex, ey, ez = lane >= 64, (lane // 32) % 2, (lane // 8) % 4, lane % 8
    blend = jnp.zeros((8, 128), jnp.float32)
    for x in range(2):
        marks = (troubled_ref[x] * level_ref[x]).astype(jnp.float32)
        marks = jnp.dot(marks, jnp.where(ez == k, 1.0, 0.0), preferred_element_type=jnp.float32)
        for y in range(4):
            row = jnp.broadcast_to(marks[y : y + 1, :], (8, 128))
            blend = jnp.where((ex == x) & (ey == y), row, blend)
    blend = blend / 5.0
    smooth, half_blend = 1.0 - blend, 0.5 * blend

    def by_row(values):
        value = jnp.full((8, 128), float(values[0]), jnp.float32)
        for n in range(1, 8):
            value = jnp.where(k == n, float(values[n]), value)
        return value

    def by_half(low, high):
        return jnp.where(upper, float(high), float(low))

    def rows(row):
        return pl.ds(pl.multiple_of(row, 8), 8)

    for n in range(5):
        for h in range(2):
            parts = [
                x_ref[pl.ds(e * ROWS + 8 * n, 8), 256 * g + 128 * h : 256 * g + 128 * h + 128]
                for g in range(2)
                for e in range(8)
            ]
            u_ref[n, pl.ds(128 * h, 128), :] = jnp.concatenate(parts, axis=0).T

    weak_z = [by_row([weak[r][(r + s) % 8] for r in range(8)]) for s in range(8)]
    scale_z = by_row(scale)
    weight_z = jnp.where(k == 7, 0.0, half_blend)

    def first(t, carry):
        at = rows(t * 8)
        u = [u_ref[n, at, :] for n in range(5)]
        rho, mom, energy = u[0], u[1:4], u[4]
        inv = 1.0 / rho
        vel = [m * inv for m in mom]
        kinetic = 0.5 * (mom[0] * vel[0] + mom[1] * vel[1] + mom[2] * vel[2])
        pressure = (HEAT_RATIO - 1.0) * (energy - kinetic)
        sound = jnp.sqrt(HEAT_RATIO * pressure * inv)
        total = energy + pressure
        for d in range(3):
            f = [mom[d]] + [mom[n] * vel[d] for n in range(3)] + [total * vel[d]]
            f[1 + d] = f[1 + d] + pressure
            speed = jnp.abs(vel[d]) + sound
            speed_ref[d, at, :] = speed
            for n in range(1, 5):
                flux_ref[d, n - 1, at, :] = f[n]
        largest = jnp.maximum(speed, pltpu.roll(speed, 7, 0))
        for n in range(5):
            turned = [f[n]] + [pltpu.roll(f[n], 8 - s, 0) for s in range(1, 8)]
            volume = weak_z[0] * turned[0]
            for s in range(1, 8):
                volume = volume + weak_z[s] * turned[s]
            g = weight_z * (f[n] + turned[1] - largest * (pltpu.roll(u[n], 7, 0) - u[n]))
            acc_ref[n, at, :] = smooth * volume + scale_z * (pltpu.roll(g, 1, 0) - g)
        return carry

    lax.fori_loop(0, 32, first, 0, unroll=4)

    def flux(d, n, at):
        return u_ref[1 + d, at, :] if n == 0 else flux_ref[d, n - 1, at, :]

    def between(i, carry):
        last, start = pl.ds(i * 64 + 7, 8, stride=8), pl.ds(i * 64, 8, stride=8)
        weight = jnp.where(ez < 7, 0.5 * EDGE, 0.0)
        largest = jnp.maximum(speed_ref[2, last, :], roll(speed_ref[2, start, :], -1))
        for n in range(5):
            jump = roll(u_ref[n, start, :], -1) - u_ref[n, last, :]
            star = weight * (flux(2, n, last) + roll(flux(2, n, start), -1) - largest * jump)
            acc_ref[n, last, :] = acc_ref[n, last, :] - star
            acc_ref[n, start, :] = acc_ref[n, start, :] + roll(star, 1)
        return carry

    lax.fori_loop(0, 4, between, 0, unroll=4)

    end_y = jnp.where(ey < 3, 0.5, 0.0)

    def second(i, carry):
        at = [rows(i * 64 + 8 * j) for j in range(8)]
        speed = [speed_ref[1, a, :] for a in at]
        largest = [jnp.maximum(speed[j], speed[j + 1]) for j in range(7)]
        largest.append(jnp.maximum(speed[7], roll(speed[0], -8)))
        for n in range(5):
            u, f = [u_ref[n, a, :] for a in at], [flux(1, n, a) for a in at]
            g = [half_blend * (f[j] + f[j + 1] - largest[j] * (u[j + 1] - u[j])) for j in range(7)]
            g.append(end_y * (f[7] + roll(f[0], -8) - largest[7] * (roll(u[0], -8) - u[7])))
            even, odd = [f[m] + f[7 - m] for m in range(4)], [f[m] - f[7 - m] for m in range(4)]
            volumes = [None] * 8
            for j in range(4):
                from_odd, from_even = (
                    sum(float(0.5 * (weak[j][m] + sign * weak[j][7 - m])) * part[m] for m in range(4))
                    for sign, part in ((-1, odd), (1, even))
                )
                volumes[j], volumes[7 - j] = from_odd + from_even, from_odd - from_even
            for j in range(8):
                volume = volumes[j]
                low = g[j - 1] if j else roll(g[7], 8)
                acc_ref[n, at[j], :] = acc_ref[n, at[j], :] + (smooth * volume + scale[j] * (low - g[j]))
        return carry


    weak_x = [[by_half(weak[r][m], weak[4 + r][4 + m]) for m in range(4)] for r in range(4)]
    cross_x = [[by_half(weak[r][4 + m], weak[4 + r][m]) for m in range(4)] for r in range(4)]
    scale_x = [by_half(scale[r], scale[4 + r]) for r in range(4)]
    end_x = jnp.where(upper, jnp.where(ex == 0, 0.5, 0.0), half_blend)

    def following(value, swapped):
        return jnp.where(upper, roll(value, 32), swapped)

    def third(j, carry):
        at = [rows(i * 64 + 8 * j) for i in range(4)]
        speed = [speed_ref[0, a, :] for a in at]
        largest = [jnp.maximum(speed[i], speed[i + 1]) for i in range(3)]
        largest.append(jnp.maximum(speed[3], following(speed[0], roll(speed[0], 64))))
        for n in range(5):
            u, f = [u_ref[n, a, :] for a in at], [flux(0, n, a) for a in at]
            swapped = [roll(v, 64) for v in f]
            g = [half_blend * (f[i] + f[i + 1] - largest[i] * (u[i + 1] - u[i])) for i in range(3)]
            jump = following(u[0], roll(u[0], 64)) - u[3]
            g.append(end_x * (f[3] + following(f[0], swapped[0]) - largest[3] * jump))
            start = jnp.where(upper, roll(g[3], 64), jnp.where(ex == 1, roll(g[3], -32), 0.0))
            for i in range(4):
                volume = weak_x[i][0] * f[0] + cross_x[i][0] * swapped[0]
                for m in range(1, 4):
                    volume = volume + weak_x[i][m] * f[m] + cross_x[i][m] * swapped[m]
                low = g[i - 1] if i else start
                acc_x_ref[n, at[i], :] = smooth * volume + scale_x[i] * (low - g[i])
        return carry

    def both(t, carry):
        second(t, carry)
        third(2 * t, carry)
        third(2 * t + 1, carry)
        return carry

    lax.fori_loop(0, 4, both, 0)

    for n in range(5):
        for h in range(2):
            at = pl.ds(128 * h, 128)
            block = (acc_ref[n, at, :] + acc_x_ref[n, at, :]).T
            for g in range(2):
                for e in range(8):
                    out_ref[pl.ds(e * ROWS + 8 * n, 8), 256 * g + 128 * h : 256 * g + 128 * h + 128] = block[
                        64 * g + 8 * e : 64 * g + 8 * e + 8, :
                    ]


def early_kernel(early_ref, x_hbm, troubled_hbm, level_hbm, out_ref, x_ref, troubled_ref, level_ref, here, *scratch):
    @pl.when(early_ref[0] != 0)
    def _():
        ends = ((x_hbm, x_ref), (troubled_hbm, troubled_ref), (level_hbm, level_ref))
        copies = [pltpu.make_async_copy(a, b, here.at[n]) for n, (a, b) in enumerate(ends)]
        for copy in copies:
            copy.start()
        for copy in copies:
            copy.wait()
        inner_kernel(x_ref, troubled_ref, level_ref, out_ref, *scratch)


def late_kernel(early_ref, done_ref, far_ref, *refs):
    del far_ref
    @pl.when(early_ref[0] != 0)
    def _():
        refs[3][...] = done_ref[...]

    @pl.when(early_ref[0] == 0)
    def _():
        inner_kernel(*refs)


def outer_kernel(place_ref, pre_ref, own_ref, halo_ref, near_ref, far_ref, out_hbm, out_ref, star_ref, left_sem):
    lane = lanes_of((8, 128))
    sub = lax.broadcasted_iota(jnp.int32, (8, 128), 0)
    left_half, low_face = lane < 64, lane % 8 < 4
    core, odd_x, odd_y = place_ref[0], place_ref[1], place_ref[2]
    zero = jnp.zeros((8, 128), jnp.float32)

    def own(tile):
        return own_ref[pl.ds(tile * 8, 8), :]

    first_core = core == 0
    mine = [own(30 + n) for n in range(5)]
    other = []
    for n in range(5):
        near = near_ref[1 - core, pl.ds((30 + n) * 8, 8), :]
        far = far_ref[pl.ds(n * 8, 8), :]
        above = jnp.where(first_core, near, far)
        below = jnp.where(first_core, far, near)
        other.append(jnp.where(low_face, roll(below, -4), roll(above, 4)))
    left = [jnp.where(low_face, o, m) for o, m in zip(other, mine)]
    right = [jnp.where(low_face, m, o) for o, m in zip(other, mine)]
    for n, star in enumerate(rusanov(left, right, 2)):
        star = EDGE * star
        for c in range(4):
            cols = slice(c * 128, (c + 1) * 128)
            star_ref[pl.ds(8 * n, 8), cols] = jnp.where(lane % 8 == 0, roll(star, -c), zero)
            star_ref[pl.ds(ROWS + 8 * n, 8), cols] = jnp.where(lane % 8 == 7, -roll(star, 3 - c), zero)

    along_x = {}
    for q in range(2):
        mine = [own(5 * q + n) for n in range(5)]
        below = [halo_ref[0, odd_x, core, pl.ds((5 * q + n) * 8, 8), :] for n in range(5)]
        for n, star in enumerate(rusanov(below, mine, 0)):
            star = EDGE * star
            along_x[2 * q, n] = jnp.where(left_half, star, zero)
            along_x[2 * q + 1, n] = jnp.where(left_half, roll(star, 64), zero)
        mine = [own(10 + 5 * q + n) for n in range(5)]
        above = [halo_ref[0, 1 - odd_x, core, pl.ds((5 * q + n) * 8, 8), :] for n in range(5)]
        for n, star in enumerate(rusanov(mine, above, 0)):
            star = -EDGE * star
            along_x[4 + 2 * q, n] = jnp.where(left_half, zero, roll(star, 64))
            along_x[5 + 2 * q, n] = jnp.where(left_half, zero, star)

    mine = [own(20 + n) for n in range(5)]
    below = [halo_ref[1, odd_y, core, pl.ds((5 + n) * 8, 8), :] for n in range(5)]
    low_y = [EDGE * s for s in rusanov(below, mine, 1)]
    mine = [own(25 + n) for n in range(5)]
    above = [halo_ref[1, 1 - odd_y, core, pl.ds(n * 8, 8), :] for n in range(5)]
    high_y = [-EDGE * s for s in rusanov(mine, above, 1)]
    row_j = (lane // 8) % 8

    copies = []
    for e in (1, 2, 5, 6, 0, 3, 4, 7):
        ex, ey = e // 4, e % 4
        for n in range(5):
            for c in range(4):
                cols = slice(c * 128, (c + 1) * 128)
                value = pre_ref[pl.ds(e * ROWS + 8 * n, 8), cols]
                low = jnp.broadcast_to(star_ref[pl.ds(8 * n + e, 1), cols], (8, 128))
                high = jnp.broadcast_to(star_ref[pl.ds(ROWS + 8 * n + e, 1), cols], (8, 128))
                value = value + jnp.where(sub == 0, low, jnp.where(sub == 7, high, zero))
                if c == (0, 3)[ex]:
                    value = value + along_x[e, n]
                start = 32 * ex + 8 * c
                if ey == 0:
                    value = value + jnp.where(row_j == 0, roll(low_y[n], -start), zero)
                if ey == 3:
                    value = value + jnp.where(row_j == 7, roll(high_y[n], 56 - start), zero)
                out_ref[pl.ds(e * ROWS + 8 * n, 8), cols] = value
        at = pl.ds(e * ROWS, ROWS)
        copies.append(pltpu.make_async_copy(out_ref.at[at], out_hbm.at[at], left_sem.at[e]))
        copies[-1].start()
    for copy in copies:
        copy.wait()


def pairs(size, shift):
    return [[(2 * n + shift) % size, (2 * n + 1 + shift) % size] for n in range(size // 2)]


def crossed(sizes, shift, first, last):
    nx, ny, nz = sizes
    moves = []
    for z in range(first, last):
        for a, b in pairs(nx, shift) if z % 2 == 0 else pairs(ny, shift):
            for other in range(ny if z % 2 == 0 else nx):
                ends = [((v * ny + other) if z % 2 == 0 else (other * ny + v)) * nz + z for v in (a, b)]
                moves += [(ends[0], ends[1]), (ends[1], ends[0])]
    return sorted(set(moves))


def in_vmem():
    return pl.BlockSpec(memory_space=pltpu.VMEM)


def in_hbm():
    return pl.BlockSpec(memory_space=pltpu.HBM)


LIMIT = pltpu.CompilerParams(vmem_limit_bytes=32 * 1024 * 1024)


def on_device(conserved, troubled, blend_level):
    sizes = [lax.axis_size(a) for a in AXES]
    ix, iy, iz = [lax.axis_index(a) for a in AXES]
    core, odd_x, odd_y = iz & 1, ix & 1, iy & 1
    state = conserved.transpose(0, 1, 3, 2, 4).reshape(8 * ROWS, 512)

    own = pl.pallas_call(
        faces_kernel,
        out_shape=jax.ShapeDtypeStruct((7 * ROWS, 128), jnp.float32),
        in_specs=[in_hbm()],
        out_specs=in_vmem(),
        scratch_shapes=[pltpu.VMEM((8 * ROWS, 512), jnp.float32), pltpu.SemaphoreType.DMA((5,))],
        compiler_params=LIMIT,
        name="faces",
    )(pltpu.with_memory_space_constraint(state, pltpu.HBM))

    both = lax.all_gather(own, "gz", axis_index_groups=pairs(sizes[2], 0))
    x_faces = both[:, : 4 * ROWS].reshape(2, 2, 2 * ROWS, 128)
    y_faces = both[:, 4 * ROWS : 6 * ROWS]
    sent = []
    for shift in range(2):
        face = odd_x if shift else 1 - odd_x
        x_part = lax.dynamic_index_in_dim(x_faces, face, 1, keepdims=False)
        sent.append(jnp.where(core == 0, x_part, y_faces))
    ahead = [lax.ppermute(v, AXES, crossed(sizes, n, 0, 2)) for n, v in enumerate(sent)]

    early = (iz < 2).astype(jnp.int32).reshape(1)
    work = [
        pltpu.VMEM((5, 256, 128), jnp.float32),
        pltpu.VMEM((3, 4, 256, 128), jnp.float32),
        pltpu.VMEM((3, 256, 128), jnp.float32),
        pltpu.VMEM((5, 256, 128), jnp.float32),
        pltpu.VMEM((5, 256, 128), jnp.float32),
    ]
    inner_call = functools.partial(
        pl.pallas_call,
        out_shape=jax.ShapeDtypeStruct((8 * ROWS, 512), jnp.float32),
        out_specs=in_vmem(),
        compiler_params=LIMIT,
        cost_estimate=pl.CostEstimate(flops=20_000_000, bytes_accessed=1_400_000, transcendentals=65536),
    )
    in_smem = pl.BlockSpec(memory_space=pltpu.SMEM)
    mine = [
        pltpu.VMEM((8 * ROWS, 512), jnp.float32),
        pltpu.VMEM((2, 4, 8), jnp.int32),
        pltpu.VMEM((2, 4, 8), jnp.int32),
        pltpu.SemaphoreType.DMA((3,)),
    ]
    done = inner_call(
        early_kernel, in_specs=[in_smem] + [in_hbm()] * 3, scratch_shapes=mine + work, name="early"
    )(early, *[pltpu.with_memory_space_constraint(v, pltpu.HBM) for v in (state, troubled, blend_level)])
    z_faces, sent, done = lax.optimization_barrier((own[6 * ROWS :], sent, done))
    swap = pairs(sizes[2], 1)
    far = lax.ppermute(z_faces, "gz", [(a, b) for a, b in swap] + [(b, a) for a, b in swap])
    after = [lax.ppermute(v, AXES, crossed(sizes, n, 2, sizes[2])) for n, v in enumerate(sent)]

    inner = inner_call(late_kernel, in_specs=[in_smem] + [in_vmem()] * 5, scratch_shapes=work, name="late")(
        early, done, far, state, troubled, blend_level
    )

    halo = lax.all_gather(jnp.stack([ahead[1] + after[1], ahead[0] + after[0]]), "gz", axis_index_groups=pairs(sizes[2], 0))
    place = jnp.stack([core, odd_x, odd_y]).astype(jnp.int32)
    full = pl.pallas_call(
        outer_kernel,
        out_shape=jax.ShapeDtypeStruct((8 * ROWS, 512), jnp.float32),
        in_specs=[pl.BlockSpec(memory_space=pltpu.SMEM)] + [in_vmem()] * 5,
        out_specs=in_hbm(),
        scratch_shapes=[
            pltpu.VMEM((8 * ROWS, 512), jnp.float32),
            pltpu.VMEM((2 * ROWS, 512), jnp.float32),
            pltpu.SemaphoreType.DMA((8,)),
        ],
        compiler_params=LIMIT,
        name="outer",
    )(place, inner, own, halo, both, far)
    return full.reshape(2, 4, 5, 8, 512).transpose(0, 1, 3, 2, 4)


def solution(mesh):
    placed = (P("gx", "gy", "gz", None, None), P("gx", "gy", "gz"), P("gx", "gy", "gz"))
    return jax.shard_map(
        on_device,
        mesh=mesh,
        in_specs=placed,
        out_specs=P("gx", "gy", "gz", None, None),
        check_vma=False,
    )
```

```python
import jax
import jax.numpy as jnp
import numpy as np
from jax import lax
from jax.experimental import pallas as pl
from jax.experimental.pallas import tpu as pltpu
from jax.sharding import PartitionSpec as P

AXES = ("gx", "gy", "gz")
HEAT_RATIO = 1.4
GRID_SCALE = 0.05
LOBATTO_POINTS = [
    -1.0,
    -0.8717401485096066,
    -0.5917001814331423,
    -0.2092992179024789,
    0.2092992179024789,
    0.5917001814331423,
    0.8717401485096066,
    1.0,
]
LOBATTO_WEIGHTS = [
    0.03571428571428571,
    0.21070422714350603,
    0.34112269248350435,
    0.4124587946587039,
    0.4124587946587039,
    0.34112269248350435,
    0.21070422714350603,
    0.03571428571428571,
]
EDGE = GRID_SCALE / LOBATTO_WEIGHTS[0]
ROWS = 40


def weak_matrix():
    points = np.array(LOBATTO_POINTS)
    weights = np.array(LOBATTO_WEIGHTS)
    bary = np.array([1.0 / np.prod([points[i] - points[j] for j in range(8) if j != i]) for i in range(8)])
    derivative = np.zeros((8, 8))
    for i in range(8):
        for j in range(8):
            if i != j:
                derivative[i, j] = bary[j] / bary[i] / (points[i] - points[j])
        derivative[i, i] = -np.sum(derivative[i])
    derivative[0, 0] += 1.0 / weights[0]
    derivative[7, 7] -= 1.0 / weights[0]
    return -GRID_SCALE * derivative


def lanes_of(shape):
    return lax.broadcasted_iota(jnp.int32, shape, len(shape) - 1)


def roll(value, shift):
    shift = shift % 128
    return value if shift == 0 else pltpu.roll(value, shift, value.ndim - 1)


def euler(u, d):
    rho, mom, energy = u[0], u[1:4], u[4]
    inv = 1.0 / rho
    normal = mom[d] * inv
    kinetic = 0.5 * (mom[0] * mom[0] + mom[1] * mom[1] + mom[2] * mom[2]) * inv
    pressure = (HEAT_RATIO - 1.0) * (energy - kinetic)
    sound = jnp.sqrt(HEAT_RATIO * pressure * inv)
    flux = [mom[d], mom[0] * normal, mom[1] * normal, mom[2] * normal, (energy + pressure) * normal]
    flux[1 + d] = flux[1 + d] + pressure
    return flux, jnp.abs(normal) + sound


def upwind(left, left_flux, left_speed, right, right_flux, right_speed):
    half = 0.5 * jnp.maximum(left_speed, right_speed)
    return [0.5 * (fl + fr) - half * (ur - ul) for ul, fl, ur, fr in zip(left, left_flux, right, right_flux)]


def rusanov(left, right, d):
    return upwind(left, *euler(left, d), right, *euler(right, d))


def faces_kernel(x_hbm, out_ref, x_ref, arrived):
    parts = ((3, 2), (0, 1), (7, 1), (1, 2), (5, 2))
    copies = [
        pltpu.make_async_copy(
            x_hbm.at[pl.ds(e * ROWS, many * ROWS)], x_ref.at[pl.ds(e * ROWS, many * ROWS)], arrived.at[n]
        )
        for n, (e, many) in enumerate(parts)
    ]
    for copy in copies:
        copy.start()
    lane = lanes_of((ROWS, 128))
    for copy in copies[:3]:
        copy.wait()
    for face, (ey, j) in enumerate(((0, 0), (3, 7))):
        packed = None
        for ex in range(2):
            for chunk in range(4):
                goal = 32 * ex + 8 * chunk
                piece = x_ref[pl.ds((ex * 4 + ey) * ROWS, ROWS), chunk * 128 : (chunk + 1) * 128]
                piece = roll(piece, goal - 8 * j)
                packed = piece if packed is None else jnp.where(lane % 64 >= goal, piece, packed)
        out_ref[pl.ds((4 + face) * ROWS, ROWS), :] = packed
    for copy in copies[3:]:
        copy.wait()
    for q in range(2):
        first = x_ref[pl.ds((2 * q) * ROWS, ROWS), 0:128]
        second = x_ref[pl.ds((2 * q + 1) * ROWS, ROWS), 0:128]
        out_ref[pl.ds(q * ROWS, ROWS), :] = jnp.where(lane < 64, first, roll(second, 64))
        first = x_ref[pl.ds((4 + 2 * q) * ROWS, ROWS), 384:512]
        second = x_ref[pl.ds((4 + 2 * q + 1) * ROWS, ROWS), 384:512]
        out_ref[pl.ds((2 + q) * ROWS, ROWS), :] = jnp.where(lane < 64, roll(first, 64), second)
    lane = lanes_of((8, 128))
    sub = lax.broadcasted_iota(jnp.int32, (8, 128), 0)
    for comp in range(5):
        packed = None
        for face, (ez, k) in enumerate(((0, 0), (7, 7))):
            for chunk in range(4):
                piece = None
                for e in range(8):
                    row = x_ref[pl.ds(e * ROWS + comp * 8 + ez, 1), chunk * 128 : (chunk + 1) * 128]
                    row = jnp.broadcast_to(row, (8, 128))
                    piece = row if piece is None else jnp.where(sub == e, row, piece)
                goal = 4 * face + chunk
                piece = roll(piece, goal - k)
                packed = piece if packed is None else jnp.where(lane % 8 >= goal, piece, packed)
        out_ref[pl.ds(6 * ROWS + comp * 8, 8), :] = packed


def inner_kernel(x_ref, troubled_ref, level_ref, out_ref, u_ref, flux_ref, speed_ref, acc_ref, acc_x_ref):
    weak, scale = weak_matrix(), [GRID_SCALE / w for w in LOBATTO_WEIGHTS]
    lane = lanes_of((8, 128))
    k = lax.broadcasted_iota(jnp.int32, (8, 128), 0)
    upper, ex, ey, ez = lane >= 64, (lane // 32) % 2, (lane // 8) % 4, lane % 8
    blend = jnp.zeros((8, 128), jnp.float32)
    for x in range(2):
        marks = (troubled_ref[x] * level_ref[x]).astype(jnp.float32)
        marks = jnp.dot(marks, jnp.where(ez == k, 1.0, 0.0), preferred_element_type=jnp.float32)
        for y in range(4):
            row = jnp.broadcast_to(marks[y : y + 1, :], (8, 128))
            blend = jnp.where((ex == x) & (ey == y), row, blend)
    blend = blend / 5.0
    smooth, half_blend = 1.0 - blend, 0.5 * blend

    def by_row(values):
        value = jnp.full((8, 128), float(values[0]), jnp.float32)
        for n in range(1, 8):
            value = jnp.where(k == n, float(values[n]), value)
        return value

    def by_half(low, high):
        return jnp.where(upper, float(high), float(low))

    def rows(row):
        return pl.ds(pl.multiple_of(row, 8), 8)

    for n in range(5):
        for h in range(2):
            parts = [
                x_ref[pl.ds(e * ROWS + 8 * n, 8), 256 * g + 128 * h : 256 * g + 128 * h + 128]
                for g in range(2)
                for e in range(8)
            ]
            u_ref[n, pl.ds(128 * h, 128), :] = jnp.concatenate(parts, axis=0).T

    weak_z = [by_row([weak[r][(r + s) % 8] for r in range(8)]) for s in range(8)]
    scale_z = by_row(scale)
    weight_z = jnp.where(k == 7, 0.0, half_blend)

    def first(t, carry):
        at = rows(t * 8)
        u = [u_ref[n, at, :] for n in range(5)]
        rho, mom, energy = u[0], u[1:4], u[4]
        inv = 1.0 / rho
        vel = [m * inv for m in mom]
        kinetic = 0.5 * (mom[0] * vel[0] + mom[1] * vel[1] + mom[2] * vel[2])
        pressure = (HEAT_RATIO - 1.0) * (energy - kinetic)
        sound = jnp.sqrt(HEAT_RATIO * pressure * inv)
        total = energy + pressure
        for d in range(3):
            f = [mom[d]] + [mom[n] * vel[d] for n in range(3)] + [total * vel[d]]
            f[1 + d] = f[1 + d] + pressure
            speed = jnp.abs(vel[d]) + sound
            speed_ref[d, at, :] = speed
            for n in range(1, 5):
                flux_ref[d, n - 1, at, :] = f[n]
        largest = jnp.maximum(speed, pltpu.roll(speed, 7, 0))
        for n in range(5):
            turned = [f[n]] + [pltpu.roll(f[n], 8 - s, 0) for s in range(1, 8)]
            volume = weak_z[0] * turned[0]
            for s in range(1, 8):
                volume = volume + weak_z[s] * turned[s]
            g = weight_z * (f[n] + turned[1] - largest * (pltpu.roll(u[n], 7, 0) - u[n]))
            acc_ref[n, at, :] = smooth * volume + scale_z * (pltpu.roll(g, 1, 0) - g)
        return carry

    lax.fori_loop(0, 32, first, 0, unroll=4)

    def flux(d, n, at):
        return u_ref[1 + d, at, :] if n == 0 else flux_ref[d, n - 1, at, :]

    def between(i, carry):
        last, start = pl.ds(i * 64 + 7, 8, stride=8), pl.ds(i * 64, 8, stride=8)
        weight = jnp.where(ez < 7, 0.5 * EDGE, 0.0)
        largest = jnp.maximum(speed_ref[2, last, :], roll(speed_ref[2, start, :], -1))
        for n in range(5):
            jump = roll(u_ref[n, start, :], -1) - u_ref[n, last, :]
            star = weight * (flux(2, n, last) + roll(flux(2, n, start), -1) - largest * jump)
            acc_ref[n, last, :] = acc_ref[n, last, :] - star
            acc_ref[n, start, :] = acc_ref[n, start, :] + roll(star, 1)
        return carry

    lax.fori_loop(0, 4, between, 0, unroll=4)

    end_y = jnp.where(ey < 3, 0.5, 0.0)

    def second(i, carry):
        at = [rows(i * 64 + 8 * j) for j in range(8)]
        speed = [speed_ref[1, a, :] for a in at]
        largest = [jnp.maximum(speed[j], speed[j + 1]) for j in range(7)]
        largest.append(jnp.maximum(speed[7], roll(speed[0], -8)))
        for n in range(5):
            u, f = [u_ref[n, a, :] for a in at], [flux(1, n, a) for a in at]
            g = [half_blend * (f[j] + f[j + 1] - largest[j] * (u[j + 1] - u[j])) for j in range(7)]
            g.append(end_y * (f[7] + roll(f[0], -8) - largest[7] * (roll(u[0], -8) - u[7])))
            even, odd = [f[m] + f[7 - m] for m in range(4)], [f[m] - f[7 - m] for m in range(4)]
            volumes = [None] * 8
            for j in range(4):
                from_odd, from_even = (
                    sum(float(0.5 * (weak[j][m] + sign * weak[j][7 - m])) * part[m] for m in range(4))
                    for sign, part in ((-1, odd), (1, even))
                )
                volumes[j], volumes[7 - j] = from_odd + from_even, from_odd - from_even
            for j in range(8):
                volume = volumes[j]
                low = g[j - 1] if j else roll(g[7], 8)
                acc_ref[n, at[j], :] = acc_ref[n, at[j], :] + (smooth * volume + scale[j] * (low - g[j]))
        return carry


    weak_x = [[by_half(weak[r][m], weak[4 + r][4 + m]) for m in range(4)] for r in range(4)]
    cross_x = [[by_half(weak[r][4 + m], weak[4 + r][m]) for m in range(4)] for r in range(4)]
    scale_x = [by_half(scale[r], scale[4 + r]) for r in range(4)]
    end_x = jnp.where(upper, jnp.where(ex == 0, 0.5, 0.0), half_blend)

    def following(value, swapped):
        return jnp.where(upper, roll(value, 32), swapped)

    def third(j, carry):
        at = [rows(i * 64 + 8 * j) for i in range(4)]
        speed = [speed_ref[0, a, :] for a in at]
        largest = [jnp.maximum(speed[i], speed[i + 1]) for i in range(3)]
        largest.append(jnp.maximum(speed[3], following(speed[0], roll(speed[0], 64))))
        for n in range(5):
            u, f = [u_ref[n, a, :] for a in at], [flux(0, n, a) for a in at]
            swapped = [roll(v, 64) for v in f]
            g = [half_blend * (f[i] + f[i + 1] - largest[i] * (u[i + 1] - u[i])) for i in range(3)]
            jump = following(u[0], roll(u[0], 64)) - u[3]
            g.append(end_x * (f[3] + following(f[0], swapped[0]) - largest[3] * jump))
            start = jnp.where(upper, roll(g[3], 64), jnp.where(ex == 1, roll(g[3], -32), 0.0))
            for i in range(4):
                volume = weak_x[i][0] * f[0] + cross_x[i][0] * swapped[0]
                for m in range(1, 4):
                    volume = volume + weak_x[i][m] * f[m] + cross_x[i][m] * swapped[m]
                low = g[i - 1] if i else start
                acc_x_ref[n, at[i], :] = smooth * volume + scale_x[i] * (low - g[i])
        return carry

    def both(t, carry):
        second(t, carry)
        third(2 * t, carry)
        third(2 * t + 1, carry)
        return carry

    lax.fori_loop(0, 4, both, 0)

    for n in range(5):
        for h in range(2):
            at = pl.ds(128 * h, 128)
            block = (acc_ref[n, at, :] + acc_x_ref[n, at, :]).T
            for g in range(2):
                for e in range(8):
                    out_ref[pl.ds(e * ROWS + 8 * n, 8), 256 * g + 128 * h : 256 * g + 128 * h + 128] = block[
                        64 * g + 8 * e : 64 * g + 8 * e + 8, :
                    ]


def middle_kernel(far_ref, *refs):
    del far_ref
    inner_kernel(*refs)


def pick_kernel(core_ref, both_ref, ahead_ref, out_ref):
    del ahead_ref
    out_ref[...] = both_ref[core_ref[0], pl.ds(6 * ROWS, ROWS), :]


def outer_kernel(place_ref, pre_ref, own_ref, halo_ref, near_ref, far_ref, out_hbm, out_ref, star_ref, left_sem):
    lane = lanes_of((8, 128))
    sub = lax.broadcasted_iota(jnp.int32, (8, 128), 0)
    left_half, low_face = lane < 64, lane % 8 < 4
    core, odd_x, odd_y = place_ref[0], place_ref[1], place_ref[2]
    zero = jnp.zeros((8, 128), jnp.float32)

    def own(tile):
        return own_ref[pl.ds(tile * 8, 8), :]

    first_core = core == 0
    mine = [own(30 + n) for n in range(5)]
    other = []
    for n in range(5):
        near = near_ref[1 - core, pl.ds((30 + n) * 8, 8), :]
        far = far_ref[pl.ds(n * 8, 8), :]
        above = jnp.where(first_core, near, far)
        below = jnp.where(first_core, far, near)
        other.append(jnp.where(low_face, roll(below, -4), roll(above, 4)))
    left = [jnp.where(low_face, o, m) for o, m in zip(other, mine)]
    right = [jnp.where(low_face, m, o) for o, m in zip(other, mine)]
    for n, star in enumerate(rusanov(left, right, 2)):
        star = EDGE * star
        for c in range(4):
            cols = slice(c * 128, (c + 1) * 128)
            star_ref[pl.ds(8 * n, 8), cols] = jnp.where(lane % 8 == 0, roll(star, -c), zero)
            star_ref[pl.ds(ROWS + 8 * n, 8), cols] = jnp.where(lane % 8 == 7, -roll(star, 3 - c), zero)

    along_x = {}
    for q in range(2):
        mine = [own(5 * q + n) for n in range(5)]
        below = [halo_ref[0, odd_x, core, pl.ds((5 * q + n) * 8, 8), :] for n in range(5)]
        for n, star in enumerate(rusanov(below, mine, 0)):
            star = EDGE * star
            along_x[2 * q, n] = jnp.where(left_half, star, zero)
            along_x[2 * q + 1, n] = jnp.where(left_half, roll(star, 64), zero)
        mine = [own(10 + 5 * q + n) for n in range(5)]
        above = [halo_ref[0, 1 - odd_x, core, pl.ds((5 * q + n) * 8, 8), :] for n in range(5)]
        for n, star in enumerate(rusanov(mine, above, 0)):
            star = -EDGE * star
            along_x[4 + 2 * q, n] = jnp.where(left_half, zero, roll(star, 64))
            along_x[5 + 2 * q, n] = jnp.where(left_half, zero, star)

    mine = [own(20 + n) for n in range(5)]
    below = [halo_ref[1, odd_y, core, pl.ds((5 + n) * 8, 8), :] for n in range(5)]
    low_y = [EDGE * s for s in rusanov(below, mine, 1)]
    mine = [own(25 + n) for n in range(5)]
    above = [halo_ref[1, 1 - odd_y, core, pl.ds(n * 8, 8), :] for n in range(5)]
    high_y = [-EDGE * s for s in rusanov(mine, above, 1)]
    row_j = (lane // 8) % 8

    copies = []
    for e in (1, 2, 5, 6, 0, 3, 4, 7):
        ex, ey = e // 4, e % 4
        for n in range(5):
            for c in range(4):
                cols = slice(c * 128, (c + 1) * 128)
                value = pre_ref[pl.ds(e * ROWS + 8 * n, 8), cols]
                low = jnp.broadcast_to(star_ref[pl.ds(8 * n + e, 1), cols], (8, 128))
                high = jnp.broadcast_to(star_ref[pl.ds(ROWS + 8 * n + e, 1), cols], (8, 128))
                value = value + jnp.where(sub == 0, low, jnp.where(sub == 7, high, zero))
                if c == (0, 3)[ex]:
                    value = value + along_x[e, n]
                start = 32 * ex + 8 * c
                if ey == 0:
                    value = value + jnp.where(row_j == 0, roll(low_y[n], -start), zero)
                if ey == 3:
                    value = value + jnp.where(row_j == 7, roll(high_y[n], 56 - start), zero)
                out_ref[pl.ds(e * ROWS + 8 * n, 8), cols] = value
        at = pl.ds(e * ROWS, ROWS)
        copies.append(pltpu.make_async_copy(out_ref.at[at], out_hbm.at[at], left_sem.at[e]))
        copies[-1].start()
    for copy in copies:
        copy.wait()


def pairs(size, shift):
    return [[(2 * n + shift) % size, (2 * n + 1 + shift) % size] for n in range(size // 2)]


def crossed(sizes, shift, first, last):
    nx, ny, nz = sizes
    moves = []
    for z in range(first, last):
        for a, b in pairs(nx, shift) if z % 2 == 0 else pairs(ny, shift):
            for other in range(ny if z % 2 == 0 else nx):
                ends = [((v * ny + other) if z % 2 == 0 else (other * ny + v)) * nz + z for v in (a, b)]
                moves += [(ends[0], ends[1]), (ends[1], ends[0])]
    return sorted(set(moves))


def in_vmem():
    return pl.BlockSpec(memory_space=pltpu.VMEM)


def in_hbm():
    return pl.BlockSpec(memory_space=pltpu.HBM)


LIMIT = pltpu.CompilerParams(vmem_limit_bytes=32 * 1024 * 1024)


def on_device(conserved, troubled, blend_level):
    sizes = [lax.axis_size(a) for a in AXES]
    ix, iy, iz = [lax.axis_index(a) for a in AXES]
    core, odd_x, odd_y = iz & 1, ix & 1, iy & 1
    state = conserved.transpose(0, 1, 3, 2, 4).reshape(8 * ROWS, 512)

    own = pl.pallas_call(
        faces_kernel,
        out_shape=jax.ShapeDtypeStruct((7 * ROWS, 128), jnp.float32),
        in_specs=[in_hbm()],
        out_specs=in_vmem(),
        scratch_shapes=[pltpu.VMEM((8 * ROWS, 512), jnp.float32), pltpu.SemaphoreType.DMA((5,))],
        compiler_params=LIMIT,
        name="faces",
    )(pltpu.with_memory_space_constraint(state, pltpu.HBM))

    both = lax.all_gather(own, "gz", axis_index_groups=pairs(sizes[2], 0))
    x_faces = both[:, : 4 * ROWS].reshape(2, 2, 2 * ROWS, 128)
    y_faces = both[:, 4 * ROWS : 6 * ROWS]
    sent = []
    for shift in range(2):
        face = odd_x if shift else 1 - odd_x
        x_part = lax.dynamic_index_in_dim(x_faces, face, 1, keepdims=False)
        sent.append(jnp.where(core == 0, x_part, y_faces))
    half = sizes[2] // 2
    ahead = [lax.ppermute(v, AXES, crossed(sizes, n, 0, half)) for n, v in enumerate(sent)]

    in_smem = pl.BlockSpec(memory_space=pltpu.SMEM)
    z_faces = pl.pallas_call(
        pick_kernel,
        out_shape=jax.ShapeDtypeStruct((ROWS, 128), jnp.float32),
        in_specs=[in_smem] + [in_vmem()] * 2,
        out_specs=in_vmem(),
        compiler_params=LIMIT,
        name="pick",
    )(core.astype(jnp.int32).reshape(1), both, sent[0])
    z_faces, sent = lax.optimization_barrier((z_faces, sent))
    swap = pairs(sizes[2], 1)
    far = lax.ppermute(z_faces, "gz", [(a, b) for a, b in swap] + [(b, a) for a, b in swap])
    after = [lax.ppermute(v, AXES, crossed(sizes, n, half, sizes[2])) for n, v in enumerate(sent)]

    inner = pl.pallas_call(
        middle_kernel,
        out_shape=jax.ShapeDtypeStruct((8 * ROWS, 512), jnp.float32),
        in_specs=[in_vmem()] * 4,
        out_specs=in_vmem(),
        scratch_shapes=[
            pltpu.VMEM((5, 256, 128), jnp.float32),
            pltpu.VMEM((3, 4, 256, 128), jnp.float32),
            pltpu.VMEM((3, 256, 128), jnp.float32),
            pltpu.VMEM((5, 256, 128), jnp.float32),
            pltpu.VMEM((5, 256, 128), jnp.float32),
        ],
        compiler_params=LIMIT,
        cost_estimate=pl.CostEstimate(flops=20_000_000, bytes_accessed=1_400_000, transcendentals=65536),
        name="inner",
    )(far, state, troubled, blend_level)

    halo = lax.all_gather(jnp.stack([ahead[1] + after[1], ahead[0] + after[0]]), "gz", axis_index_groups=pairs(sizes[2], 0))
    place = jnp.stack([core, odd_x, odd_y]).astype(jnp.int32)
    full = pl.pallas_call(
        outer_kernel,
        out_shape=jax.ShapeDtypeStruct((8 * ROWS, 512), jnp.float32),
        in_specs=[pl.BlockSpec(memory_space=pltpu.SMEM)] + [in_vmem()] * 5,
        out_specs=in_hbm(),
        scratch_shapes=[
            pltpu.VMEM((8 * ROWS, 512), jnp.float32),
            pltpu.VMEM((2 * ROWS, 512), jnp.float32),
            pltpu.SemaphoreType.DMA((8,)),
        ],
        compiler_params=LIMIT,
        name="outer",
    )(place, inner, own, halo, both, far)
    return full.reshape(2, 4, 5, 8, 512).transpose(0, 1, 3, 2, 4)


def solution(mesh):
    placed = (P("gx", "gy", "gz", None, None), P("gx", "gy", "gz"), P("gx", "gy", "gz"))
    return jax.shard_map(
        on_device,
        mesh=mesh,
        in_specs=placed,
        out_specs=P("gx", "gy", "gz", None, None),
        check_vma=False,
    )
```

```python
import jax
import jax.numpy as jnp
import numpy as np
from jax import lax
from jax.experimental import pallas as pl
from jax.experimental.pallas import tpu as pltpu
from jax.sharding import PartitionSpec as P

AXES = ("gx", "gy", "gz")
HEAT_RATIO = 1.4
GRID_SCALE = 0.05
LOBATTO_POINTS = [
    -1.0,
    -0.8717401485096066,
    -0.5917001814331423,
    -0.2092992179024789,
    0.2092992179024789,
    0.5917001814331423,
    0.8717401485096066,
    1.0,
]
LOBATTO_WEIGHTS = [
    0.03571428571428571,
    0.21070422714350603,
    0.34112269248350435,
    0.4124587946587039,
    0.4124587946587039,
    0.34112269248350435,
    0.21070422714350603,
    0.03571428571428571,
]
EDGE = GRID_SCALE / LOBATTO_WEIGHTS[0]
ROWS = 40


def weak_matrix():
    points = np.array(LOBATTO_POINTS)
    weights = np.array(LOBATTO_WEIGHTS)
    bary = np.array([1.0 / np.prod([points[i] - points[j] for j in range(8) if j != i]) for i in range(8)])
    derivative = np.zeros((8, 8))
    for i in range(8):
        for j in range(8):
            if i != j:
                derivative[i, j] = bary[j] / bary[i] / (points[i] - points[j])
        derivative[i, i] = -np.sum(derivative[i])
    derivative[0, 0] += 1.0 / weights[0]
    derivative[7, 7] -= 1.0 / weights[0]
    return -GRID_SCALE * derivative


def lanes_of(shape):
    return lax.broadcasted_iota(jnp.int32, shape, len(shape) - 1)


def roll(value, shift):
    shift = shift % 128
    return value if shift == 0 else pltpu.roll(value, shift, value.ndim - 1)


def euler(u, d):
    rho, mom, energy = u[0], u[1:4], u[4]
    inv = 1.0 / rho
    normal = mom[d] * inv
    kinetic = 0.5 * (mom[0] * mom[0] + mom[1] * mom[1] + mom[2] * mom[2]) * inv
    pressure = (HEAT_RATIO - 1.0) * (energy - kinetic)
    sound = jnp.sqrt(HEAT_RATIO * pressure * inv)
    flux = [mom[d], mom[0] * normal, mom[1] * normal, mom[2] * normal, (energy + pressure) * normal]
    flux[1 + d] = flux[1 + d] + pressure
    return flux, jnp.abs(normal) + sound


def upwind(left, left_flux, left_speed, right, right_flux, right_speed):
    half = 0.5 * jnp.maximum(left_speed, right_speed)
    return [0.5 * (fl + fr) - half * (ur - ul) for ul, fl, ur, fr in zip(left, left_flux, right, right_flux)]


def rusanov(left, right, d):
    return upwind(left, *euler(left, d), right, *euler(right, d))


def faces_kernel(x_hbm, out_ref, x_ref, arrived):
    parts = ((3, 2), (0, 1), (7, 1), (1, 2), (5, 2))
    copies = [
        pltpu.make_async_copy(
            x_hbm.at[pl.ds(e * ROWS, many * ROWS)], x_ref.at[pl.ds(e * ROWS, many * ROWS)], arrived.at[n]
        )
        for n, (e, many) in enumerate(parts)
    ]
    for copy in copies:
        copy.start()
    lane = lanes_of((ROWS, 128))
    for copy in copies[:3]:
        copy.wait()
    for face, (ey, j) in enumerate(((0, 0), (3, 7))):
        packed = None
        for ex in range(2):
            for chunk in range(4):
                goal = 32 * ex + 8 * chunk
                piece = x_ref[pl.ds((ex * 4 + ey) * ROWS, ROWS), chunk * 128 : (chunk + 1) * 128]
                piece = roll(piece, goal - 8 * j)
                packed = piece if packed is None else jnp.where(lane % 64 >= goal, piece, packed)
        out_ref[pl.ds((4 + face) * ROWS, ROWS), :] = packed
    for copy in copies[3:]:
        copy.wait()
    for q in range(2):
        first = x_ref[pl.ds((2 * q) * ROWS, ROWS), 0:128]
        second = x_ref[pl.ds((2 * q + 1) * ROWS, ROWS), 0:128]
        out_ref[pl.ds(q * ROWS, ROWS), :] = jnp.where(lane < 64, first, roll(second, 64))
        first = x_ref[pl.ds((4 + 2 * q) * ROWS, ROWS), 384:512]
        second = x_ref[pl.ds((4 + 2 * q + 1) * ROWS, ROWS), 384:512]
        out_ref[pl.ds((2 + q) * ROWS, ROWS), :] = jnp.where(lane < 64, roll(first, 64), second)
    lane = lanes_of((8, 128))
    sub = lax.broadcasted_iota(jnp.int32, (8, 128), 0)
    for comp in range(5):
        packed = None
        for face, (ez, k) in enumerate(((0, 0), (7, 7))):
            for chunk in range(4):
                piece = None
                for e in range(8):
                    row = x_ref[pl.ds(e * ROWS + comp * 8 + ez, 1), chunk * 128 : (chunk + 1) * 128]
                    row = jnp.broadcast_to(row, (8, 128))
                    piece = row if piece is None else jnp.where(sub == e, row, piece)
                goal = 4 * face + chunk
                piece = roll(piece, goal - k)
                packed = piece if packed is None else jnp.where(lane % 8 >= goal, piece, packed)
        out_ref[pl.ds(6 * ROWS + comp * 8, 8), :] = packed


def inner_kernel(x_ref, troubled_ref, level_ref, out_ref, u_ref, flux_ref, speed_ref, acc_ref, acc_x_ref):
    weak, scale = weak_matrix(), [GRID_SCALE / w for w in LOBATTO_WEIGHTS]
    lane = lanes_of((8, 128))
    k = lax.broadcasted_iota(jnp.int32, (8, 128), 0)
    upper, ex, ey, ez = lane >= 64, (lane // 32) % 2, (lane // 8) % 4, lane % 8
    blend = jnp.zeros((8, 128), jnp.float32)
    for x in range(2):
        marks = (troubled_ref[x] * level_ref[x]).astype(jnp.float32)
        marks = jnp.dot(marks, jnp.where(ez == k, 1.0, 0.0), preferred_element_type=jnp.float32)
        for y in range(4):
            row = jnp.broadcast_to(marks[y : y + 1, :], (8, 128))
            blend = jnp.where((ex == x) & (ey == y), row, blend)
    blend = blend / 5.0
    smooth, half_blend = 1.0 - blend, 0.5 * blend

    def by_row(values):
        value = jnp.full((8, 128), float(values[0]), jnp.float32)
        for n in range(1, 8):
            value = jnp.where(k == n, float(values[n]), value)
        return value

    def by_half(low, high):
        return jnp.where(upper, float(high), float(low))

    def rows(row):
        return pl.ds(pl.multiple_of(row, 8), 8)

    for n in range(5):
        for h in range(2):
            parts = [
                x_ref[pl.ds(e * ROWS + 8 * n, 8), 256 * g + 128 * h : 256 * g + 128 * h + 128]
                for g in range(2)
                for e in range(8)
            ]
            u_ref[n, pl.ds(128 * h, 128), :] = jnp.concatenate(parts, axis=0).T

    weak_z = [by_row([weak[r][(r + s) % 8] for r in range(8)]) for s in range(8)]
    scale_z = by_row(scale)
    weight_z = jnp.where(k == 7, 0.0, half_blend)

    def first(t, carry):
        at = rows(t * 8)
        u = [u_ref[n, at, :] for n in range(5)]
        rho, mom, energy = u[0], u[1:4], u[4]
        inv = 1.0 / rho
        vel = [m * inv for m in mom]
        kinetic = 0.5 * (mom[0] * vel[0] + mom[1] * vel[1] + mom[2] * vel[2])
        pressure = (HEAT_RATIO - 1.0) * (energy - kinetic)
        sound = jnp.sqrt(HEAT_RATIO * pressure * inv)
        total = energy + pressure
        for d in range(3):
            f = [mom[d]] + [mom[n] * vel[d] for n in range(3)] + [total * vel[d]]
            f[1 + d] = f[1 + d] + pressure
            speed = jnp.abs(vel[d]) + sound
            speed_ref[d, at, :] = speed
            for n in range(1, 5):
                flux_ref[d, n - 1, at, :] = f[n]
        largest = jnp.maximum(speed, pltpu.roll(speed, 7, 0))
        for n in range(5):
            turned = [f[n]] + [pltpu.roll(f[n], 8 - s, 0) for s in range(1, 8)]
            volume = weak_z[0] * turned[0]
            for s in range(1, 8):
                volume = volume + weak_z[s] * turned[s]
            g = weight_z * (f[n] + turned[1] - largest * (pltpu.roll(u[n], 7, 0) - u[n]))
            acc_ref[n, at, :] = smooth * volume + scale_z * (pltpu.roll(g, 1, 0) - g)
        return carry

    lax.fori_loop(0, 32, first, 0, unroll=4)

    def flux(d, n, at):
        return u_ref[1 + d, at, :] if n == 0 else flux_ref[d, n - 1, at, :]

    def between(i, carry):
        last, start = pl.ds(i * 64 + 7, 8, stride=8), pl.ds(i * 64, 8, stride=8)
        weight = jnp.where(ez < 7, 0.5 * EDGE, 0.0)
        largest = jnp.maximum(speed_ref[2, last, :], roll(speed_ref[2, start, :], -1))
        for n in range(5):
            jump = roll(u_ref[n, start, :], -1) - u_ref[n, last, :]
            star = weight * (flux(2, n, last) + roll(flux(2, n, start), -1) - largest * jump)
            acc_ref[n, last, :] = acc_ref[n, last, :] - star
            acc_ref[n, start, :] = acc_ref[n, start, :] + roll(star, 1)
        return carry

    lax.fori_loop(0, 4, between, 0, unroll=4)

    end_y = jnp.where(ey < 3, 0.5, 0.0)

    def second(i, carry):
        at = [rows(i * 64 + 8 * j) for j in range(8)]
        speed = [speed_ref[1, a, :] for a in at]
        largest = [jnp.maximum(speed[j], speed[j + 1]) for j in range(7)]
        largest.append(jnp.maximum(speed[7], roll(speed[0], -8)))
        for n in range(5):
            u, f = [u_ref[n, a, :] for a in at], [flux(1, n, a) for a in at]
            g = [half_blend * (f[j] + f[j + 1] - largest[j] * (u[j + 1] - u[j])) for j in range(7)]
            g.append(end_y * (f[7] + roll(f[0], -8) - largest[7] * (roll(u[0], -8) - u[7])))
            even, odd = [f[m] + f[7 - m] for m in range(4)], [f[m] - f[7 - m] for m in range(4)]
            volumes = [None] * 8
            for j in range(4):
                from_odd, from_even = (
                    sum(float(0.5 * (weak[j][m] + sign * weak[j][7 - m])) * part[m] for m in range(4))
                    for sign, part in ((-1, odd), (1, even))
                )
                volumes[j], volumes[7 - j] = from_odd + from_even, from_odd - from_even
            for j in range(8):
                volume = volumes[j]
                low = g[j - 1] if j else roll(g[7], 8)
                acc_ref[n, at[j], :] = acc_ref[n, at[j], :] + (smooth * volume + scale[j] * (low - g[j]))
        return carry


    weak_x = [[by_half(weak[r][m], weak[4 + r][4 + m]) for m in range(4)] for r in range(4)]
    cross_x = [[by_half(weak[r][4 + m], weak[4 + r][m]) for m in range(4)] for r in range(4)]
    scale_x = [by_half(scale[r], scale[4 + r]) for r in range(4)]
    end_x = jnp.where(upper, jnp.where(ex == 0, 0.5, 0.0), half_blend)

    def following(value, swapped):
        return jnp.where(upper, roll(value, 32), swapped)

    def third(j, carry):
        at = [rows(i * 64 + 8 * j) for i in range(4)]
        speed = [speed_ref[0, a, :] for a in at]
        largest = [jnp.maximum(speed[i], speed[i + 1]) for i in range(3)]
        largest.append(jnp.maximum(speed[3], following(speed[0], roll(speed[0], 64))))
        for n in range(5):
            u, f = [u_ref[n, a, :] for a in at], [flux(0, n, a) for a in at]
            swapped = [roll(v, 64) for v in f]
            g = [half_blend * (f[i] + f[i + 1] - largest[i] * (u[i + 1] - u[i])) for i in range(3)]
            jump = following(u[0], roll(u[0], 64)) - u[3]
            g.append(end_x * (f[3] + following(f[0], swapped[0]) - largest[3] * jump))
            start = jnp.where(upper, roll(g[3], 64), jnp.where(ex == 1, roll(g[3], -32), 0.0))
            for i in range(4):
                volume = weak_x[i][0] * f[0] + cross_x[i][0] * swapped[0]
                for m in range(1, 4):
                    volume = volume + weak_x[i][m] * f[m] + cross_x[i][m] * swapped[m]
                low = g[i - 1] if i else start
                acc_x_ref[n, at[i], :] = smooth * volume + scale_x[i] * (low - g[i])
        return carry

    def both(t, carry):
        second(t, carry)
        third(2 * t, carry)
        third(2 * t + 1, carry)
        return carry

    lax.fori_loop(0, 4, both, 0)

    for n in range(5):
        for h in range(2):
            at = pl.ds(128 * h, 128)
            block = (acc_ref[n, at, :] + acc_x_ref[n, at, :]).T
            for g in range(2):
                for e in range(8):
                    out_ref[pl.ds(e * ROWS + 8 * n, 8), 256 * g + 128 * h : 256 * g + 128 * h + 128] = block[
                        64 * g + 8 * e : 64 * g + 8 * e + 8, :
                    ]


def pick_kernel(core_ref, both_ref, ahead_ref, out_ref):
    del ahead_ref
    out_ref[...] = both_ref[core_ref[0], pl.ds(6 * ROWS, ROWS), :]


def outer_kernel(place_ref, pre_ref, own_ref, halo_ref, near_ref, far_ref, out_hbm, out_ref, star_ref, left_sem):
    lane = lanes_of((8, 128))
    sub = lax.broadcasted_iota(jnp.int32, (8, 128), 0)
    left_half, low_face = lane < 64, lane % 8 < 4
    core, odd_x, odd_y = place_ref[0], place_ref[1], place_ref[2]
    zero = jnp.zeros((8, 128), jnp.float32)

    def own(tile):
        return own_ref[pl.ds(tile * 8, 8), :]

    first_core = core == 0
    mine = [own(30 + n) for n in range(5)]
    other = []
    for n in range(5):
        near = near_ref[1 - core, pl.ds((30 + n) * 8, 8), :]
        far = far_ref[pl.ds(n * 8, 8), :]
        above = jnp.where(first_core, near, far)
        below = jnp.where(first_core, far, near)
        other.append(jnp.where(low_face, roll(below, -4), roll(above, 4)))
    left = [jnp.where(low_face, o, m) for o, m in zip(other, mine)]
    right = [jnp.where(low_face, m, o) for o, m in zip(other, mine)]
    for n, star in enumerate(rusanov(left, right, 2)):
        star = EDGE * star
        for c in range(4):
            cols = slice(c * 128, (c + 1) * 128)
            star_ref[pl.ds(8 * n, 8), cols] = jnp.where(lane % 8 == 0, roll(star, -c), zero)
            star_ref[pl.ds(ROWS + 8 * n, 8), cols] = jnp.where(lane % 8 == 7, -roll(star, 3 - c), zero)

    along_x = {}
    for q in range(2):
        mine = [own(5 * q + n) for n in range(5)]
        below = [halo_ref[0, odd_x, core, pl.ds((5 * q + n) * 8, 8), :] for n in range(5)]
        for n, star in enumerate(rusanov(below, mine, 0)):
            star = EDGE * star
            along_x[2 * q, n] = jnp.where(left_half, star, zero)
            along_x[2 * q + 1, n] = jnp.where(left_half, roll(star, 64), zero)
        mine = [own(10 + 5 * q + n) for n in range(5)]
        above = [halo_ref[0, 1 - odd_x, core, pl.ds((5 * q + n) * 8, 8), :] for n in range(5)]
        for n, star in enumerate(rusanov(mine, above, 0)):
            star = -EDGE * star
            along_x[4 + 2 * q, n] = jnp.where(left_half, zero, roll(star, 64))
            along_x[5 + 2 * q, n] = jnp.where(left_half, zero, star)

    mine = [own(20 + n) for n in range(5)]
    below = [halo_ref[1, odd_y, core, pl.ds((5 + n) * 8, 8), :] for n in range(5)]
    low_y = [EDGE * s for s in rusanov(below, mine, 1)]
    mine = [own(25 + n) for n in range(5)]
    above = [halo_ref[1, 1 - odd_y, core, pl.ds(n * 8, 8), :] for n in range(5)]
    high_y = [-EDGE * s for s in rusanov(mine, above, 1)]
    row_j = (lane // 8) % 8

    copies = []
    for e in (1, 2, 5, 6, 0, 3, 4, 7):
        ex, ey = e // 4, e % 4
        for n in range(5):
            for c in range(4):
                cols = slice(c * 128, (c + 1) * 128)
                value = pre_ref[pl.ds(e * ROWS + 8 * n, 8), cols]
                low = jnp.broadcast_to(star_ref[pl.ds(8 * n + e, 1), cols], (8, 128))
                high = jnp.broadcast_to(star_ref[pl.ds(ROWS + 8 * n + e, 1), cols], (8, 128))
                value = value + jnp.where(sub == 0, low, jnp.where(sub == 7, high, zero))
                if c == (0, 3)[ex]:
                    value = value + along_x[e, n]
                start = 32 * ex + 8 * c
                if ey == 0:
                    value = value + jnp.where(row_j == 0, roll(low_y[n], -start), zero)
                if ey == 3:
                    value = value + jnp.where(row_j == 7, roll(high_y[n], 56 - start), zero)
                out_ref[pl.ds(e * ROWS + 8 * n, 8), cols] = value
        at = pl.ds(e * ROWS, ROWS)
        copies.append(pltpu.make_async_copy(out_ref.at[at], out_hbm.at[at], left_sem.at[e]))
        copies[-1].start()
    for copy in copies:
        copy.wait()


def pairs(size, shift):
    return [[(2 * n + shift) % size, (2 * n + 1 + shift) % size] for n in range(size // 2)]


def crossed(sizes, shift, first, last):
    nx, ny, nz = sizes
    moves = []
    for z in range(first, last):
        for a, b in pairs(nx, shift) if z % 2 == 0 else pairs(ny, shift):
            for other in range(ny if z % 2 == 0 else nx):
                ends = [((v * ny + other) if z % 2 == 0 else (other * ny + v)) * nz + z for v in (a, b)]
                moves += [(ends[0], ends[1]), (ends[1], ends[0])]
    return sorted(set(moves))


def in_vmem():
    return pl.BlockSpec(memory_space=pltpu.VMEM)


def in_hbm():
    return pl.BlockSpec(memory_space=pltpu.HBM)


LIMIT = pltpu.CompilerParams(vmem_limit_bytes=32 * 1024 * 1024)


def on_device(conserved, troubled, blend_level):
    sizes = [lax.axis_size(a) for a in AXES]
    ix, iy, iz = [lax.axis_index(a) for a in AXES]
    core, odd_x, odd_y = iz & 1, ix & 1, iy & 1
    state = conserved.transpose(0, 1, 3, 2, 4).reshape(8 * ROWS, 512)

    own = pl.pallas_call(
        faces_kernel,
        out_shape=jax.ShapeDtypeStruct((7 * ROWS, 128), jnp.float32),
        in_specs=[in_hbm()],
        out_specs=in_vmem(),
        scratch_shapes=[pltpu.VMEM((8 * ROWS, 512), jnp.float32), pltpu.SemaphoreType.DMA((5,))],
        compiler_params=LIMIT,
        name="faces",
    )(pltpu.with_memory_space_constraint(state, pltpu.HBM))

    both = lax.all_gather(own, "gz", axis_index_groups=pairs(sizes[2], 0))
    x_faces = both[:, : 4 * ROWS].reshape(2, 2, 2 * ROWS, 128)
    y_faces = both[:, 4 * ROWS : 6 * ROWS]
    sent = []
    for shift in range(2):
        face = odd_x if shift else 1 - odd_x
        x_part = lax.dynamic_index_in_dim(x_faces, face, 1, keepdims=False)
        sent.append(jnp.where(core == 0, x_part, y_faces))
    half = sizes[2] // 2
    ahead = [lax.ppermute(v, AXES, crossed(sizes, n, 0, half)) for n, v in enumerate(sent)]

    in_smem = pl.BlockSpec(memory_space=pltpu.SMEM)
    z_faces = pl.pallas_call(
        pick_kernel,
        out_shape=jax.ShapeDtypeStruct((ROWS, 128), jnp.float32),
        in_specs=[in_smem] + [in_vmem()] * 2,
        out_specs=in_vmem(),
        compiler_params=LIMIT,
        name="pick",
    )(core.astype(jnp.int32).reshape(1), both, sent[0])
    z_faces, sent = lax.optimization_barrier((z_faces, sent))
    swap = pairs(sizes[2], 1)
    far = lax.ppermute(z_faces, "gz", [(a, b) for a, b in swap] + [(b, a) for a, b in swap])
    after = [lax.ppermute(v, AXES, crossed(sizes, n, half, sizes[2])) for n, v in enumerate(sent)]

    inner = pl.pallas_call(
        inner_kernel,
        out_shape=jax.ShapeDtypeStruct((8 * ROWS, 512), jnp.float32),
        in_specs=[in_vmem()] * 3,
        out_specs=in_vmem(),
        scratch_shapes=[
            pltpu.VMEM((5, 256, 128), jnp.float32),
            pltpu.VMEM((3, 4, 256, 128), jnp.float32),
            pltpu.VMEM((3, 256, 128), jnp.float32),
            pltpu.VMEM((5, 256, 128), jnp.float32),
            pltpu.VMEM((5, 256, 128), jnp.float32),
        ],
        compiler_params=LIMIT,
        cost_estimate=pl.CostEstimate(flops=20_000_000, bytes_accessed=1_400_000, transcendentals=65536),
        name="inner",
    )(state, troubled, blend_level)

    gathered = jnp.stack([ahead[1] + after[1], ahead[0] + after[0]])
    gathered, far = lax.optimization_barrier((gathered, far))
    halo = lax.all_gather(gathered, "gz", axis_index_groups=pairs(sizes[2], 0))
    place = jnp.stack([core, odd_x, odd_y]).astype(jnp.int32)
    full = pl.pallas_call(
        outer_kernel,
        out_shape=jax.ShapeDtypeStruct((8 * ROWS, 512), jnp.float32),
        in_specs=[pl.BlockSpec(memory_space=pltpu.SMEM)] + [in_vmem()] * 5,
        out_specs=in_hbm(),
        scratch_shapes=[
            pltpu.VMEM((8 * ROWS, 512), jnp.float32),
            pltpu.VMEM((2 * ROWS, 512), jnp.float32),
            pltpu.SemaphoreType.DMA((8,)),
        ],
        compiler_params=LIMIT,
        name="outer",
    )(place, inner, own, halo, both, far)
    return full.reshape(2, 4, 5, 8, 512).transpose(0, 1, 3, 2, 4)


def solution(mesh):
    placed = (P("gx", "gy", "gz", None, None), P("gx", "gy", "gz"), P("gx", "gy", "gz"))
    return jax.shard_map(
        on_device,
        mesh=mesh,
        in_specs=placed,
        out_specs=P("gx", "gy", "gz", None, None),
        check_vma=False,
    )
```
